32 devices in a mesh: dp: 4 (over x, core), expert: 8 (over z, y).
Axes of the slice: x: 2, y: 2, z: 4, core: 2. Of those that a mesh axis runs over, the one named last changes fastest.
Arguments:
- tokens: bfloat16 [4096, 2048], P(('dp', 'expert')), may hold values from -6 to 6
- cotangent: bfloat16 [4096, 2048], P(('dp', 'expert')), may hold values from -1.5 to 1.5
- routes: int32 [4096, 8], P(('dp', 'expert')), may hold values from 0 to 31, all different within a row; in each aligned block of 128 rows (0 to 127, 128 to 255, ...) at most 56 rows name the same one
- gates: bfloat16 [4096, 8], P(('dp', 'expert')), may hold values from 0.049804688 to 0.44921875
- w_gate: bfloat16 [32, 2048, 768], P(('dp', 'expert')), may hold values from -0.125 to 0.125
- w_up: bfloat16 [32, 2048, 768], P(('dp', 'expert')), may hold values from -0.125 to 0.125
- w_down: bfloat16 [32, 768, 2048], P(('dp', 'expert')), may hold values from -0.21875 to 0.21875
Outputs:
- input_grad: bfloat16 [4096, 2048], P(('dp', 'expert'))
- gate_grad: bfloat16 [4096, 8], P(('dp', 'expert'))
- w_gate_grad: bfloat16 [32, 2048, 768], P(('dp', 'expert'))
- w_up_grad: bfloat16 [32, 2048, 768], P(('dp', 'expert'))
- w_down_grad: bfloat16 [32, 768, 2048], P(('dp', 'expert'))
The draws below stay inside these ranges and needn't reach their ends.
Inputs may be any that keep to these rules, and one draw needn't show every extreme that they name: `routes`: each row names 8 different experts. The tokens of one device name one expert at most 56 times, and in every draw some expert is named exactly 56 times by the tokens of some device.
All inputs are finite; a program needn't handle non-finite values.
Results may differ from the reference program's by a relative error of at most 0.0064.
Values may be sent and summed in bfloat16 or wider, within the bound.
No kernel may reach another device: no remote copies, remote signals or barrier semaphores. Data moves between devices by JAX's collectives and lax.ppermute only.
A program may use at most 192 MiB of HBM per device.

```python
import math
import jax
import jax.numpy as jnp
import numpy as np
from jax import lax

D = 2048
FF = 768
TOPK = 8
TOK_DEV = 128
EXPERTS = 32
TOKENS = 4096
MOST = 56
N_DP = 4
N_EXPERT = 8


def levels(rng, dims, pieces, smallest, high):
    factor_of = 1.0
    for position, blocks in pieces:
        steps = jax.random.uniform(jax.random.fold_in(jax.random.fold_in(rng, 6), position), (blocks,), jnp.float32, smallest / len(pieces), high / len(pieces))
        factor_of = factor_of * jnp.repeat(jnp.exp(steps), dims[position] // blocks).reshape((-1,) + (1,) * (len(dims) - 1 - position))
    return factor_of


def deal_out(rng, own, number, rows, count, top, limit, skew):
    order = jax.random.permutation(rng, count)
    heavy_load, common = load_shares(count, rows * top, limit, skew, True), load_shares(count, rows * top, limit, skew, False)
    places = jnp.arange(count)

    def named(sizes, turn):
        used = int((sizes > 0).sum())
        fixed = max(1, used // 4)
        shifted = fixed + (places - fixed + turn * (used - fixed)) % max(1, count - fixed)
        return jnp.zeros((count,), jnp.int32).at[order[jnp.where(places < fixed, places, shifted)]].set(jnp.asarray(sizes, jnp.int32))

    sizes = jnp.where(number % 4 == 0, named(heavy_load, number // 4), named(common, number - number // 4 - 1))
    mixed = jax.random.permutation(jax.random.fold_in(own, 3), count)
    source_of, sink = mixed[0:count // 2 * 2:2], mixed[1:count // 2 * 2:2]
    room = jnp.minimum(sizes[source_of] - 1, limit - sizes[sink]) // 2
    room = jnp.where((source_of == order[0]) | (sink == order[0]) | (sizes[sink] == 0), 0, jnp.maximum(room, 0))
    shifted = jax.random.randint(jax.random.fold_in(own, 4), (count // 2,), 0, 1 << 20) % (room + 1)
    sizes = sizes.at[source_of].add(-shifted).at[sink].add(shifted)
    items = jnp.searchsorted(jnp.cumsum(sizes), jnp.arange(rows * top), side="right").astype(jnp.int32)
    table = items.reshape(top, rows).T
    table = table[jax.random.permutation(jax.random.fold_in(own, 1), rows)]
    turn = jax.random.randint(jax.random.fold_in(own, 2), (rows, 1), 0, top)
    return jnp.take_along_axis(table, (jnp.arange(top)[None, :] + turn) % top, axis=1)


def load_shares(count, total, limit, skew, full):
    loads = [(1 << 20) // math.isqrt(rank ** skew) + 1 for rank in range(1, count + 1)]
    largest = limit if full else min(limit, max(-(-total // count), total * loads[0] // sum(loads)))
    least = 1 if total - largest >= count - 1 else 0
    holding, surplus = [largest] + [least] * (count - 1), total - largest - least * (count - 1)
    while surplus > 0:
        free = [i for i in range(1, count) if holding[i] < largest] or [i for i in range(1, count) if holding[i] < limit]
        mass, left = sum([loads[i] for i in free]), surplus
        for i in free:
            addition = min(limit - holding[i], max(1, left * loads[i] // mass), surplus)
            holding[i] = holding[i] + addition
            surplus = surplus - addition
    return np.array(holding)


def centred(key, shape, scale, most, cuts=(), held_as=jnp.bfloat16):
    gain = levels(key, shape, cuts, -0.22, 0.18) if cuts else 1.0
    values = jax.random.normal(key, shape, jnp.float32) * scale * gain
    return jnp.minimum(jnp.maximum(values, -most), most).astype(held_as)


def setup_inputs(seed: int = 0) -> dict:
    splits = jax.random.split(jax.random.key(seed), 8)
    tokens = centred(splits[0], (TOKENS, D), 1.0, 6.0, ((0, 32),))
    cotangent = centred(splits[1], (TOKENS, D), 0.25, 1.5, ((0, 32),))
    routes_keys = jax.random.split(jax.random.fold_in(splits[2], 1), TOKENS // TOK_DEV)
    routes_turns = jax.random.permutation(jax.random.fold_in(splits[2], 3), TOKENS // TOK_DEV)
    routes = jax.vmap(lambda own, number: deal_out(jax.random.fold_in(splits[2], 2), own, number, TOK_DEV, EXPERTS, TOPK, MOST, 2))(routes_keys, routes_turns).reshape((TOKENS, TOPK))
    gates = jnp.clip(0.049804688 + 0.39941406 * jax.random.uniform(splits[3], (TOKENS, TOPK), jnp.float32) ** levels(splits[3], (TOKENS, TOPK), ((0, 32),), -0.2, 0.2), 0.049804688, 0.44921875).astype(jnp.bfloat16)
    w_gate = centred(splits[4], (EXPERTS, D, FF), D ** -0.5, 0.125, ((0, 32),))
    w_up = centred(splits[5], (EXPERTS, D, FF), D ** -0.5, 0.125, ((0, 32),))
    w_down = centred(splits[6], (EXPERTS, FF, D), FF ** -0.5, 0.21875, ((0, 32),))
    return dict(tokens=tokens, cotangent=cotangent, routes=routes, gates=gates, w_gate=w_gate, w_up=w_up, w_down=w_down)


def expert_rows(inputs, cotangent_rows, router_weight, gate_matrix, up_matrix, down_matrix):
    pre_gate = jnp.dot(inputs, gate_matrix, preferred_element_type=jnp.float32)
    pre_up = jnp.dot(inputs, up_matrix, preferred_element_type=jnp.float32)
    sigmoid_gate = jax.nn.sigmoid(pre_gate)
    silu_gate = pre_gate * sigmoid_gate
    hidden = (silu_gate * pre_up).astype(jnp.bfloat16)
    expert_out = jnp.dot(hidden, down_matrix, preferred_element_type=jnp.float32)
    gate_grad = jnp.sum(cotangent_rows.astype(jnp.float32) * expert_out, axis=1).astype(jnp.bfloat16)
    out_grad = (router_weight.astype(jnp.float32)[:, None] * cotangent_rows.astype(jnp.float32)).astype(jnp.bfloat16)
    hidden_grad = lax.dot_general(out_grad, down_matrix, (((1,), (1,)), ((), ())), preferred_element_type=jnp.float32)
    pre_gate_grad = (hidden_grad * pre_up * sigmoid_gate * (1.0 + pre_gate * (1.0 - sigmoid_gate))).astype(jnp.bfloat16)
    pre_up_grad = (hidden_grad * silu_gate).astype(jnp.bfloat16)
    row_grad = lax.dot_general(pre_gate_grad, gate_matrix, (((1,), (1,)), ((), ())), preferred_element_type=jnp.float32)
    row_grad = row_grad + lax.dot_general(pre_up_grad, up_matrix, (((1,), (1,)), ((), ())), preferred_element_type=jnp.float32)
    gate_term = lax.dot_general(inputs, pre_gate_grad, (((0,), (0,)), ((), ())), preferred_element_type=jnp.float32)
    up_term = lax.dot_general(inputs, pre_up_grad, (((0,), (0,)), ((), ())), preferred_element_type=jnp.float32)
    down_term = lax.dot_general(hidden, out_grad, (((0,), (0,)), ((), ())), preferred_element_type=jnp.float32)
    return row_grad.astype(jnp.bfloat16), gate_grad, gate_term, up_term, down_term


def reference(tokens, cotangent, routes, gates, w_gate, w_up, w_down):
    row_count = TOKENS * TOPK
    slot_total = N_DP * N_EXPERT * MOST
    flat_expert = routes.reshape(row_count).astype(jnp.int32)
    flat_weight = gates.reshape(row_count)
    zero_value = jnp.zeros((), jnp.bfloat16)

    def one_expert(carried, member):
        grad_rows, gate_rows = carried
        expert_id, gate_matrix, up_matrix, down_matrix = member
        picked = jnp.nonzero(flat_expert == expert_id, size=slot_total, fill_value=row_count)[0].astype(jnp.int32)
        is_live = picked < row_count
        safe_pick = jnp.minimum(picked, row_count - 1).astype(jnp.int32)
        token_id = (safe_pick // TOPK).astype(jnp.int32)
        block_tokens = jnp.where(is_live[:, None], tokens[token_id], zero_value)
        block_cotangent = jnp.where(is_live[:, None], cotangent[token_id], zero_value)
        block_weight = jnp.where(is_live, flat_weight[safe_pick], zero_value)
        row_grad, gate_grad, gate_term, up_term, down_term = expert_rows(
            block_tokens, block_cotangent, block_weight, gate_matrix, up_matrix, down_matrix)
        grad_rows = grad_rows.at[picked].set(row_grad, mode="drop")
        gate_rows = gate_rows.at[picked].set(gate_grad, mode="drop")
        return (grad_rows, gate_rows), (gate_term.astype(jnp.bfloat16), up_term.astype(jnp.bfloat16), down_term.astype(jnp.bfloat16))

    initial = (jnp.zeros((row_count, D), jnp.bfloat16), jnp.zeros((row_count,), jnp.bfloat16))
    carried, weight_grads = lax.scan(one_expert, initial, (jnp.arange(EXPERTS, dtype=jnp.int32), w_gate, w_up, w_down))
    grad_rows, gate_rows = carried
    input_grad = jnp.sum(grad_rows.reshape(TOKENS, TOPK, D), axis=1, dtype=jnp.float32).astype(jnp.bfloat16)
    gate_grad = gate_rows.reshape(TOKENS, TOPK)
    return input_grad, gate_grad, weight_grads[0], weight_grads[1], weight_grads[2]
```

```python
import jax
import jax.numpy as jnp
from jax import lax
from jax.sharding import PartitionSpec as P

block_rows = 256
gather_limit = 32 * 2**20


def expert_parts(inputs, cotangent_rows, router_weight, gate_matrix, up_matrix, down_matrix):
    pre_gate = jnp.dot(inputs, gate_matrix, preferred_element_type=jnp.float32)
    pre_up = jnp.dot(inputs, up_matrix, preferred_element_type=jnp.float32)
    sigmoid_gate = jax.nn.sigmoid(pre_gate)
    silu_gate = pre_gate * sigmoid_gate
    hidden = (silu_gate * pre_up).astype(jnp.bfloat16)
    expert_out = jnp.dot(hidden, down_matrix, preferred_element_type=jnp.float32)
    gate_grad = jnp.sum(cotangent_rows.astype(jnp.float32) * expert_out, axis=1).astype(
        jnp.bfloat16
    )
    out_grad = (
        router_weight.astype(jnp.float32)[:, None] * cotangent_rows.astype(jnp.float32)
    ).astype(jnp.bfloat16)
    hidden_grad = lax.dot_general(
        out_grad, down_matrix, (((1,), (1,)), ((), ())), preferred_element_type=jnp.float32
    )
    pre_gate_grad = (
        hidden_grad * pre_up * sigmoid_gate * (1.0 + pre_gate * (1.0 - sigmoid_gate))
    ).astype(jnp.bfloat16)
    pre_up_grad = (hidden_grad * silu_gate).astype(jnp.bfloat16)
    row_grad = lax.dot_general(
        pre_gate_grad, gate_matrix, (((1,), (1,)), ((), ())), preferred_element_type=jnp.float32
    )
    row_grad = row_grad + lax.dot_general(
        pre_up_grad, up_matrix, (((1,), (1,)), ((), ())), preferred_element_type=jnp.float32
    )
    return (row_grad.astype(jnp.bfloat16), gate_grad, pre_gate_grad, pre_up_grad, hidden, out_grad)


def outer_terms(inputs, pre_gate_grad, pre_up_grad, hidden, out_grad):
    gate_term = lax.dot_general(
        inputs, pre_gate_grad, (((0,), (0,)), ((), ())), preferred_element_type=jnp.float32
    )
    up_term = lax.dot_general(
        inputs, pre_up_grad, (((0,), (0,)), ((), ())), preferred_element_type=jnp.float32
    )
    down_term = lax.dot_general(
        hidden, out_grad, (((0,), (0,)), ((), ())), preferred_element_type=jnp.float32
    )
    return (gate_term, up_term, down_term)


def exchange_path(tokens, cotangent, routes, gates, w_gate, w_up, w_down):
    dp_count = lax.axis_size("dp")
    expert_count = lax.axis_size("expert")
    device_count = dp_count * expert_count
    tok_local, model_width = tokens.shape
    top_count = routes.shape[1]
    row_count = tok_local * top_count
    most_rows = 7 * row_count // (4 * device_count)
    slot_total = device_count * most_rows
    zero_value = jnp.zeros((), jnp.bfloat16)
    flat_expert = routes.reshape(row_count)
    onehot = (flat_expert[:, None] == jnp.arange(device_count, dtype=jnp.int32)[None, :]).astype(
        jnp.int32
    )
    rank_in_expert = jnp.sum(jnp.cumsum(onehot, axis=0) * onehot, axis=1) - 1
    slot_index = flat_expert * most_rows + rank_in_expert
    row_of_slot = (
        jnp.full((slot_total,), row_count, jnp.int32)
        .at[slot_index]
        .set(jnp.arange(row_count, dtype=jnp.int32))
    )
    slot_live = row_of_slot < row_count
    safe_row = jnp.minimum(row_of_slot, row_count - 1)
    token_of_slot = safe_row // top_count
    send_tokens = jnp.where(slot_live[:, None], tokens[token_of_slot], zero_value).reshape(
        device_count, most_rows, model_width
    )
    send_cotangent = jnp.where(slot_live[:, None], cotangent[token_of_slot], zero_value).reshape(
        device_count, most_rows, model_width
    )
    send_weight = jnp.where(slot_live, gates.reshape(row_count)[safe_row], zero_value).reshape(
        device_count, most_rows
    )
    arrived = (
        lax.all_to_all(send_tokens, ("dp", "expert"), split_axis=0, concat_axis=0, tiled=True),
        lax.all_to_all(send_cotangent, ("dp", "expert"), split_axis=0, concat_axis=0, tiled=True),
        lax.all_to_all(send_weight, ("dp", "expert"), split_axis=0, concat_axis=0, tiled=True),
    )
    got_tokens = arrived[0].reshape(slot_total, model_width)
    got_cotangent = arrived[1].reshape(slot_total, model_width)
    got_weight = arrived[2].reshape(slot_total)
    gate_matrix = w_gate[0]
    up_matrix = w_up[0]
    down_matrix = w_down[0]
    hidden_width = gate_matrix.shape[1]
    is_used = got_weight != zero_value
    used_count = jnp.sum(is_used.astype(jnp.int32))
    padded_total = -(-slot_total // block_rows) * block_rows
    compact_pos = jnp.cumsum(is_used.astype(jnp.int32)) - 1
    slot_of_compact = (
        jnp.full((padded_total,), slot_total, jnp.int32)
        .at[jnp.where(is_used, compact_pos, padded_total)]
        .set(jnp.arange(slot_total, dtype=jnp.int32), mode="drop")
    )
    block_count = (used_count + block_rows - 1) // block_rows

    def block_step(block_index, carried):
        gate_acc, up_acc, down_acc, grad_slots, gate_slots = carried
        picked = lax.dynamic_slice_in_dim(slot_of_compact, block_index * block_rows, block_rows)
        is_live = picked < slot_total
        safe_pick = jnp.minimum(picked, slot_total - 1)
        block_tokens = jnp.where(is_live[:, None], got_tokens[safe_pick], zero_value)
        block_cotangent = jnp.where(is_live[:, None], got_cotangent[safe_pick], zero_value)
        block_weight = jnp.where(is_live, got_weight[safe_pick], zero_value)
        row_grad, gate_grad, pre_gate_grad, pre_up_grad, hidden, out_grad = expert_parts(
            block_tokens, block_cotangent, block_weight, gate_matrix, up_matrix, down_matrix
        )
        gate_term, up_term, down_term = outer_terms(
            block_tokens, pre_gate_grad, pre_up_grad, hidden, out_grad
        )
        target = jnp.where(is_live, picked, slot_total)
        grad_slots = grad_slots.at[target].set(row_grad, mode="drop")
        gate_slots = gate_slots.at[target].set(gate_grad, mode="drop")
        return (
            gate_acc + gate_term,
            up_acc + up_term,
            down_acc + down_term,
            grad_slots,
            gate_slots,
        )

    initial = (
        jnp.zeros((model_width, hidden_width), jnp.float32),
        jnp.zeros((model_width, hidden_width), jnp.float32),
        jnp.zeros((hidden_width, model_width), jnp.float32),
        jnp.zeros((slot_total, model_width), jnp.bfloat16),
        jnp.zeros((slot_total,), jnp.bfloat16),
    )
    finished = lax.fori_loop(0, block_count, block_step, initial)
    gate_acc, up_acc, down_acc, grad_slots, gate_slots = finished
    grad_out = grad_slots.reshape(device_count, most_rows, model_width)
    gate_out = gate_slots.reshape(device_count, most_rows)
    returned = (
        lax.all_to_all(grad_out, ("dp", "expert"), split_axis=0, concat_axis=0, tiled=True),
        lax.all_to_all(gate_out, ("dp", "expert"), split_axis=0, concat_axis=0, tiled=True),
    )
    back_grad = returned[0].reshape(slot_total, model_width)
    back_gate = returned[1].reshape(slot_total)
    row_grads = back_grad[slot_index].reshape(tok_local, top_count, model_width)
    input_grad = jnp.sum(row_grads, axis=1, dtype=jnp.float32).astype(jnp.bfloat16)
    gate_grad = back_gate[slot_index].reshape(tok_local, top_count)
    return (
        input_grad,
        gate_grad,
        gate_acc.astype(jnp.bfloat16)[None],
        up_acc.astype(jnp.bfloat16)[None],
        down_acc.astype(jnp.bfloat16)[None],
    )


def select_lane(info, index):
    lanes = lax.broadcasted_iota(jnp.int32, info.shape, info.ndim - 1)
    return jnp.sum(jnp.where(lanes == index, info, jnp.zeros((), info.dtype)), axis=-1)


def gather_path(tokens, cotangent, routes, gates, w_gate, w_up, w_down):
    dp_count = lax.axis_size("dp")
    expert_count = lax.axis_size("expert")
    device_count = dp_count * expert_count
    tok_local, model_width = tokens.shape
    top_count = routes.shape[1]
    most_rows = 7 * tok_local * top_count // (4 * device_count)
    ring = expert_count // 2
    bf16, f32 = jnp.bfloat16, jnp.float32

    def swap_core(v):
        return lax.ppermute(v, "dp", [(p, p ^ 1) for p in range(dp_count)])

    def swap_x(v):
        return lax.ppermute(v, "dp", [(p, p ^ 2) for p in range(dp_count)])

    def swap_y(v):
        return lax.ppermute(v, "expert", [(q, q ^ 1) for q in range(expert_count)])

    def ring_up(v):
        return lax.ppermute(
            v, "expert", [(q, (q + 2) % expert_count) for q in range(expert_count)]
        )

    def ring_down(v):
        return lax.ppermute(
            v, "expert", [(q, (q - 2) % expert_count) for q in range(expert_count)]
        )

    dp_index = lax.axis_index("dp")
    expert_index = lax.axis_index("expert")
    mine = dp_index * expert_count + expert_index
    other = (dp_index ^ 1) * expert_count + expert_index

    hit = routes[:, :, None] == jnp.arange(device_count, dtype=jnp.int32)[None, None, :]
    gate_dense = jnp.sum(jnp.where(hit, gates[:, :, None].astype(f32), 0.0), axis=1)
    named = jnp.sum(hit.astype(f32), axis=1)
    token_iota = jnp.arange(tok_local)
    before = (token_iota[None, :] < token_iota[:, None]).astype(bf16)
    rank = jnp.dot(before, named.astype(bf16), preferred_element_type=f32)
    rank = jnp.where(named > 0.0, rank, -1.0)
    info_width = -(-2 * device_count // 128) * 128
    info = jnp.concatenate(
        [
            gate_dense.astype(bf16),
            rank.astype(bf16),
            jnp.zeros((tok_local, info_width - 2 * device_count), bf16),
        ],
        axis=1,
    )

    cuts = (0, 3 * model_width // 8, 3 * model_width // 4, model_width)

    def part_of(v, n):
        return v[:, cuts[n] : cuts[n + 1]]

    def gather_zyx(v):
        hops = [v]
        for _ in range(ring - 1):
            hops.append(ring_up(hops[-1]))
        near = jnp.stack(hops)
        far = swap_y(near)
        both = jnp.stack([near, far])
        return jnp.stack([both, swap_x(both)])

    def gather_zxy(v):
        hops = [v]
        for _ in range(ring - 1):
            hops.append(ring_up(hops[-1]))
        near = jnp.stack(hops)
        far = swap_x(near)
        both = jnp.stack([near, far])
        return jnp.stack([both, swap_y(both)], axis=1)

    def gather_xyz(v):
        pair = jnp.stack([v, swap_x(v)])
        quad = jnp.stack([pair, swap_y(pair)], axis=1)
        hops = [quad]
        for _ in range(ring - 1):
            hops.append(ring_up(hops[-1]))
        return jnp.stack(hops, axis=2)

    gathers = (gather_zyx, gather_zxy, gather_xyz)

    def pick(places, v):
        return jnp.einsum("ijrct,ijrtd->ijrcd", places, v, preferred_element_type=f32).astype(bf16)

    def compact(v):
        keep = pick(place_mine, v)
        give = swap_core(pick(place_other, v))
        return jnp.stack([keep, give]).reshape(2 * 4 * ring * most_rows, v.shape[-1])

    token_parts = [part_of(tokens, n) for n in range(3)]
    token_parts[0] = jnp.concatenate([info, token_parts[0]], axis=1)
    got = [gathers[n](token_parts[n]) for n in range(3)]
    got_info = got[0][..., :info_width]
    slots = jnp.arange(most_rows, dtype=f32)

    def places_of(index):
        ranks = select_lane(got_info, device_count + index).astype(f32)
        return (ranks[..., None, :] == slots[:, None]).astype(bf16)

    place_mine = places_of(mine)
    place_other = places_of(other)
    rows = [compact(v) for v in got]
    row_gate = select_lane(rows[0][:, :info_width], mine).astype(f32)[:, None]
    rows[0] = rows[0][:, info_width:]
    got_cot = [gathers[n](part_of(cotangent, n)) for n in range(3)]
    cot_rows = [compact(v) for v in got_cot]

    gate_matrix, up_matrix, down_matrix = w_gate[0], w_up[0], w_down[0]
    x_rows = jnp.concatenate(rows, axis=1)
    c_rows = jnp.concatenate(cot_rows, axis=1)
    pre_gate = jnp.dot(x_rows, gate_matrix, preferred_element_type=f32)
    pre_up = jnp.dot(x_rows, up_matrix, preferred_element_type=f32)
    back = lax.dot_general(
        c_rows, down_matrix, (((1,), (1,)), ((), ())), preferred_element_type=f32
    )
    sigmoid_gate = jax.nn.sigmoid(pre_gate)
    silu_gate = pre_gate * sigmoid_gate
    hidden = silu_gate * pre_up
    gate_grad = jnp.sum(hidden * back, axis=1, keepdims=True)
    weighted = (hidden * row_gate).astype(bf16)
    hidden_grad = back * row_gate
    pre_gate_grad = (
        hidden_grad * pre_up * sigmoid_gate * (1.0 + pre_gate * (1.0 - sigmoid_gate))
    ).astype(bf16)
    pre_up_grad = (hidden_grad * silu_gate).astype(bf16)
    lanes = lax.broadcasted_iota(jnp.int32, (1, info_width), 1)
    gate_lanes = jnp.where(lanes == mine, gate_grad, 0.0).astype(bf16)

    def row_grad_of(n):
        matrix = slice(cuts[n], cuts[n + 1])
        nt = (((1,), (1,)), ((), ()))
        total = lax.dot_general(
            pre_gate_grad, gate_matrix[matrix], nt, preferred_element_type=f32
        ) + lax.dot_general(pre_up_grad, up_matrix[matrix], nt, preferred_element_type=f32)
        return total.astype(bf16)

    place_both = jnp.concatenate([place_mine, place_other], axis=-2)

    def pair_rows(v):
        halves = v.reshape(2, 2, 2, ring, most_rows, v.shape[-1])
        return jnp.concatenate([halves[0], swap_core(halves[1])], axis=-2)

    def spread(places, v):
        return jnp.einsum("...ct,...cd->...td", places, v, preferred_element_type=f32)

    def add(own, arrived):
        return (own.astype(f32) + arrived.astype(f32)).astype(bf16)

    def ring_sum(blocks):
        moving = blocks[ring - 1]
        for r in range(ring - 2, -1, -1):
            moving = add(blocks[r], ring_down(moving))
        return moving

    def sum_xyz(v):
        first = swap_x(spread(place_both[1], v[1]).astype(bf16))
        both = (spread(place_both[0], v[0]) + first.astype(f32)).astype(bf16)
        return ring_sum(add(both[0], swap_y(both[1])))

    def sum_yxz(v):
        first = swap_y(spread(place_both[:, 1], v[:, 1]).astype(bf16))
        both = (spread(place_both[:, 0], v[:, 0]) + first.astype(f32)).astype(bf16)
        return ring_sum(add(both[0], swap_x(both[1])))

    def sum_zyx(v):
        moving = spread(place_both[:, :, ring - 1], v[:, :, ring - 1]).astype(bf16)
        for r in range(ring - 2, -1, -1):
            here = spread(place_both[:, :, r], v[:, :, r])
            moving = (here + ring_down(moving).astype(f32)).astype(bf16)
        pair = add(moving[:, 0], swap_y(moving[:, 1]))
        return add(pair[0], swap_x(pair[1]))

    sums = (sum_xyz, sum_yxz, sum_zyx)
    grads = []
    for n in (2, 0, 1):
        part = row_grad_of(n)
        if n == 0:
            part = jnp.concatenate([gate_lanes, part], axis=1)
        grads.append(sums[n](pair_rows(part)))
    grads = [grads[1], grads[2], grads[0]]
    gate_back = grads[0][:, :device_count].astype(f32)
    input_grad = jnp.concatenate([grads[0][:, info_width:], grads[1], grads[2]], axis=1)
    gate_grad_out = jnp.sum(jnp.where(hit, gate_back[:, None, :], 0.0), axis=2).astype(bf16)

    tn = (((0,), (0,)), ((), ()))
    w_gate_grad = lax.dot_general(x_rows, pre_gate_grad, tn, preferred_element_type=f32)
    w_up_grad = lax.dot_general(x_rows, pre_up_grad, tn, preferred_element_type=f32)
    w_down_grad = lax.dot_general(weighted, c_rows, tn, preferred_element_type=f32)
    return (
        input_grad,
        gate_grad_out,
        w_gate_grad.astype(bf16)[None],
        w_up_grad.astype(bf16)[None],
        w_down_grad.astype(bf16)[None],
    )


def on_device(tokens, cotangent, routes, gates, w_gate, w_up, w_down):
    dp_count = lax.axis_size("dp")
    expert_count = lax.axis_size("expert")
    gathered_bytes = dp_count * expert_count * tokens.size * 2
    if dp_count == 4 and expert_count % 2 == 0 and gathered_bytes <= gather_limit:
        return gather_path(tokens, cotangent, routes, gates, w_gate, w_up, w_down)
    return exchange_path(tokens, cotangent, routes, gates, w_gate, w_up, w_down)


def solution(mesh):
    in_specs = (
        P(("dp", "expert"), None),
        P(("dp", "expert"), None),
        P(("dp", "expert"), None),
        P(("dp", "expert"), None),
        P(("dp", "expert"), None, None),
        P(("dp", "expert"), None, None),
        P(("dp", "expert"), None, None),
    )
    out_specs = (
        P(("dp", "expert"), None),
        P(("dp", "expert"), None),
        P(("dp", "expert"), None, None),
        P(("dp", "expert"), None, None),
        P(("dp", "expert"), None, None),
    )
    return jax.shard_map(
        on_device, mesh=mesh, in_specs=in_specs, out_specs=out_specs, check_vma=False
    )
```

```python
import jax
import jax.numpy as jnp
from jax import lax
from jax.experimental import pallas as pl
from jax.experimental.pallas import tpu as pltpu
from jax.sharding import PartitionSpec as P

block_rows = 256
gather_limit = 32 * 2**20


def expert_parts(inputs, cotangent_rows, router_weight, gate_matrix, up_matrix, down_matrix):
    pre_gate = jnp.dot(inputs, gate_matrix, preferred_element_type=jnp.float32)
    pre_up = jnp.dot(inputs, up_matrix, preferred_element_type=jnp.float32)
    sigmoid_gate = jax.nn.sigmoid(pre_gate)
    silu_gate = pre_gate * sigmoid_gate
    hidden = (silu_gate * pre_up).astype(jnp.bfloat16)
    expert_out = jnp.dot(hidden, down_matrix, preferred_element_type=jnp.float32)
    gate_grad = jnp.sum(cotangent_rows.astype(jnp.float32) * expert_out, axis=1).astype(
        jnp.bfloat16
    )
    out_grad = (
        router_weight.astype(jnp.float32)[:, None] * cotangent_rows.astype(jnp.float32)
    ).astype(jnp.bfloat16)
    hidden_grad = lax.dot_general(
        out_grad, down_matrix, (((1,), (1,)), ((), ())), preferred_element_type=jnp.float32
    )
    pre_gate_grad = (
        hidden_grad * pre_up * sigmoid_gate * (1.0 + pre_gate * (1.0 - sigmoid_gate))
    ).astype(jnp.bfloat16)
    pre_up_grad = (hidden_grad * silu_gate).astype(jnp.bfloat16)
    row_grad = lax.dot_general(
        pre_gate_grad, gate_matrix, (((1,), (1,)), ((), ())), preferred_element_type=jnp.float32
    )
    row_grad = row_grad + lax.dot_general(
        pre_up_grad, up_matrix, (((1,), (1,)), ((), ())), preferred_element_type=jnp.float32
    )
    return (row_grad.astype(jnp.bfloat16), gate_grad, pre_gate_grad, pre_up_grad, hidden, out_grad)


def outer_terms(inputs, pre_gate_grad, pre_up_grad, hidden, out_grad):
    gate_term = lax.dot_general(
        inputs, pre_gate_grad, (((0,), (0,)), ((), ())), preferred_element_type=jnp.float32
    )
    up_term = lax.dot_general(
        inputs, pre_up_grad, (((0,), (0,)), ((), ())), preferred_element_type=jnp.float32
    )
    down_term = lax.dot_general(
        hidden, out_grad, (((0,), (0,)), ((), ())), preferred_element_type=jnp.float32
    )
    return (gate_term, up_term, down_term)


def exchange_path(tokens, cotangent, routes, gates, w_gate, w_up, w_down):
    dp_count = lax.axis_size("dp")
    expert_count = lax.axis_size("expert")
    device_count = dp_count * expert_count
    tok_local, model_width = tokens.shape
    top_count = routes.shape[1]
    row_count = tok_local * top_count
    most_rows = 7 * row_count // (4 * device_count)
    slot_total = device_count * most_rows
    zero_value = jnp.zeros((), jnp.bfloat16)
    flat_expert = routes.reshape(row_count)
    onehot = (flat_expert[:, None] == jnp.arange(device_count, dtype=jnp.int32)[None, :]).astype(
        jnp.int32
    )
    rank_in_expert = jnp.sum(jnp.cumsum(onehot, axis=0) * onehot, axis=1) - 1
    slot_index = flat_expert * most_rows + rank_in_expert
    row_of_slot = (
        jnp.full((slot_total,), row_count, jnp.int32)
        .at[slot_index]
        .set(jnp.arange(row_count, dtype=jnp.int32))
    )
    slot_live = row_of_slot < row_count
    safe_row = jnp.minimum(row_of_slot, row_count - 1)
    token_of_slot = safe_row // top_count
    send_tokens = jnp.where(slot_live[:, None], tokens[token_of_slot], zero_value).reshape(
        device_count, most_rows, model_width
    )
    send_cotangent = jnp.where(slot_live[:, None], cotangent[token_of_slot], zero_value).reshape(
        device_count, most_rows, model_width
    )
    send_weight = jnp.where(slot_live, gates.reshape(row_count)[safe_row], zero_value).reshape(
        device_count, most_rows
    )
    arrived = (
        lax.all_to_all(send_tokens, ("dp", "expert"), split_axis=0, concat_axis=0, tiled=True),
        lax.all_to_all(send_cotangent, ("dp", "expert"), split_axis=0, concat_axis=0, tiled=True),
        lax.all_to_all(send_weight, ("dp", "expert"), split_axis=0, concat_axis=0, tiled=True),
    )
    got_tokens = arrived[0].reshape(slot_total, model_width)
    got_cotangent = arrived[1].reshape(slot_total, model_width)
    got_weight = arrived[2].reshape(slot_total)
    gate_matrix = w_gate[0]
    up_matrix = w_up[0]
    down_matrix = w_down[0]
    hidden_width = gate_matrix.shape[1]
    is_used = got_weight != zero_value
    used_count = jnp.sum(is_used.astype(jnp.int32))
    padded_total = -(-slot_total // block_rows) * block_rows
    compact_pos = jnp.cumsum(is_used.astype(jnp.int32)) - 1
    slot_of_compact = (
        jnp.full((padded_total,), slot_total, jnp.int32)
        .at[jnp.where(is_used, compact_pos, padded_total)]
        .set(jnp.arange(slot_total, dtype=jnp.int32), mode="drop")
    )
    block_count = (used_count + block_rows - 1) // block_rows

    def block_step(block_index, carried):
        gate_acc, up_acc, down_acc, grad_slots, gate_slots = carried
        picked = lax.dynamic_slice_in_dim(slot_of_compact, block_index * block_rows, block_rows)
        is_live = picked < slot_total
        safe_pick = jnp.minimum(picked, slot_total - 1)
        block_tokens = jnp.where(is_live[:, None], got_tokens[safe_pick], zero_value)
        block_cotangent = jnp.where(is_live[:, None], got_cotangent[safe_pick], zero_value)
        block_weight = jnp.where(is_live, got_weight[safe_pick], zero_value)
        row_grad, gate_grad, pre_gate_grad, pre_up_grad, hidden, out_grad = expert_parts(
            block_tokens, block_cotangent, block_weight, gate_matrix, up_matrix, down_matrix
        )
        gate_term, up_term, down_term = outer_terms(
            block_tokens, pre_gate_grad, pre_up_grad, hidden, out_grad
        )
        target = jnp.where(is_live, picked, slot_total)
        grad_slots = grad_slots.at[target].set(row_grad, mode="drop")
        gate_slots = gate_slots.at[target].set(gate_grad, mode="drop")
        return (
            gate_acc + gate_term,
            up_acc + up_term,
            down_acc + down_term,
            grad_slots,
            gate_slots,
        )

    initial = (
        jnp.zeros((model_width, hidden_width), jnp.float32),
        jnp.zeros((model_width, hidden_width), jnp.float32),
        jnp.zeros((hidden_width, model_width), jnp.float32),
        jnp.zeros((slot_total, model_width), jnp.bfloat16),
        jnp.zeros((slot_total,), jnp.bfloat16),
    )
    finished = lax.fori_loop(0, block_count, block_step, initial)
    gate_acc, up_acc, down_acc, grad_slots, gate_slots = finished
    grad_out = grad_slots.reshape(device_count, most_rows, model_width)
    gate_out = gate_slots.reshape(device_count, most_rows)
    returned = (
        lax.all_to_all(grad_out, ("dp", "expert"), split_axis=0, concat_axis=0, tiled=True),
        lax.all_to_all(gate_out, ("dp", "expert"), split_axis=0, concat_axis=0, tiled=True),
    )
    back_grad = returned[0].reshape(slot_total, model_width)
    back_gate = returned[1].reshape(slot_total)
    row_grads = back_grad[slot_index].reshape(tok_local, top_count, model_width)
    input_grad = jnp.sum(row_grads, axis=1, dtype=jnp.float32).astype(jnp.bfloat16)
    gate_grad = back_gate[slot_index].reshape(tok_local, top_count)
    return (
        input_grad,
        gate_grad,
        gate_acc.astype(jnp.bfloat16)[None],
        up_acc.astype(jnp.bfloat16)[None],
        down_acc.astype(jnp.bfloat16)[None],
    )


def gather_path(tokens, cotangent, routes, gates, w_gate, w_up, w_down):
    dp_count = lax.axis_size("dp")
    expert_count = lax.axis_size("expert")
    device_count = dp_count * expert_count
    tok_local, model_width = tokens.shape
    hidden_width = w_gate.shape[2]
    top_count = routes.shape[1]
    most_rows = 7 * tok_local * top_count // (4 * device_count)
    source_count = 16
    half_rows = source_count * most_rows
    bf16, f32 = jnp.bfloat16, jnp.float32

    def swap_core(v):
        return lax.ppermute(v, "dp", [(p, p ^ 1) for p in range(dp_count)])

    def swap_x(v):
        return lax.ppermute(v, "dp", [(p, p ^ 2) for p in range(dp_count)])

    def swap_y(v):
        return lax.ppermute(v, "expert", [(q, q ^ 1) for q in range(expert_count)])

    def ring_up(v):
        return lax.ppermute(
            v, "expert", [(q, (q + 2) % expert_count) for q in range(expert_count)]
        )

    def ring_down(v):
        return lax.ppermute(
            v, "expert", [(q, (q - 2) % expert_count) for q in range(expert_count)]
        )

    dp_index = lax.axis_index("dp")
    expert_index = lax.axis_index("expert")
    mine = dp_index * expert_count + expert_index
    other = (dp_index ^ 1) * expert_count + expert_index

    hit = routes[:, :, None] == jnp.arange(device_count, dtype=jnp.int32)[None, None, :]
    gate_dense = jnp.sum(jnp.where(hit, gates[:, :, None].astype(f32), 0.0), axis=1)
    named = jnp.sum(hit.astype(f32), axis=1)
    token_iota = jnp.arange(tok_local)
    before = (token_iota[None, :] < token_iota[:, None]).astype(bf16)
    rank = jnp.dot(before, named.astype(bf16), preferred_element_type=f32)
    rank = jnp.where(named > 0.0, rank, -1.0)
    info_width = -(-2 * device_count // 128) * 128
    info = jnp.concatenate(
        [
            gate_dense.astype(bf16),
            rank.astype(bf16),
            jnp.zeros((tok_local, info_width - 2 * device_count), bf16),
        ],
        axis=1,
    )

    cuts = (0, 3 * model_width // 8, 3 * model_width // 4, model_width)

    def part_of(v, n):
        return v[:, cuts[n] : cuts[n + 1]]

    def gather_zyx(v, near_axis, far_axis, a_first, hold=None):
        hops = [v]
        for _ in range(3):
            hops.append(ring_up(hops[-1]))
        blocks, where = [], {}
        for g in range(2):
            near = jnp.stack([hops[2 * g], hops[2 * g + 1]])
            both = jnp.concatenate([near, near_axis(near)])
            if g == 1 and hold is not None:
                both = hold(both)
            blocks += [both, far_axis(both)]
            for far in range(2):
                for mid in range(2):
                    for s in range(2):
                        i, j = (far, mid) if a_first else (mid, far)
                        where[g, i, j, s] = (2 * g + far, 2 * mid + s)
        return blocks, where

    def gather_xyz(v, hold=None):
        pair = jnp.stack([v, swap_x(v)])
        quad = jnp.concatenate([pair, swap_y(pair)])
        hops = [quad]
        for _ in range(3):
            hops.append(ring_up(hops[-1]))
        where = {}
        for r in range(4):
            for j in range(2):
                for i in range(2):
                    where[r // 2, i, j, r % 2] = (r, 2 * j + i)
        return hops, where

    gathers = (
        lambda v, hold=None: gather_zyx(v, swap_y, swap_x, True, hold),
        lambda v, hold=None: gather_zyx(v, swap_x, swap_y, False, hold),
        gather_xyz,
    )
    order = [(g, i, j, s) for g in range(2) for i in range(2) for j in range(2) for s in range(2)]

    def compact(gathered):
        blocks, where = gathered
        width = blocks[0].shape[-1]

        def body(places, *refs):
            ins, keep, give = refs[: len(blocks)], refs[-2], refs[-1]
            for n, source in enumerate(order):
                block, at = where[source]
                picked = jnp.dot(places[n], ins[block][at], preferred_element_type=f32)
                keep[n] = picked[:most_rows].astype(bf16)
                give[n] = picked[most_rows:].astype(bf16)

        shape = jax.ShapeDtypeStruct((source_count, most_rows, width), bf16)
        keep, give = pl.pallas_call(
            body,
            out_shape=(shape, shape),
            in_specs=[pl.BlockSpec(memory_space=pltpu.VMEM)] * (1 + len(blocks)),
            out_specs=(pl.BlockSpec(memory_space=pltpu.VMEM),) * 2,
            compiler_params=pltpu.CompilerParams(vmem_limit_bytes=24 * 2**20),
            cost_estimate=pl.CostEstimate(
                flops=2 * source_count * 2 * most_rows * tok_local * width,
                bytes_accessed=12 * 2**20,
                transcendentals=0,
            ),
        )(place_both, *blocks)
        return keep.reshape(half_rows, width), swap_core(give).reshape(half_rows, width)

    def row_call(body, ins, whole, outs, flops):
        block = half_rows // 4
        in_specs = []
        for v in ins:
            if v.ndim == 2:
                in_specs.append(pl.BlockSpec((block, v.shape[1]), lambda b: (b, 0)))
            else:
                in_specs.append(pl.BlockSpec((2, block, v.shape[2]), lambda b: (0, b, 0)))
        for v, shape, place in whole:
            in_specs.append(pl.BlockSpec(shape, lambda b, place=place: place))
        return pl.pallas_call(
            body,
            grid=(4,),
            out_shape=tuple(jax.ShapeDtypeStruct((2, half_rows, w), d) for w, d in outs),
            in_specs=in_specs,
            out_specs=tuple(pl.BlockSpec((2, block, w), lambda b: (0, b, 0)) for w, _ in outs),
            compiler_params=pltpu.CompilerParams(vmem_limit_bytes=48 * 2**20),
            cost_estimate=pl.CostEstimate(
                flops=flops, bytes_accessed=24 * 2**20, transcendentals=0
            ),
        )(*ins, *[v for v, _, _ in whole])

    nt = (((1,), (1,)), ((), ()))
    gate_matrix, up_matrix, down_matrix = w_gate[0], w_up[0], w_down[0]
    lanes = lax.broadcasted_iota(jnp.int32, (1, info_width), 1)
    lane_mask = (lanes == mine).astype(f32)
    mask_spec = (lane_mask, (1, info_width), (0, 0))
    unit = 2 * 2 * half_rows * model_width * hidden_width

    token_parts = [part_of(tokens, n) for n in range(3)]
    token_parts[0] = jnp.concatenate([info, token_parts[0]], axis=1)
    got = [gathers[n](token_parts[n]) for n in range(3)]
    blocks, where = got[0]
    got_info = jnp.stack([blocks[where[k][0]][where[k][1], :, :info_width] for k in order])
    slots = jnp.arange(most_rows, dtype=f32)

    def places_of(index):
        at = lax.broadcasted_iota(jnp.int32, got_info.shape, 2) == device_count + index
        ranks = jnp.sum(jnp.where(at, got_info, jnp.zeros((), bf16)).astype(f32), axis=-1)
        return (ranks[:, None, :] == slots[:, None]).astype(bf16)

    place_both = jnp.concatenate([places_of(mine), places_of(other)], axis=1)
    rows = [half for n in range(3) for half in compact(got[n])]

    def forward(*refs):
        halves, (gates_at, wg, wu), outs = refs[:6], refs[6:9], refs[9:]
        gated, slope, silu, weighted = outs
        for h in range(2):
            parts = [halves[h][:, info_width:], halves[2 + h][...], halves[4 + h][...]]
            row_gate = jnp.sum(
                halves[h][:, :info_width].astype(f32) * gates_at[...], axis=1, keepdims=True
            )
            pre_gate, pre_up = 0.0, 0.0
            for n in range(3):
                pre_gate += jnp.dot(
                    parts[n], wg[cuts[n] : cuts[n + 1]], preferred_element_type=f32
                )
                pre_up += jnp.dot(parts[n], wu[cuts[n] : cuts[n + 1]], preferred_element_type=f32)
            sigmoid_gate = 1.0 / (1.0 + jnp.exp(-pre_gate))
            silu_gate = pre_gate * sigmoid_gate
            hidden = silu_gate * pre_up
            gated[h] = hidden
            slope[h] = row_gate * pre_up * sigmoid_gate * (1.0 + pre_gate * (1.0 - sigmoid_gate))
            silu[h] = row_gate * silu_gate
            weighted[h] = (row_gate * hidden).astype(bf16)

    square = (model_width, hidden_width)
    hidden, slope, silu, weighted = row_call(
        forward,
        rows,
        [mask_spec, (gate_matrix, square, (0, 0)), (up_matrix, square, (0, 0))],
        [(hidden_width, f32)] * 3 + [(hidden_width, bf16)],
        2 * unit,
    )

    held = [hidden]

    def hold(v):
        v, held[0] = lax.optimization_barrier((v, held[0]))
        return v

    got_cot = [gathers[n](part_of(cotangent, n), hold if n < 2 else None) for n in range(3)]
    hidden = held[0]
    cot_rows = [half for n in (2, 1, 0) for half in compact(got_cot[n])]
    cot_rows = cot_rows[4:] + cot_rows[2:4] + cot_rows[:2]

    def row_grad(pgg, pug, wg, wu):
        return lax.dot_general(pgg, wg, nt, preferred_element_type=f32) + lax.dot_general(
            pug, wu, nt, preferred_element_type=f32
        )

    def backward(*refs):
        halves, (gated, slope, silu) = refs[:6], refs[6:9]
        (gates_at, wd, wg, wu), (pgg, pug, gate_lanes, last_grad) = refs[9:13], refs[13:]
        for h in range(2):
            back = 0.0
            for n in range(3):
                back += lax.dot_general(
                    halves[2 * n + h][...],
                    wd[:, cuts[n] : cuts[n + 1]],
                    nt,
                    preferred_element_type=f32,
                )
            gate_grad = jnp.sum(gated[h] * back, axis=1, keepdims=True)
            gate_lanes[h] = (gate_grad * gates_at[...]).astype(bf16)
            gate_side = (back * slope[h]).astype(bf16)
            up_side = (back * silu[h]).astype(bf16)
            pgg[h] = gate_side
            pug[h] = up_side
            last_grad[h] = row_grad(gate_side, up_side, wg[...], wu[...]).astype(bf16)

    last = (cuts[3] - cuts[2], hidden_width)
    third = (cuts[1], hidden_width)
    last_at = cuts[2] // last[0]
    pre_gate_grad, pre_up_grad, gate_lanes, grad_last = row_call(
        backward,
        cot_rows + [hidden, slope, silu],
        [
            mask_spec,
            (down_matrix, (hidden_width, model_width), (0, 0)),
            (gate_matrix, last, (last_at, 0)),
            (up_matrix, last, (last_at, 0)),
        ],
        [(hidden_width, bf16)] * 2 + [(info_width, bf16), (last[0], bf16)],
        3 * unit // 2,
    )

    def first_grad(pgg, pug, gate_lanes, wg, wu, out):
        for h in range(2):
            out[h, :, :info_width] = gate_lanes[h]
            out[h, :, info_width:] = row_grad(pgg[h], pug[h], wg[...], wu[...]).astype(bf16)

    def second_grad(pgg, pug, wg, wu, out):
        for h in range(2):
            out[h] = row_grad(pgg[h], pug[h], wg[...], wu[...]).astype(bf16)

    (grad_first,) = row_call(
        first_grad,
        [pre_gate_grad, pre_up_grad, gate_lanes],
        [(gate_matrix, third, (0, 0)), (up_matrix, third, (0, 0))],
        [(info_width + third[0], bf16)],
        3 * unit // 4,
    )
    (grad_second,) = row_call(
        second_grad,
        [pre_gate_grad, pre_up_grad],
        [(gate_matrix, third, (1, 0)), (up_matrix, third, (1, 0))],
        [(third[0], bf16)],
        3 * unit // 4,
    )

    place_grid = place_both.reshape(2, 2, 2, 2, 2 * most_rows, tok_local)

    def pair_rows(v):
        width = v.shape[-1]
        own = v[0].reshape(source_count, most_rows, width)
        given = swap_core(v[1]).reshape(source_count, most_rows, width)
        return jnp.concatenate([own, given], axis=1).reshape(2, 2, 2, 2, 2 * most_rows, width)

    def spread(places, v):
        return jnp.einsum("...ct,...cd->...td", places, v, preferred_element_type=f32)

    def add(own, arrived):
        return (own.astype(f32) + arrived.astype(f32)).astype(bf16)

    def sum_two(v, take, far_axis, near_axis):
        blocks = [None] * 4
        for g in (1, 0):
            moved = far_axis(spread(take(place_grid[g], 1), take(v[g], 1)).astype(bf16))
            near = add(spread(take(place_grid[g], 0), take(v[g], 0)), moved)
            pair = add(near[0], near_axis(near[1]))
            blocks[2 * g], blocks[2 * g + 1] = pair[0], pair[1]
        moving = blocks[3]
        for r in (2, 1, 0):
            moving = add(blocks[r], ring_down(moving))
        return moving

    def sum_xyz(v):
        return sum_two(v, lambda u, i: u[i], swap_x, swap_y)

    def sum_yxz(v):
        return sum_two(v, lambda u, j: u[:, j], swap_y, swap_x)

    def sum_zyx(v):
        def block(r):
            g, s = r // 2, r % 2
            return spread(place_grid[g, :, :, s], v[g, :, :, s])

        moving = block(3).astype(bf16)
        for r in (2, 1, 0):
            moving = add(block(r), ring_down(moving))
        pair = add(moving[:, 0], swap_y(moving[:, 1]))
        return add(pair[0], swap_x(pair[1]))

    sum_last = sum_zyx(pair_rows(grad_last))
    sum_first = sum_xyz(pair_rows(grad_first))
    sum_second = sum_yxz(pair_rows(grad_second))
    gate_back = sum_first[:, :device_count].astype(f32)
    input_grad = jnp.concatenate([sum_first[:, info_width:], sum_second, sum_last], axis=1)
    gate_grad_out = jnp.sum(jnp.where(hit, gate_back[:, None, :], 0.0), axis=2).astype(bf16)

    def whole(halves, skip):
        parts = [jnp.concatenate(halves[2 * n : 2 * n + 2]) for n in range(3)]
        return jnp.concatenate([parts[0][:, skip:], parts[1], parts[2]], axis=1)

    tn = (((0,), (0,)), ((), ()))
    x_rows = whole(rows, info_width)
    c_rows = whole(cot_rows, 0)

    def flat(v):
        return v.reshape(2 * half_rows, v.shape[-1])

    w_gate_grad = lax.dot_general(x_rows, flat(pre_gate_grad), tn, preferred_element_type=f32)
    w_up_grad = lax.dot_general(x_rows, flat(pre_up_grad), tn, preferred_element_type=f32)
    w_down_grad = lax.dot_general(flat(weighted), c_rows, tn, preferred_element_type=f32)
    return (
        input_grad,
        gate_grad_out,
        w_gate_grad.astype(bf16)[None],
        w_up_grad.astype(bf16)[None],
        w_down_grad.astype(bf16)[None],
    )


def on_device(tokens, cotangent, routes, gates, w_gate, w_up, w_down):
    dp_count = lax.axis_size("dp")
    expert_count = lax.axis_size("expert")
    gathered_bytes = dp_count * expert_count * tokens.size * 2
    if dp_count == 4 and expert_count == 8 and gathered_bytes <= gather_limit:
        return gather_path(tokens, cotangent, routes, gates, w_gate, w_up, w_down)
    return exchange_path(tokens, cotangent, routes, gates, w_gate, w_up, w_down)


def solution(mesh):
    in_specs = (
        P(("dp", "expert"), None),
        P(("dp", "expert"), None),
        P(("dp", "expert"), None),
        P(("dp", "expert"), None),
        P(("dp", "expert"), None, None),
        P(("dp", "expert"), None, None),
        P(("dp", "expert"), None, None),
    )
    out_specs = (
        P(("dp", "expert"), None),
        P(("dp", "expert"), None),
        P(("dp", "expert"), None, None),
        P(("dp", "expert"), None, None),
        P(("dp", "expert"), None, None),
    )
    return jax.shard_map(
        on_device, mesh=mesh, in_specs=in_specs, out_specs=out_specs, check_vma=False
    )
```

```python
import jax
import jax.numpy as jnp
from jax import lax
from jax.experimental import pallas as pl
from jax.experimental.pallas import tpu as pltpu
from jax.sharding import PartitionSpec as P

block_rows = 256
gather_limit = 32 * 2**20


def expert_parts(inputs, cotangent_rows, router_weight, gate_matrix, up_matrix, down_matrix):
    pre_gate = jnp.dot(inputs, gate_matrix, preferred_element_type=jnp.float32)
    pre_up = jnp.dot(inputs, up_matrix, preferred_element_type=jnp.float32)
    sigmoid_gate = jax.nn.sigmoid(pre_gate)
    silu_gate = pre_gate * sigmoid_gate
    hidden = (silu_gate * pre_up).astype(jnp.bfloat16)
    expert_out = jnp.dot(hidden, down_matrix, preferred_element_type=jnp.float32)
    gate_grad = jnp.sum(cotangent_rows.astype(jnp.float32) * expert_out, axis=1).astype(
        jnp.bfloat16
    )
    out_grad = (
        router_weight.astype(jnp.float32)[:, None] * cotangent_rows.astype(jnp.float32)
    ).astype(jnp.bfloat16)
    hidden_grad = lax.dot_general(
        out_grad, down_matrix, (((1,), (1,)), ((), ())), preferred_element_type=jnp.float32
    )
    pre_gate_grad = (
        hidden_grad * pre_up * sigmoid_gate * (1.0 + pre_gate * (1.0 - sigmoid_gate))
    ).astype(jnp.bfloat16)
    pre_up_grad = (hidden_grad * silu_gate).astype(jnp.bfloat16)
    row_grad = lax.dot_general(
        pre_gate_grad, gate_matrix, (((1,), (1,)), ((), ())), preferred_element_type=jnp.float32
    )
    row_grad = row_grad + lax.dot_general(
        pre_up_grad, up_matrix, (((1,), (1,)), ((), ())), preferred_element_type=jnp.float32
    )
    return (row_grad.astype(jnp.bfloat16), gate_grad, pre_gate_grad, pre_up_grad, hidden, out_grad)


def outer_terms(inputs, pre_gate_grad, pre_up_grad, hidden, out_grad):
    gate_term = lax.dot_general(
        inputs, pre_gate_grad, (((0,), (0,)), ((), ())), preferred_element_type=jnp.float32
    )
    up_term = lax.dot_general(
        inputs, pre_up_grad, (((0,), (0,)), ((), ())), preferred_element_type=jnp.float32
    )
    down_term = lax.dot_general(
        hidden, out_grad, (((0,), (0,)), ((), ())), preferred_element_type=jnp.float32
    )
    return (gate_term, up_term, down_term)


def exchange_path(tokens, cotangent, routes, gates, w_gate, w_up, w_down):
    dp_count = lax.axis_size("dp")
    expert_count = lax.axis_size("expert")
    device_count = dp_count * expert_count
    tok_local, model_width = tokens.shape
    top_count = routes.shape[1]
    row_count = tok_local * top_count
    most_rows = 7 * row_count // (4 * device_count)
    slot_total = device_count * most_rows
    zero_value = jnp.zeros((), jnp.bfloat16)
    flat_expert = routes.reshape(row_count)
    onehot = (flat_expert[:, None] == jnp.arange(device_count, dtype=jnp.int32)[None, :]).astype(
        jnp.int32
    )
    rank_in_expert = jnp.sum(jnp.cumsum(onehot, axis=0) * onehot, axis=1) - 1
    slot_index = flat_expert * most_rows + rank_in_expert
    row_of_slot = (
        jnp.full((slot_total,), row_count, jnp.int32)
        .at[slot_index]
        .set(jnp.arange(row_count, dtype=jnp.int32))
    )
    slot_live = row_of_slot < row_count
    safe_row = jnp.minimum(row_of_slot, row_count - 1)
    token_of_slot = safe_row // top_count
    send_tokens = jnp.where(slot_live[:, None], tokens[token_of_slot], zero_value).reshape(
        device_count, most_rows, model_width
    )
    send_cotangent = jnp.where(slot_live[:, None], cotangent[token_of_slot], zero_value).reshape(
        device_count, most_rows, model_width
    )
    send_weight = jnp.where(slot_live, gates.reshape(row_count)[safe_row], zero_value).reshape(
        device_count, most_rows
    )
    arrived = (
        lax.all_to_all(send_tokens, ("dp", "expert"), split_axis=0, concat_axis=0, tiled=True),
        lax.all_to_all(send_cotangent, ("dp", "expert"), split_axis=0, concat_axis=0, tiled=True),
        lax.all_to_all(send_weight, ("dp", "expert"), split_axis=0, concat_axis=0, tiled=True),
    )
    got_tokens = arrived[0].reshape(slot_total, model_width)
    got_cotangent = arrived[1].reshape(slot_total, model_width)
    got_weight = arrived[2].reshape(slot_total)
    gate_matrix = w_gate[0]
    up_matrix = w_up[0]
    down_matrix = w_down[0]
    hidden_width = gate_matrix.shape[1]
    is_used = got_weight != zero_value
    used_count = jnp.sum(is_used.astype(jnp.int32))
    padded_total = -(-slot_total // block_rows) * block_rows
    compact_pos = jnp.cumsum(is_used.astype(jnp.int32)) - 1
    slot_of_compact = (
        jnp.full((padded_total,), slot_total, jnp.int32)
        .at[jnp.where(is_used, compact_pos, padded_total)]
        .set(jnp.arange(slot_total, dtype=jnp.int32), mode="drop")
    )
    block_count = (used_count + block_rows - 1) // block_rows

    def block_step(block_index, carried):
        gate_acc, up_acc, down_acc, grad_slots, gate_slots = carried
        picked = lax.dynamic_slice_in_dim(slot_of_compact, block_index * block_rows, block_rows)
        is_live = picked < slot_total
        safe_pick = jnp.minimum(picked, slot_total - 1)
        block_tokens = jnp.where(is_live[:, None], got_tokens[safe_pick], zero_value)
        block_cotangent = jnp.where(is_live[:, None], got_cotangent[safe_pick], zero_value)
        block_weight = jnp.where(is_live, got_weight[safe_pick], zero_value)
        row_grad, gate_grad, pre_gate_grad, pre_up_grad, hidden, out_grad = expert_parts(
            block_tokens, block_cotangent, block_weight, gate_matrix, up_matrix, down_matrix
        )
        gate_term, up_term, down_term = outer_terms(
            block_tokens, pre_gate_grad, pre_up_grad, hidden, out_grad
        )
        target = jnp.where(is_live, picked, slot_total)
        grad_slots = grad_slots.at[target].set(row_grad, mode="drop")
        gate_slots = gate_slots.at[target].set(gate_grad, mode="drop")
        return (
            gate_acc + gate_term,
            up_acc + up_term,
            down_acc + down_term,
            grad_slots,
            gate_slots,
        )

    initial = (
        jnp.zeros((model_width, hidden_width), jnp.float32),
        jnp.zeros((model_width, hidden_width), jnp.float32),
        jnp.zeros((hidden_width, model_width), jnp.float32),
        jnp.zeros((slot_total, model_width), jnp.bfloat16),
        jnp.zeros((slot_total,), jnp.bfloat16),
    )
    finished = lax.fori_loop(0, block_count, block_step, initial)
    gate_acc, up_acc, down_acc, grad_slots, gate_slots = finished
    grad_out = grad_slots.reshape(device_count, most_rows, model_width)
    gate_out = gate_slots.reshape(device_count, most_rows)
    returned = (
        lax.all_to_all(grad_out, ("dp", "expert"), split_axis=0, concat_axis=0, tiled=True),
        lax.all_to_all(gate_out, ("dp", "expert"), split_axis=0, concat_axis=0, tiled=True),
    )
    back_grad = returned[0].reshape(slot_total, model_width)
    back_gate = returned[1].reshape(slot_total)
    row_grads = back_grad[slot_index].reshape(tok_local, top_count, model_width)
    input_grad = jnp.sum(row_grads, axis=1, dtype=jnp.float32).astype(jnp.bfloat16)
    gate_grad = back_gate[slot_index].reshape(tok_local, top_count)
    return (
        input_grad,
        gate_grad,
        gate_acc.astype(jnp.bfloat16)[None],
        up_acc.astype(jnp.bfloat16)[None],
        down_acc.astype(jnp.bfloat16)[None],
    )


def gather_path(tokens, cotangent, routes, gates, w_gate, w_up, w_down):
    dp_count = lax.axis_size("dp")
    expert_count = lax.axis_size("expert")
    device_count = dp_count * expert_count
    tok_local, model_width = tokens.shape
    hidden_width = w_gate.shape[2]
    top_count = routes.shape[1]
    most_rows = 7 * tok_local * top_count // (4 * device_count)
    source_count = 16
    half_rows = source_count * most_rows
    bf16, f32 = jnp.bfloat16, jnp.float32

    def swap_core(v):
        return lax.ppermute(v, "dp", [(p, p ^ 1) for p in range(dp_count)])

    def swap_x(v):
        return lax.ppermute(v, "dp", [(p, p ^ 2) for p in range(dp_count)])

    def swap_y(v):
        return lax.ppermute(v, "expert", [(q, q ^ 1) for q in range(expert_count)])

    def ring_up(v):
        return lax.ppermute(
            v, "expert", [(q, (q + 2) % expert_count) for q in range(expert_count)]
        )

    def ring_down(v):
        return lax.ppermute(
            v, "expert", [(q, (q - 2) % expert_count) for q in range(expert_count)]
        )

    dp_index = lax.axis_index("dp")
    expert_index = lax.axis_index("expert")
    mine = dp_index * expert_count + expert_index
    other = (dp_index ^ 1) * expert_count + expert_index

    hit = routes[:, :, None] == jnp.arange(device_count, dtype=jnp.int32)[None, None, :]
    gate_dense = jnp.sum(jnp.where(hit, gates[:, :, None].astype(f32), 0.0), axis=1)
    named = jnp.sum(hit.astype(f32), axis=1)
    token_iota = jnp.arange(tok_local)
    before = (token_iota[None, :] < token_iota[:, None]).astype(bf16)
    rank = jnp.dot(before, named.astype(bf16), preferred_element_type=f32)
    rank = jnp.where(named > 0.0, rank, -1.0)
    info_width = -(-2 * device_count // 128) * 128
    info = jnp.concatenate(
        [
            gate_dense.astype(bf16),
            rank.astype(bf16),
            jnp.zeros((tok_local, info_width - 2 * device_count), bf16),
        ],
        axis=1,
    )

    cuts = (0, 3 * model_width // 8, 3 * model_width // 4, model_width)

    def part_of(v, n):
        return v[:, cuts[n] : cuts[n + 1]]

    links = {"x": [], "y": [], "z": []}
    ways = {"x": swap_x, "y": swap_y, "z": ring_up, "d": ring_down}

    def send(way, v):
        queue = links["z" if way == "d" else way]
        if len(queue) >= 2:
            v, _ = lax.optimization_barrier((v, queue[-2]))
        queue.append(ways[way](v))
        return queue[-1]

    order = [(g, i, j, s) for g in range(2) for i in range(2) for j in range(2) for s in range(2)]
    where = [{}, {}, {}]
    for g, i, j, s in order:
        where[0][g, i, j, s] = (2 * g + i, 2 * j + s)
        where[1][g, i, j, s] = (2 * g + j, 2 * i + s)
        where[2][g, i, j, s] = (2 * g + s, 2 * j + i)

    def with_other(way, v):
        return jnp.concatenate([v, send(way, v)])

    def compact(blocks, where):
        width = blocks[0].shape[-1]

        def body(places, *refs):
            ins, keep, give = refs[: len(blocks)], refs[-2], refs[-1]
            for n, source in enumerate(order):
                block, at = where[source]
                picked = jnp.dot(places[n], ins[block][at], preferred_element_type=f32)
                keep[n] = picked[:most_rows].astype(bf16)
                give[n] = picked[most_rows:].astype(bf16)

        shape = jax.ShapeDtypeStruct((source_count, most_rows, width), bf16)
        keep, give = pl.pallas_call(
            body,
            out_shape=(shape, shape),
            in_specs=[pl.BlockSpec(memory_space=pltpu.VMEM)] * (1 + len(blocks)),
            out_specs=(pl.BlockSpec(memory_space=pltpu.VMEM),) * 2,
            compiler_params=pltpu.CompilerParams(vmem_limit_bytes=24 * 2**20),
            cost_estimate=pl.CostEstimate(
                flops=2 * source_count * 2 * most_rows * tok_local * width,
                bytes_accessed=12 * 2**20,
                transcendentals=0,
            ),
        )(place_both, *blocks)
        return keep.reshape(half_rows, width), swap_core(give).reshape(half_rows, width)

    block_rows_here = half_rows // 4

    def row_call(body, ins, whole, outs, flops):
        row_spec = [pl.BlockSpec((block_rows_here, v.shape[1]), lambda b: (b, 0)) for v in ins]
        whole_spec = [
            pl.BlockSpec(shape, lambda b, place=place: place, pipeline_mode=pl.Buffered(1))
            for _, shape, place in whole
        ]
        outs = [out for out in outs for _ in range(2)]
        return pl.pallas_call(
            body,
            grid=(4,),
            out_shape=tuple(jax.ShapeDtypeStruct((half_rows, w), d) for w, d in outs),
            in_specs=row_spec + whole_spec,
            out_specs=tuple(pl.BlockSpec((block_rows_here, w), lambda b: (b, 0)) for w, _ in outs),
            compiler_params=pltpu.CompilerParams(vmem_limit_bytes=44 * 2**20),
            cost_estimate=pl.CostEstimate(
                flops=flops, bytes_accessed=24 * 2**20, transcendentals=0
            ),
        )(*ins, *[v for v, _, _ in whole])

    def both_halves(refs, at=slice(None)):
        return jnp.concatenate([refs[0][:, at], refs[1][:, at]])

    def put(refs, v, at=slice(None)):
        refs[0][:, at] = v[:block_rows_here]
        refs[1][:, at] = v[block_rows_here:]

    nt = (((1,), (1,)), ((), ()))
    gate_matrix, up_matrix, down_matrix = w_gate[0], w_up[0], w_down[0]
    lanes = lax.broadcasted_iota(jnp.int32, (1, info_width), 1)
    lane_mask = (lanes == mine).astype(f32)
    mask_spec = (lane_mask, (1, info_width), (0, 0))
    unit = 2 * 2 * half_rows * model_width * hidden_width

    t0 = jnp.concatenate([part_of(tokens, 0), info], axis=1)
    t1, t2 = part_of(tokens, 1), part_of(tokens, 2)
    c0, c1, c2 = (part_of(cotangent, n) for n in range(3))
    t0_hops, t1_hops, c0_hops, c1_hops = [t0], [t1], [c0], [c1]

    def hop(hops):
        hops.append(send("z", hops[-1]))

    def near(way, hops, g):
        return with_other(way, jnp.stack([hops[2 * g], hops[2 * g + 1]]))

    hop(t0_hops)
    hop(t1_hops)
    t2_hops = [with_other("y", with_other("x", t2[None]))]
    t0_near = [near("y", t0_hops, 0)]
    t1_near = [near("x", t1_hops, 0)]
    hop(t0_hops)
    hop(t1_hops)
    t0_far = [send("x", t0_near[0])]
    t1_far = [send("y", t1_near[0])]
    hop(t0_hops)
    hop(t1_hops)
    t1_near.append(near("x", t1_hops, 1))
    t0_near.append(near("y", t0_hops, 1))
    hop(t2_hops)
    hop(c0_hops)
    hop(c1_hops)
    t0_far.append(send("x", t0_near[1]))
    t1_far.append(send("y", t1_near[1]))
    hop(t2_hops)
    c2_hops = [with_other("y", with_other("x", c2[None]))]
    c0_near = [near("y", c0_hops, 0)]
    c1_near = [near("x", c1_hops, 0)]
    hop(c0_hops)
    hop(c1_hops)
    hop(t2_hops)
    c0_far = [send("x", c0_near[0])]
    c1_far = [send("y", c1_near[0])]
    hop(c0_hops)
    hop(c1_hops)
    c1_near.append(near("x", c1_hops, 1))
    c0_near.append(near("y", c0_hops, 1))
    hop(c2_hops)
    c0_far.append(send("x", c0_near[1]))
    c1_far.append(send("y", c1_near[1]))
    hop(c2_hops)

    t0_blocks = [t0_near[0], t0_far[0], t0_near[1], t0_far[1]]
    t1_blocks = [t1_near[0], t1_far[0], t1_near[1], t1_far[1]]
    got_info = jnp.stack(
        [t0_blocks[where[0][k][0]][where[0][k][1], :, cuts[1] :] for k in order]
    )
    slots = jnp.arange(most_rows, dtype=f32)

    def places_of(index):
        at = lax.broadcasted_iota(jnp.int32, got_info.shape, 2) == device_count + index
        ranks = jnp.sum(jnp.where(at, got_info, jnp.zeros((), bf16)).astype(f32), axis=-1)
        return (ranks[:, None, :] == slots[:, None]).astype(bf16)

    place_both = jnp.concatenate([places_of(mine), places_of(other)], axis=1)
    rows = [
        half
        for n, blocks in enumerate((t0_blocks, t1_blocks, t2_hops))
        for half in compact(blocks, where[n])
    ]

    def forward(*refs):
        halves, (gates_at, wg, wu), outs = refs[:6], refs[6:9], refs[9:]
        parts = [both_halves(halves[2 * n : 2 * n + 2], slice(0, cuts[n + 1] - cuts[n])) for n in range(3)]
        sent = both_halves(halves[:2], slice(cuts[1], None))
        row_gate = jnp.sum(sent.astype(f32) * gates_at[...], axis=1, keepdims=True)
        pre_gate, pre_up = 0.0, 0.0
        for n in range(3):
            rows_at = slice(cuts[n], cuts[n + 1])
            pre_gate += jnp.dot(parts[n], wg[rows_at], preferred_element_type=f32)
            pre_up += jnp.dot(parts[n], wu[rows_at], preferred_element_type=f32)
        sigmoid_gate = 1.0 / (1.0 + jnp.exp(-pre_gate))
        silu_gate = pre_gate * sigmoid_gate
        hidden = silu_gate * pre_up
        put(outs[0:2], hidden)
        slope = pre_up * sigmoid_gate * (1.0 + pre_gate * (1.0 - sigmoid_gate))
        put(outs[2:4], row_gate * slope)
        put(outs[4:6], row_gate * silu_gate)
        put(outs[6:8], (row_gate * hidden).astype(bf16))

    square = (model_width, hidden_width)
    forward_out = row_call(
        forward,
        rows,
        [mask_spec, (gate_matrix, square, (0, 0)), (up_matrix, square, (0, 0))],
        [(hidden_width, f32)] * 3 + [(hidden_width, bf16)],
        2 * unit,
    )
    before_last, held = lax.optimization_barrier((c2_hops[-1], forward_out[0]))
    c2_hops.append(send("z", before_last))
    kept, weighted = (held,) + forward_out[1:6], forward_out[6:]
    c1_rows = compact([c1_near[0], c1_far[0], c1_near[1], c1_far[1]], where[1])
    c0_rows = compact([c0_near[0], c0_far[0], c0_near[1], c0_far[1]], where[0])
    cot_rows = [*c0_rows, *c1_rows, *compact(c2_hops, where[2])]

    def row_grad(pgg, pug, wg, wu):
        return lax.dot_general(pgg, wg, nt, preferred_element_type=f32) + lax.dot_general(
            pug, wu, nt, preferred_element_type=f32
        )

    def backward(*refs):
        halves, gated, slope, silu = refs[:6], refs[6:8], refs[8:10], refs[10:12]
        (gates_at, wd, wg, wu), outs = refs[12:16], refs[16:]
        back = 0.0
        for n in range(3):
            back += lax.dot_general(
                both_halves(halves[2 * n : 2 * n + 2]),
                wd[:, cuts[n] : cuts[n + 1]],
                nt,
                preferred_element_type=f32,
            )
        gate_grad = jnp.sum(both_halves(gated) * back, axis=1, keepdims=True)
        gate_side = (back * both_halves(slope)).astype(bf16)
        up_side = (back * both_halves(silu)).astype(bf16)
        put(outs[0:2], gate_side)
        put(outs[2:4], up_side)
        put(outs[4:6], (gate_grad * gates_at[...]).astype(bf16))
        put(outs[6:8], row_grad(gate_side, up_side, wg[...], wu[...]).astype(bf16))

    last = (cuts[3] - cuts[2], hidden_width)
    third = (cuts[1], hidden_width)
    last_at = cuts[2] // last[0]
    backward_out = row_call(
        backward,
        cot_rows + list(kept),
        [
            mask_spec,
            (down_matrix, (hidden_width, model_width), (0, 0)),
            (gate_matrix, last, (last_at, 0)),
            (up_matrix, last, (last_at, 0)),
        ],
        [(hidden_width, bf16)] * 2 + [(info_width, bf16), (last[0], bf16)],
        3 * unit // 2,
    )
    sides, gate_lanes, grad_last = backward_out[:4], backward_out[4:6], backward_out[6:]

    def first_grad(*refs):
        outs = refs[8:]
        grad = row_grad(both_halves(refs[0:2]), both_halves(refs[2:4]), refs[6][...], refs[7][...])
        put(outs, grad.astype(bf16), slice(0, cuts[1]))
        put(outs, both_halves(refs[4:6]), slice(cuts[1], None))

    def second_grad(*refs):
        grad = row_grad(both_halves(refs[0:2]), both_halves(refs[2:4]), refs[4][...], refs[5][...])
        put(refs[6:], grad.astype(bf16))

    grad_first = row_call(
        first_grad,
        [*sides, *gate_lanes],
        [(gate_matrix, third, (0, 0)), (up_matrix, third, (0, 0))],
        [(info_width + third[0], bf16)],
        3 * unit // 4,
    )
    grad_second = row_call(
        second_grad,
        [*sides],
        [(gate_matrix, third, (1, 0)), (up_matrix, third, (1, 0))],
        [(third[0], bf16)],
        3 * unit // 4,
    )

    place_grid = place_both.reshape(2, 2, 2, 2, 2 * most_rows, tok_local)

    def pair_rows(halves):
        width = halves[0].shape[-1]
        own = halves[0].reshape(source_count, most_rows, width)
        given = swap_core(halves[1]).reshape(source_count, most_rows, width)
        return jnp.concatenate([own, given], axis=1).reshape(2, 2, 2, 2, 2 * most_rows, width)

    def spread(places, v):
        return jnp.einsum("...ct,...cd->...td", places, v, preferred_element_type=f32)

    def add(own, arrived):
        return (own.astype(f32) + arrived.astype(f32)).astype(bf16)

    links["x"].clear()
    links["y"].clear()
    links["z"].clear()
    v2 = pair_rows(grad_last)
    v0 = pair_rows(grad_first)
    v1 = pair_rows(grad_second)

    def spread_last(r):
        return spread(place_grid[r // 2, :, :, r % 2], v2[r // 2, :, :, r % 2])

    first_last = spread_last(3).astype(bf16)
    moving2 = send("d", first_last)
    far0 = [spread(place_grid[g, 1], v0[g, 1]).astype(bf16) for g in range(2)]
    far1 = [spread(place_grid[g, :, 1], v1[g, :, 1]).astype(bf16) for g in range(2)]
    sent0, sent1, half0, half1, near0, near1 = ([None, None] for _ in range(6))
    sent0[1] = send("x", far0[1])
    sent1[1] = send("y", far1[1])
    sides_tied, _, _, _ = lax.optimization_barrier((sides, far0[1], far1[1], first_last))
    moving2 = send("d", add(spread_last(2), moving2))
    half1[1] = add(spread(place_grid[1, :, 0], v1[1, :, 0]), sent1[1])
    near1[1] = send("x", half1[1][1])
    half0[1] = add(spread(place_grid[1, 0], v0[1, 0]), sent0[1])
    near0[1] = send("y", half0[1][1])
    weighted_tied, _, _ = lax.optimization_barrier((weighted, half0[1], half1[1]))
    sent0[0] = send("x", far0[0])
    sent1[0] = send("y", far1[0])
    moving2 = send("d", add(spread_last(1), moving2))
    sum0_high = add(half0[1][0], near0[1])
    sum1_high = add(half1[1][0], near1[1])
    moving0 = send("d", sum0_high[1])
    moving1 = send("d", sum1_high[1])
    half1[0] = add(spread(place_grid[0, :, 0], v1[0, :, 0]), sent1[0])
    near1[0] = send("x", half1[0][1])
    half0[0] = add(spread(place_grid[0, 0], v0[0, 0]), sent0[0])
    near0[0] = send("y", half0[0][1])
    moving0 = send("d", add(sum0_high[0], moving0))
    moving1 = send("d", add(sum1_high[0], moving1))
    pair = add(spread_last(0), moving2)
    pair = add(pair[:, 0], send("y", pair[:, 1]))
    sum_last = add(pair[0], send("x", pair[1]))
    sum0_low = add(half0[0][0], near0[0])
    sum1_low = add(half1[0][0], near1[0])
    moving0 = send("d", add(sum0_low[1], moving0))
    moving1 = send("d", add(sum1_low[1], moving1))
    sum_first = add(sum0_low[0], moving0)
    sum_second = add(sum1_low[0], moving1)
    gate_back = sum_first[:, cuts[1] : cuts[1] + device_count].astype(f32)
    input_grad = jnp.concatenate([sum_first[:, : cuts[1]], sum_second, sum_last], axis=1)
    gate_grad_out = jnp.sum(jnp.where(hit, gate_back[:, None, :], 0.0), axis=2).astype(bf16)

    tile = 256
    firsts = [cut // tile for cut in cuts]

    def tile_spec(n):
        top = firsts[n + 1] - firsts[n] - 1
        return pl.BlockSpec(
            (half_rows, tile), lambda b: (0, jnp.clip(b - firsts[n], 0, top))
        )

    tile_specs = [tile_spec(n) for n in range(3) for _ in range(2)]
    tn = (((0,), (0,)), ((), ()))

    def tn_dot(a, b):
        return lax.dot_general(a, b, tn, preferred_element_type=f32)

    def side_weights(*refs):
        halves, (pgg0, pgg1, pug0, pug1), (gate_out, up_out) = refs[:6], refs[6:10], refs[10:]
        step = pl.program_id(0)
        for n in range(3):

            @pl.when((step >= firsts[n]) & (step < firsts[n + 1]))
            def _(n=n):
                x0, x1 = halves[2 * n][...], halves[2 * n + 1][...]
                gate_out[...] = (tn_dot(x0, pgg0[...]) + tn_dot(x1, pgg1[...])).astype(bf16)
                up_out[...] = (tn_dot(x0, pug0[...]) + tn_dot(x1, pug1[...])).astype(bf16)

    def down_weights(*refs):
        halves, (w0, w1), out = refs[:6], refs[6:8], refs[8]
        step = pl.program_id(0)
        for n in range(3):

            @pl.when((step >= firsts[n]) & (step < firsts[n + 1]))
            def _(n=n):
                c0_tile, c1_tile = halves[2 * n][...], halves[2 * n + 1][...]
                out[...] = (tn_dot(w0[...], c0_tile) + tn_dot(w1[...], c1_tile)).astype(bf16)

    half_spec = pl.BlockSpec(
        (half_rows, hidden_width), lambda b: (0, 0), pipeline_mode=pl.Buffered(1)
    )
    grad_spec = pl.BlockSpec((tile, hidden_width), lambda b: (b, 0))
    grad_shape = jax.ShapeDtypeStruct((model_width, hidden_width), bf16)
    w_gate_grad, w_up_grad = pl.pallas_call(
        side_weights,
        grid=(firsts[3],),
        out_shape=(grad_shape, grad_shape),
        in_specs=tile_specs + [half_spec] * 4,
        out_specs=(grad_spec, grad_spec),
        compiler_params=pltpu.CompilerParams(vmem_limit_bytes=28 * 2**20),
        cost_estimate=pl.CostEstimate(
            flops=2 * unit, bytes_accessed=20 * 2**20, transcendentals=0
        ),
    )(*rows, *sides_tied)
    w_down_grad = pl.pallas_call(
        down_weights,
        grid=(firsts[3],),
        out_shape=jax.ShapeDtypeStruct((hidden_width, model_width), bf16),
        in_specs=tile_specs + [half_spec] * 2,
        out_specs=pl.BlockSpec((hidden_width, tile), lambda b: (0, b)),
        compiler_params=pltpu.CompilerParams(vmem_limit_bytes=28 * 2**20),
        cost_estimate=pl.CostEstimate(flops=unit, bytes_accessed=14 * 2**20, transcendentals=0),
    )(*cot_rows, *weighted_tied)
    return (input_grad, gate_grad_out, w_gate_grad[None], w_up_grad[None], w_down_grad[None])


def on_device(tokens, cotangent, routes, gates, w_gate, w_up, w_down):
    dp_count = lax.axis_size("dp")
    expert_count = lax.axis_size("expert")
    gathered_bytes = dp_count * expert_count * tokens.size * 2
    if dp_count == 4 and expert_count == 8 and gathered_bytes <= gather_limit:
        return gather_path(tokens, cotangent, routes, gates, w_gate, w_up, w_down)
    return exchange_path(tokens, cotangent, routes, gates, w_gate, w_up, w_down)


def solution(mesh):
    in_specs = (
        P(("dp", "expert"), None),
        P(("dp", "expert"), None),
        P(("dp", "expert"), None),
        P(("dp", "expert"), None),
        P(("dp", "expert"), None, None),
        P(("dp", "expert"), None, None),
        P(("dp", "expert"), None, None),
    )
    out_specs = (
        P(("dp", "expert"), None),
        P(("dp", "expert"), None),
        P(("dp", "expert"), None, None),
        P(("dp", "expert"), None, None),
        P(("dp", "expert"), None, None),
    )
    return jax.shard_map(
        on_device, mesh=mesh, in_specs=in_specs, out_specs=out_specs, check_vma=False
    )
```

```python
import jax
import jax.numpy as jnp
from jax import lax
from jax.experimental import pallas as pl
from jax.experimental.pallas import tpu as pltpu
from jax.sharding import PartitionSpec as P

block_rows = 256
gather_limit = 32 * 2**20


def expert_parts(inputs, cotangent_rows, router_weight, gate_matrix, up_matrix, down_matrix):
    pre_gate = jnp.dot(inputs, gate_matrix, preferred_element_type=jnp.float32)
    pre_up = jnp.dot(inputs, up_matrix, preferred_element_type=jnp.float32)
    sigmoid_gate = jax.nn.sigmoid(pre_gate)
    silu_gate = pre_gate * sigmoid_gate
    hidden = (silu_gate * pre_up).astype(jnp.bfloat16)
    expert_out = jnp.dot(hidden, down_matrix, preferred_element_type=jnp.float32)
    gate_grad = jnp.sum(cotangent_rows.astype(jnp.float32) * expert_out, axis=1).astype(
        jnp.bfloat16
    )
    out_grad = (
        router_weight.astype(jnp.float32)[:, None] * cotangent_rows.astype(jnp.float32)
    ).astype(jnp.bfloat16)
    hidden_grad = lax.dot_general(
        out_grad, down_matrix, (((1,), (1,)), ((), ())), preferred_element_type=jnp.float32
    )
    pre_gate_grad = (
        hidden_grad * pre_up * sigmoid_gate * (1.0 + pre_gate * (1.0 - sigmoid_gate))
    ).astype(jnp.bfloat16)
    pre_up_grad = (hidden_grad * silu_gate).astype(jnp.bfloat16)
    row_grad = lax.dot_general(
        pre_gate_grad, gate_matrix, (((1,), (1,)), ((), ())), preferred_element_type=jnp.float32
    )
    row_grad = row_grad + lax.dot_general(
        pre_up_grad, up_matrix, (((1,), (1,)), ((), ())), preferred_element_type=jnp.float32
    )
    return (row_grad.astype(jnp.bfloat16), gate_grad, pre_gate_grad, pre_up_grad, hidden, out_grad)


def outer_terms(inputs, pre_gate_grad, pre_up_grad, hidden, out_grad):
    gate_term = lax.dot_general(
        inputs, pre_gate_grad, (((0,), (0,)), ((), ())), preferred_element_type=jnp.float32
    )
    up_term = lax.dot_general(
        inputs, pre_up_grad, (((0,), (0,)), ((), ())), preferred_element_type=jnp.float32
    )
    down_term = lax.dot_general(
        hidden, out_grad, (((0,), (0,)), ((), ())), preferred_element_type=jnp.float32
    )
    return (gate_term, up_term, down_term)


def exchange_path(tokens, cotangent, routes, gates, w_gate, w_up, w_down):
    dp_count = lax.axis_size("dp")
    expert_count = lax.axis_size("expert")
    device_count = dp_count * expert_count
    tok_local, model_width = tokens.shape
    top_count = routes.shape[1]
    row_count = tok_local * top_count
    most_rows = 7 * row_count // (4 * device_count)
    slot_total = device_count * most_rows
    zero_value = jnp.zeros((), jnp.bfloat16)
    flat_expert = routes.reshape(row_count)
    onehot = (flat_expert[:, None] == jnp.arange(device_count, dtype=jnp.int32)[None, :]).astype(
        jnp.int32
    )
    rank_in_expert = jnp.sum(jnp.cumsum(onehot, axis=0) * onehot, axis=1) - 1
    slot_index = flat_expert * most_rows + rank_in_expert
    row_of_slot = (
        jnp.full((slot_total,), row_count, jnp.int32)
        .at[slot_index]
        .set(jnp.arange(row_count, dtype=jnp.int32))
    )
    slot_live = row_of_slot < row_count
    safe_row = jnp.minimum(row_of_slot, row_count - 1)
    token_of_slot = safe_row // top_count
    send_tokens = jnp.where(slot_live[:, None], tokens[token_of_slot], zero_value).reshape(
        device_count, most_rows, model_width
    )
    send_cotangent = jnp.where(slot_live[:, None], cotangent[token_of_slot], zero_value).reshape(
        device_count, most_rows, model_width
    )
    send_weight = jnp.where(slot_live, gates.reshape(row_count)[safe_row], zero_value).reshape(
        device_count, most_rows
    )
    arrived = (
        lax.all_to_all(send_tokens, ("dp", "expert"), split_axis=0, concat_axis=0, tiled=True),
        lax.all_to_all(send_cotangent, ("dp", "expert"), split_axis=0, concat_axis=0, tiled=True),
        lax.all_to_all(send_weight, ("dp", "expert"), split_axis=0, concat_axis=0, tiled=True),
    )
    got_tokens = arrived[0].reshape(slot_total, model_width)
    got_cotangent = arrived[1].reshape(slot_total, model_width)
    got_weight = arrived[2].reshape(slot_total)
    gate_matrix = w_gate[0]
    up_matrix = w_up[0]
    down_matrix = w_down[0]
    hidden_width = gate_matrix.shape[1]
    is_used = got_weight != zero_value
    used_count = jnp.sum(is_used.astype(jnp.int32))
    padded_total = -(-slot_total // block_rows) * block_rows
    compact_pos = jnp.cumsum(is_used.astype(jnp.int32)) - 1
    slot_of_compact = (
        jnp.full((padded_total,), slot_total, jnp.int32)
        .at[jnp.where(is_used, compact_pos, padded_total)]
        .set(jnp.arange(slot_total, dtype=jnp.int32), mode="drop")
    )
    block_count = (used_count + block_rows - 1) // block_rows

    def block_step(block_index, carried):
        gate_acc, up_acc, down_acc, grad_slots, gate_slots = carried
        picked = lax.dynamic_slice_in_dim(slot_of_compact, block_index * block_rows, block_rows)
        is_live = picked < slot_total
        safe_pick = jnp.minimum(picked, slot_total - 1)
        block_tokens = jnp.where(is_live[:, None], got_tokens[safe_pick], zero_value)
        block_cotangent = jnp.where(is_live[:, None], got_cotangent[safe_pick], zero_value)
        block_weight = jnp.where(is_live, got_weight[safe_pick], zero_value)
        row_grad, gate_grad, pre_gate_grad, pre_up_grad, hidden, out_grad = expert_parts(
            block_tokens, block_cotangent, block_weight, gate_matrix, up_matrix, down_matrix
        )
        gate_term, up_term, down_term = outer_terms(
            block_tokens, pre_gate_grad, pre_up_grad, hidden, out_grad
        )
        target = jnp.where(is_live, picked, slot_total)
        grad_slots = grad_slots.at[target].set(row_grad, mode="drop")
        gate_slots = gate_slots.at[target].set(gate_grad, mode="drop")
        return (
            gate_acc + gate_term,
            up_acc + up_term,
            down_acc + down_term,
            grad_slots,
            gate_slots,
        )

    initial = (
        jnp.zeros((model_width, hidden_width), jnp.float32),
        jnp.zeros((model_width, hidden_width), jnp.float32),
        jnp.zeros((hidden_width, model_width), jnp.float32),
        jnp.zeros((slot_total, model_width), jnp.bfloat16),
        jnp.zeros((slot_total,), jnp.bfloat16),
    )
    finished = lax.fori_loop(0, block_count, block_step, initial)
    gate_acc, up_acc, down_acc, grad_slots, gate_slots = finished
    grad_out = grad_slots.reshape(device_count, most_rows, model_width)
    gate_out = gate_slots.reshape(device_count, most_rows)
    returned = (
        lax.all_to_all(grad_out, ("dp", "expert"), split_axis=0, concat_axis=0, tiled=True),
        lax.all_to_all(gate_out, ("dp", "expert"), split_axis=0, concat_axis=0, tiled=True),
    )
    back_grad = returned[0].reshape(slot_total, model_width)
    back_gate = returned[1].reshape(slot_total)
    row_grads = back_grad[slot_index].reshape(tok_local, top_count, model_width)
    input_grad = jnp.sum(row_grads, axis=1, dtype=jnp.float32).astype(jnp.bfloat16)
    gate_grad = back_gate[slot_index].reshape(tok_local, top_count)
    return (
        input_grad,
        gate_grad,
        gate_acc.astype(jnp.bfloat16)[None],
        up_acc.astype(jnp.bfloat16)[None],
        down_acc.astype(jnp.bfloat16)[None],
    )


def gather_path(tokens, cotangent, routes, gates, w_gate, w_up, w_down):
    dp_count = lax.axis_size("dp")
    expert_count = lax.axis_size("expert")
    device_count = dp_count * expert_count
    tok_local, model_width = tokens.shape
    hidden_width = w_gate.shape[2]
    top_count = routes.shape[1]
    most_rows = 7 * tok_local * top_count // (4 * device_count)
    source_count = 16
    half_rows = source_count * most_rows
    bf16, f32 = jnp.bfloat16, jnp.float32

    def swap_core(v):
        return lax.ppermute(v, "dp", [(p, p ^ 1) for p in range(dp_count)])

    def swap_x(v):
        return lax.ppermute(v, "dp", [(p, p ^ 2) for p in range(dp_count)])

    def swap_y(v):
        return lax.ppermute(v, "expert", [(q, q ^ 1) for q in range(expert_count)])

    def ring_up(v):
        return lax.ppermute(
            v, "expert", [(q, (q + 2) % expert_count) for q in range(expert_count)]
        )

    def ring_down(v):
        return lax.ppermute(
            v, "expert", [(q, (q - 2) % expert_count) for q in range(expert_count)]
        )

    dp_index = lax.axis_index("dp")
    expert_index = lax.axis_index("expert")
    mine = dp_index * expert_count + expert_index
    other = (dp_index ^ 1) * expert_count + expert_index

    hit = routes[:, :, None] == jnp.arange(device_count, dtype=jnp.int32)[None, None, :]
    gate_dense = jnp.sum(jnp.where(hit, gates[:, :, None].astype(f32), 0.0), axis=1)
    named = jnp.sum(hit.astype(f32), axis=1)
    token_iota = jnp.arange(tok_local)
    before = (token_iota[None, :] < token_iota[:, None]).astype(bf16)
    rank = jnp.dot(before, named.astype(bf16), preferred_element_type=f32)
    rank = jnp.where(named > 0.0, rank, -1.0)
    info_width = -(-2 * device_count // 128) * 128
    info = jnp.concatenate(
        [
            gate_dense.astype(bf16),
            rank.astype(bf16),
            jnp.zeros((tok_local, info_width - 2 * device_count), bf16),
        ],
        axis=1,
    )

    t_cuts = (0, model_width // 2, model_width)
    c_cuts = (0, model_width // 4, model_width // 2, model_width)
    cuts = (0, 3 * model_width // 8, 3 * model_width // 4, model_width)

    links = {"x": [], "y": [], "z": []}
    depth = {"x": 2, "y": 2, "z": 3}
    ways = {"x": swap_x, "y": swap_y, "z": ring_up, "d": ring_down}

    def send(way, v):
        link = "z" if way == "d" else way
        queue = links[link]
        if len(queue) >= depth[link]:
            v, _ = lax.optimization_barrier((v, queue[-depth[link]]))
        queue.append(ways[way](v))
        return queue[-1]

    order = [(g, i, j, s) for g in range(2) for i in range(2) for j in range(2) for s in range(2)]
    where = [{}, {}, {}, {}, {}]
    for g, i, j, s in order:
        where[0][g, i, j, s] = (2 * g + i, 2 * j + s)
        where[1][g, i, j, s] = (2 * g + j, 2 * i + s)
        where[2][g, i, j, s] = (2 * g + s, 2 * j + i)
        where[3][g, i, j, s] = (i, 4 * j + 2 * g + s)
        where[4][g, i, j, s] = (j, 4 * i + 2 * g + s)

    def with_other(way, v):
        return jnp.concatenate([v, send(way, v)])

    def compact(place_both, blocks, where):
        width = blocks[0].shape[-1]

        def body(places, *refs):
            ins, keep, give = refs[: len(blocks)], refs[-2], refs[-1]
            for n, source in enumerate(order):
                block, at = where[source]
                picked = jnp.dot(places[n], ins[block][at], preferred_element_type=f32)
                keep[n] = picked[:most_rows].astype(bf16)
                give[n] = picked[most_rows:].astype(bf16)

        shape = jax.ShapeDtypeStruct((source_count, most_rows, width), bf16)
        keep, give = pl.pallas_call(
            body,
            out_shape=(shape, shape),
            in_specs=[pl.BlockSpec(memory_space=pltpu.VMEM)] * (1 + len(blocks)),
            out_specs=(pl.BlockSpec(memory_space=pltpu.VMEM),) * 2,
            compiler_params=pltpu.CompilerParams(vmem_limit_bytes=24 * 2**20),
            cost_estimate=pl.CostEstimate(
                flops=2 * source_count * 2 * most_rows * tok_local * width, bytes_accessed=12 * 2**20, transcendentals=0,
            ),
        )(place_both, *blocks)
        return keep.reshape(half_rows, width), swap_core(give).reshape(half_rows, width)

    def row_call(body, ins, whole, outs, flops, steps=4, copies=2):
        block_rows_here = half_rows // steps
        row_spec = [pl.BlockSpec((block_rows_here, v.shape[1]), lambda b: (b, 0)) for v in ins]
        whole_spec = [
            pl.BlockSpec(shape, lambda b, place=place: place, pipeline_mode=pl.Buffered(1))
            for _, shape, place in whole
        ]
        outs = [out for out in outs for _ in range(copies)]
        return pl.pallas_call(
            body,
            grid=(steps,),
            out_shape=tuple(jax.ShapeDtypeStruct((half_rows, w), d) for w, d in outs),
            in_specs=row_spec + whole_spec,
            out_specs=tuple(pl.BlockSpec((block_rows_here, w), lambda b: (b, 0)) for w, _ in outs),
            compiler_params=pltpu.CompilerParams(vmem_limit_bytes=38 * 2**20),
            cost_estimate=pl.CostEstimate(
                flops=flops, bytes_accessed=flops // 200, transcendentals=0
            ),
        )(*ins, *[v for v, _, _ in whole])

    def both_halves(refs, at=slice(None)):
        return jnp.concatenate([refs[0][:, at], refs[1][:, at]])

    def put(refs, v, at=slice(None)):
        refs[0][:, at] = v[: v.shape[0] // 2]
        refs[1][:, at] = v[v.shape[0] // 2 :]

    nt = (((1,), (1,)), ((), ()))
    gate_matrix, up_matrix, down_matrix = w_gate[0], w_up[0], w_down[0]
    lanes = lax.broadcasted_iota(jnp.int32, (1, info_width), 1)
    lane_mask = (lanes == mine).astype(f32)
    mask_spec = (lane_mask, (1, info_width), (0, 0))
    unit = 2 * 2 * half_rows * model_width * hidden_width

    t0 = jnp.concatenate([tokens[:, : t_cuts[1]], info], axis=1)
    t1 = tokens[:, t_cuts[1] :]
    c0, c1, c2 = (cotangent[:, c_cuts[n] : c_cuts[n + 1]] for n in range(3))
    t0_hops, t1_hops, c0_hops, c1_hops = [t0], [t1], [c0], [c1]

    def hop(hops):
        hops.append(send("z", hops[-1]))

    def near(way, hops, g):
        return with_other(way, jnp.stack([hops[2 * g], hops[2 * g + 1]]))

    hop(t0_hops)
    hop(t1_hops)
    c2_hops = [with_other("y", with_other("x", c2[None]))]
    t0_near = [near("y", t0_hops, 0)]
    t1_near = [near("x", t1_hops, 0)]
    hop(t0_hops)
    hop(t1_hops)
    t0_far = [send("x", t0_near[0])]
    t1_far = [send("y", t1_near[0])]
    hop(t0_hops)
    hop(t1_hops)
    t1_near.append(near("x", t1_hops, 1))
    t0_near.append(near("y", t0_hops, 1))
    hop(c0_hops)
    hop(c1_hops)
    t0_far.append(send("x", t0_near[1]))
    t1_far.append(send("y", t1_near[1]))
    hop(c0_hops)
    hop(c1_hops)
    hop(c0_hops)
    hop(c1_hops)
    hop(c2_hops)
    c1_near = with_other("x", jnp.stack(c1_hops))
    c0_near = with_other("y", jnp.stack(c0_hops))
    hop(c2_hops)
    t0_blocks = [t0_near[0], t0_far[0], t0_near[1], t0_far[1]]
    t1_blocks = [t1_near[0], t1_far[0], t1_near[1], t1_far[1]]
    got_info = jnp.stack(
        [t0_blocks[where[0][k][0]][where[0][k][1], :, t_cuts[1] :] for k in order]
    )
    slots = jnp.arange(most_rows, dtype=f32)

    def places_of(index):
        at = lax.broadcasted_iota(jnp.int32, got_info.shape, 2) == device_count + index
        ranks = jnp.sum(jnp.where(at, got_info, jnp.zeros((), bf16)).astype(f32), axis=-1)
        return (ranks[:, None, :] == slots[:, None]).astype(bf16)

    place_both = jnp.concatenate([places_of(mine), places_of(other)], axis=1)
    rows = [
        half
        for n, blocks in enumerate((t0_blocks, t1_blocks))
        for half in compact(place_both, blocks, where[n])
    ]

    def forward(*refs):
        (part0, part1), (gates_at, wg, wu), outs = refs[:2], refs[2:5], refs[5:]
        sent = part0[:, t_cuts[1] :].astype(f32)
        row_gate = jnp.sum(sent * gates_at[...], axis=1, keepdims=True)
        parts = (part0[:, : t_cuts[1]], part1[...])
        pre_gate, pre_up = 0.0, 0.0
        for n in range(2):
            rows_at = slice(t_cuts[n], t_cuts[n + 1])
            pre_gate += jnp.dot(parts[n], wg[rows_at], preferred_element_type=f32)
            pre_up += jnp.dot(parts[n], wu[rows_at], preferred_element_type=f32)
        sigmoid_gate = 1.0 / (1.0 + jnp.exp(-pre_gate))
        silu_gate = pre_gate * sigmoid_gate
        hidden = silu_gate * pre_up
        outs[0][...] = hidden
        slope = pre_up * sigmoid_gate * (1.0 + pre_gate * (1.0 - sigmoid_gate))
        outs[1][...] = row_gate * slope
        outs[2][...] = row_gate * silu_gate
        outs[3][...] = (row_gate * hidden).astype(bf16)

    square = (model_width, hidden_width)
    def forward_half(part0, part1, flops):
        return row_call(
            forward,
            [part0, part1],
            [mask_spec, (gate_matrix, square, (0, 0)), (up_matrix, square, (0, 0))],
            [(hidden_width, f32)] * 3 + [(hidden_width, bf16)],
            flops,
            2,
            1,
        )

    forward_own = forward_half(rows[0], rows[2], 2 * unit)
    first_kept = forward_own[0]
    c0_far = send("x", c0_near)
    c1_far = send("y", c1_near)
    hop(c2_hops)
    given_in, _, _ = lax.optimization_barrier((rows[1], c0_near, c2_hops[2]))
    forward_out = [[first_kept, *forward_own[1:]], forward_half(given_in, rows[3], 2 * unit)]
    kept = [forward_out[h][n] for n in range(3) for h in range(2)]
    weighted = [forward_out[h][3] for h in range(2)]
    place_tied, kept[0], kept[1] = lax.optimization_barrier((place_both, kept[0], kept[1]))
    c1_rows = compact(place_tied, [c1_near, c1_far], where[4])
    c0_rows = compact(place_tied, [c0_near, c0_far], where[3])

    def early(*refs):
        total = 0.0
        for n in range(2):
            total += lax.dot_general(
                both_halves(refs[2 * n : 2 * n + 2]),
                refs[4][:, c_cuts[n] : c_cuts[n + 1]],
                nt,
                preferred_element_type=f32,
            )
        put(refs[5:], total)

    early_back = row_call(
        early,
        [*c0_rows, *c1_rows],
        [(down_matrix, (hidden_width, c_cuts[2]), (0, 0))],
        [(hidden_width, f32)],
        1024,
    )
    place_tied, early_first = lax.optimization_barrier((place_both, early_back[0]))
    early_back = [early_first, early_back[1]]
    c2_rows = compact(place_tied, c2_hops, where[2])
    cot_rows = [*c0_rows, *c1_rows, *c2_rows]

    def row_grad(pgg, pug, wg, wu):
        return lax.dot_general(pgg, wg, nt, preferred_element_type=f32) + lax.dot_general(
            pug, wu, nt, preferred_element_type=f32
        )

    def backward(*refs):
        half, first, gated, slope, silu, gates_at, wd, wg, wu = refs[:9]
        pgg, pug, grad0, grad1, grad2 = refs[9:]
        back = first[...] + lax.dot_general(
            half[...], wd[...], nt, preferred_element_type=f32
        )
        gate_grad = jnp.sum(gated[...] * back, axis=1, keepdims=True)
        gate_side = (back * slope[...]).astype(bf16)
        up_side = (back * silu[...]).astype(bf16)
        pgg[...] = gate_side
        pug[...] = up_side
        for n, out in ((2, grad2), (0, grad0), (1, grad1)):
            at = slice(cuts[n], cuts[n + 1])
            grad = row_grad(gate_side, up_side, wg[at], wu[at])
            out[:, : cuts[n + 1] - cuts[n]] = grad.astype(bf16)
        grad0[:, cuts[1] :] = (gate_grad * gates_at[...]).astype(bf16)

    def backward_half(h, half):
        return row_call(
            backward,
            [half, early_back[h], kept[h], kept[2 + h], kept[4 + h]],
            [
                mask_spec,
                (down_matrix, (hidden_width, c_cuts[3] - c_cuts[2]), (0, 1)),
                (gate_matrix, square, (0, 0)),
                (up_matrix, square, (0, 0)),
            ],
            [(hidden_width, bf16)] * 2
            + [(info_width + cuts[1], bf16), (cuts[2] - cuts[1], bf16), (cuts[3] - cuts[2], bf16)],
            1024,
            2,
            1,
        )

    given_out = backward_half(1, c2_rows[1])
    own_in, tied = lax.optimization_barrier((c2_rows[0], given_out[0]))
    own_out = backward_half(0, own_in)
    sides = [own_out[0], tied, own_out[1], given_out[1]]
    grad_first, grad_second, grad_last = ((own_out[n], given_out[n]) for n in (2, 3, 4))

    place_grid = place_both.reshape(2, 2, 2, 2, 2 * most_rows, tok_local)

    def pair_rows(halves):
        width = halves[0].shape[-1]
        own = halves[0].reshape(source_count, most_rows, width)
        given = swap_core(halves[1]).reshape(source_count, most_rows, width)
        return jnp.concatenate([own, given], axis=1).reshape(2, 2, 2, 2, 2 * most_rows, width)

    def spread(places, v):
        return jnp.einsum("...ct,...cd->...td", places, v, preferred_element_type=f32)

    def add(own, arrived):
        return (own.astype(f32) + arrived.astype(f32)).astype(bf16)

    links["x"].clear()
    links["y"].clear()
    links["z"].clear()
    depth.update(x=3, y=3, z=3)
    v2 = pair_rows(grad_last)
    v0 = pair_rows(grad_first)
    v1 = pair_rows(grad_second)

    def spread_last(r):
        return spread(place_grid[r // 2, :, :, r % 2], v2[r // 2, :, :, r % 2])

    first_last = spread_last(3).astype(bf16)
    far0 = [spread(place_grid[g, 1], v0[g, 1]).astype(bf16) for g in range(2)]
    far1 = [spread(place_grid[g, :, 1], v1[g, :, 1]).astype(bf16) for g in range(2)]
    first_last, far0, far1 = lax.optimization_barrier((first_last, far0, far1))
    moving2 = send("d", first_last)
    sent0, sent1, half0, half1, near0, near1 = ([None, None] for _ in range(6))
    sent0[1] = send("x", far0[1])
    sent1[1] = send("y", far1[1])
    sent0[0] = send("x", far0[0])
    sent1[0] = send("y", far1[0])
    gate_tied, _, _, _ = lax.optimization_barrier((sides[:2], far0, far1, first_last))
    moving2 = add(spread_last(2), moving2)
    up_tied, moving2 = lax.optimization_barrier((sides[2:], moving2))
    moving2 = send("d", moving2)
    half1[1] = add(spread(place_grid[1, :, 0], v1[1, :, 0]), sent1[1])
    half0[1] = add(spread(place_grid[1, 0], v0[1, 0]), sent0[1])
    moving2 = add(spread_last(1), moving2)
    half1[1], half0[1], moving2 = lax.optimization_barrier((half1[1], half0[1], moving2))
    moving2 = send("d", moving2)
    near1[1] = send("x", half1[1][1])
    near0[1] = send("y", half0[1][1])
    half1[0] = add(spread(place_grid[0, :, 0], v1[0, :, 0]), sent1[0])
    half0[0] = add(spread(place_grid[0, 0], v0[0, 0]), sent0[0])
    near1[0] = send("x", half1[0][1])
    near0[0] = send("y", half0[0][1])
    sum0_high = add(half0[1][0], near0[1])
    sum1_high = add(half1[1][0], near1[1])
    weighted_tied, _, _ = lax.optimization_barrier((weighted, half0[0], half1[0]))
    moving0 = send("d", sum0_high[1])
    moving1 = send("d", sum1_high[1])
    pair = add(spread_last(0), moving2)
    pair = add(pair[:, 0], send("y", pair[:, 1]))
    sum_last = add(pair[0], send("x", pair[1]))
    moving0 = send("d", add(sum0_high[0], moving0))
    moving1 = send("d", add(sum1_high[0], moving1))
    sum0_low = add(half0[0][0], near0[0])
    sum1_low = add(half1[0][0], near1[0])
    moving0 = send("d", add(sum0_low[1], moving0))
    moving1 = send("d", add(sum1_low[1], moving1))
    sum_first = add(sum0_low[0], moving0)
    sum_second = add(sum1_low[0], moving1)
    gate_back = sum_first[:, cuts[1] : cuts[1] + device_count].astype(f32)
    input_grad = jnp.concatenate([sum_first[:, : cuts[1]], sum_second, sum_last], axis=1)
    gate_grad_out = jnp.sum(jnp.where(hit, gate_back[:, None, :], 0.0), axis=2).astype(bf16)

    tile = 256
    tn = (((0,), (0,)), ((), ()))

    def tn_dot(a, b):
        return lax.dot_general(a, b, tn, preferred_element_type=f32)

    def weight_call(body, halves, cuts, wide, out_spec, out_shape):
        firsts = [cut // tile for cut in cuts]
        count = len(halves)

        def run(*refs):
            step = pl.program_id(0)
            for n in range(count // 2):

                @pl.when((step >= firsts[n]) & (step < firsts[n + 1]))
                def _(n=n):
                    tiles = (refs[2 * n][...], refs[2 * n + 1][...])
                    refs[-1][...] = body(tiles, refs[count : count + 2]).astype(bf16)

        def tile_spec(n):
            low, top = firsts[n], firsts[n + 1] - firsts[n] - 1
            return pl.BlockSpec((half_rows, tile), lambda b: (0, jnp.clip(b - low, 0, top)))

        half_spec = pl.BlockSpec(
            (half_rows, hidden_width), lambda b: (0, 0), pipeline_mode=pl.Buffered(1)
        )
        return pl.pallas_call(
            run,
            grid=(firsts[-1],),
            out_shape=jax.ShapeDtypeStruct(out_shape, bf16),
            in_specs=[tile_spec(n // 2) for n in range(count)] + [half_spec] * 2,
            out_specs=out_spec,
            compiler_params=pltpu.CompilerParams(vmem_limit_bytes=16 * 2**20),
            cost_estimate=pl.CostEstimate(
                flops=unit, bytes_accessed=14 * 2**20, transcendentals=0
            ),
        )(*halves, *wide)

    def side_weights(sides):
        return weight_call(
            lambda x, side: tn_dot(x[0], side[0][...]) + tn_dot(x[1], side[1][...]),
            rows,
            t_cuts,
            sides,
            pl.BlockSpec((tile, hidden_width), lambda b: (b, 0)),
            (model_width, hidden_width),
        )

    w_gate_grad = side_weights(gate_tied)
    w_up_grad = side_weights(up_tied)
    w_down_grad = weight_call(
        lambda c, w: tn_dot(w[0][...], c[0]) + tn_dot(w[1][...], c[1]),
        cot_rows,
        c_cuts,
        weighted_tied,
        pl.BlockSpec((hidden_width, tile), lambda b: (0, b)),
        (hidden_width, model_width),
    )
    return (input_grad, gate_grad_out, w_gate_grad[None], w_up_grad[None], w_down_grad[None])


def on_device(tokens, cotangent, routes, gates, w_gate, w_up, w_down):
    dp_count = lax.axis_size("dp")
    expert_count = lax.axis_size("expert")
    gathered_bytes = dp_count * expert_count * tokens.size * 2
    if dp_count == 4 and expert_count == 8 and gathered_bytes <= gather_limit:
        return gather_path(tokens, cotangent, routes, gates, w_gate, w_up, w_down)
    return exchange_path(tokens, cotangent, routes, gates, w_gate, w_up, w_down)


def solution(mesh):
    in_specs = (
        P(("dp", "expert"), None),
        P(("dp", "expert"), None),
        P(("dp", "expert"), None),
        P(("dp", "expert"), None),
        P(("dp", "expert"), None, None),
        P(("dp", "expert"), None, None),
        P(("dp", "expert"), None, None),
    )
    out_specs = (
        P(("dp", "expert"), None),
        P(("dp", "expert"), None),
        P(("dp", "expert"), None, None),
        P(("dp", "expert"), None, None),
        P(("dp", "expert"), None, None),
    )
    return jax.shard_map(
        on_device, mesh=mesh, in_specs=in_specs, out_specs=out_specs, check_vma=False
    )
```

```python
import jax
import jax.numpy as jnp
from jax import lax
from jax.experimental import pallas as pl
from jax.experimental.pallas import tpu as pltpu
from jax.sharding import PartitionSpec as P

block_rows = 256
gather_limit = 32 * 2**20


def expert_parts(inputs, cotangent_rows, router_weight, gate_matrix, up_matrix, down_matrix):
    pre_gate = jnp.dot(inputs, gate_matrix, preferred_element_type=jnp.float32)
    pre_up = jnp.dot(inputs, up_matrix, preferred_element_type=jnp.float32)
    sigmoid_gate = jax.nn.sigmoid(pre_gate)
    silu_gate = pre_gate * sigmoid_gate
    hidden = (silu_gate * pre_up).astype(jnp.bfloat16)
    expert_out = jnp.dot(hidden, down_matrix, preferred_element_type=jnp.float32)
    gate_grad = jnp.sum(cotangent_rows.astype(jnp.float32) * expert_out, axis=1).astype(
        jnp.bfloat16
    )
    out_grad = (
        router_weight.astype(jnp.float32)[:, None] * cotangent_rows.astype(jnp.float32)
    ).astype(jnp.bfloat16)
    hidden_grad = lax.dot_general(
        out_grad, down_matrix, (((1,), (1,)), ((), ())), preferred_element_type=jnp.float32
    )
    pre_gate_grad = (
        hidden_grad * pre_up * sigmoid_gate * (1.0 + pre_gate * (1.0 - sigmoid_gate))
    ).astype(jnp.bfloat16)
    pre_up_grad = (hidden_grad * silu_gate).astype(jnp.bfloat16)
    row_grad = lax.dot_general(
        pre_gate_grad, gate_matrix, (((1,), (1,)), ((), ())), preferred_element_type=jnp.float32
    )
    row_grad = row_grad + lax.dot_general(
        pre_up_grad, up_matrix, (((1,), (1,)), ((), ())), preferred_element_type=jnp.float32
    )
    return (row_grad.astype(jnp.bfloat16), gate_grad, pre_gate_grad, pre_up_grad, hidden, out_grad)


def outer_terms(inputs, pre_gate_grad, pre_up_grad, hidden, out_grad):
    gate_term = lax.dot_general(
        inputs, pre_gate_grad, (((0,), (0,)), ((), ())), preferred_element_type=jnp.float32
    )
    up_term = lax.dot_general(
        inputs, pre_up_grad, (((0,), (0,)), ((), ())), preferred_element_type=jnp.float32
    )
    down_term = lax.dot_general(
        hidden, out_grad, (((0,), (0,)), ((), ())), preferred_element_type=jnp.float32
    )
    return (gate_term, up_term, down_term)


def exchange_path(tokens, cotangent, routes, gates, w_gate, w_up, w_down):
    dp_count = lax.axis_size("dp")
    expert_count = lax.axis_size("expert")
    device_count = dp_count * expert_count
    tok_local, model_width = tokens.shape
    top_count = routes.shape[1]
    row_count = tok_local * top_count
    most_rows = 7 * row_count // (4 * device_count)
    slot_total = device_count * most_rows
    zero_value = jnp.zeros((), jnp.bfloat16)
    flat_expert = routes.reshape(row_count)
    onehot = (flat_expert[:, None] == jnp.arange(device_count, dtype=jnp.int32)[None, :]).astype(
        jnp.int32
    )
    rank_in_expert = jnp.sum(jnp.cumsum(onehot, axis=0) * onehot, axis=1) - 1
    slot_index = flat_expert * most_rows + rank_in_expert
    row_of_slot = (
        jnp.full((slot_total,), row_count, jnp.int32)
        .at[slot_index]
        .set(jnp.arange(row_count, dtype=jnp.int32))
    )
    slot_live = row_of_slot < row_count
    safe_row = jnp.minimum(row_of_slot, row_count - 1)
    token_of_slot = safe_row // top_count
    send_tokens = jnp.where(slot_live[:, None], tokens[token_of_slot], zero_value).reshape(
        device_count, most_rows, model_width
    )
    send_cotangent = jnp.where(slot_live[:, None], cotangent[token_of_slot], zero_value).reshape(
        device_count, most_rows, model_width
    )
    send_weight = jnp.where(slot_live, gates.reshape(row_count)[safe_row], zero_value).reshape(
        device_count, most_rows
    )
    arrived = (
        lax.all_to_all(send_tokens, ("dp", "expert"), split_axis=0, concat_axis=0, tiled=True),
        lax.all_to_all(send_cotangent, ("dp", "expert"), split_axis=0, concat_axis=0, tiled=True),
        lax.all_to_all(send_weight, ("dp", "expert"), split_axis=0, concat_axis=0, tiled=True),
    )
    got_tokens = arrived[0].reshape(slot_total, model_width)
    got_cotangent = arrived[1].reshape(slot_total, model_width)
    got_weight = arrived[2].reshape(slot_total)
    gate_matrix = w_gate[0]
    up_matrix = w_up[0]
    down_matrix = w_down[0]
    hidden_width = gate_matrix.shape[1]
    is_used = got_weight != zero_value
    used_count = jnp.sum(is_used.astype(jnp.int32))
    padded_total = -(-slot_total // block_rows) * block_rows
    compact_pos = jnp.cumsum(is_used.astype(jnp.int32)) - 1
    slot_of_compact = (
        jnp.full((padded_total,), slot_total, jnp.int32)
        .at[jnp.where(is_used, compact_pos, padded_total)]
        .set(jnp.arange(slot_total, dtype=jnp.int32), mode="drop")
    )
    block_count = (used_count + block_rows - 1) // block_rows

    def block_step(block_index, carried):
        gate_acc, up_acc, down_acc, grad_slots, gate_slots = carried
        picked = lax.dynamic_slice_in_dim(slot_of_compact, block_index * block_rows, block_rows)
        is_live = picked < slot_total
        safe_pick = jnp.minimum(picked, slot_total - 1)
        block_tokens = jnp.where(is_live[:, None], got_tokens[safe_pick], zero_value)
        block_cotangent = jnp.where(is_live[:, None], got_cotangent[safe_pick], zero_value)
        block_weight = jnp.where(is_live, got_weight[safe_pick], zero_value)
        row_grad, gate_grad, pre_gate_grad, pre_up_grad, hidden, out_grad = expert_parts(
            block_tokens, block_cotangent, block_weight, gate_matrix, up_matrix, down_matrix
        )
        gate_term, up_term, down_term = outer_terms(
            block_tokens, pre_gate_grad, pre_up_grad, hidden, out_grad
        )
        target = jnp.where(is_live, picked, slot_total)
        grad_slots = grad_slots.at[target].set(row_grad, mode="drop")
        gate_slots = gate_slots.at[target].set(gate_grad, mode="drop")
        return (
            gate_acc + gate_term,
            up_acc + up_term,
            down_acc + down_term,
            grad_slots,
            gate_slots,
        )

    initial = (
        jnp.zeros((model_width, hidden_width), jnp.float32),
        jnp.zeros((model_width, hidden_width), jnp.float32),
        jnp.zeros((hidden_width, model_width), jnp.float32),
        jnp.zeros((slot_total, model_width), jnp.bfloat16),
        jnp.zeros((slot_total,), jnp.bfloat16),
    )
    finished = lax.fori_loop(0, block_count, block_step, initial)
    gate_acc, up_acc, down_acc, grad_slots, gate_slots = finished
    grad_out = grad_slots.reshape(device_count, most_rows, model_width)
    gate_out = gate_slots.reshape(device_count, most_rows)
    returned = (
        lax.all_to_all(grad_out, ("dp", "expert"), split_axis=0, concat_axis=0, tiled=True),
        lax.all_to_all(gate_out, ("dp", "expert"), split_axis=0, concat_axis=0, tiled=True),
    )
    back_grad = returned[0].reshape(slot_total, model_width)
    back_gate = returned[1].reshape(slot_total)
    row_grads = back_grad[slot_index].reshape(tok_local, top_count, model_width)
    input_grad = jnp.sum(row_grads, axis=1, dtype=jnp.float32).astype(jnp.bfloat16)
    gate_grad = back_gate[slot_index].reshape(tok_local, top_count)
    return (
        input_grad,
        gate_grad,
        gate_acc.astype(jnp.bfloat16)[None],
        up_acc.astype(jnp.bfloat16)[None],
        down_acc.astype(jnp.bfloat16)[None],
    )


def gather_path(tokens, cotangent, routes, gates, w_gate, w_up, w_down):
    dp_count = lax.axis_size("dp")
    expert_count = lax.axis_size("expert")
    device_count = dp_count * expert_count
    tok_local, model_width = tokens.shape
    hidden_width = w_gate.shape[2]
    top_count = routes.shape[1]
    most_rows = 7 * tok_local * top_count // (4 * device_count)
    source_count = 16
    half_rows = source_count * most_rows
    bf16, f32 = jnp.bfloat16, jnp.float32

    def swap_core(v):
        return lax.ppermute(v, "dp", [(p, p ^ 1) for p in range(dp_count)])

    def swap_x(v):
        return lax.ppermute(v, "dp", [(p, p ^ 2) for p in range(dp_count)])

    def swap_y(v):
        return lax.ppermute(v, "expert", [(q, q ^ 1) for q in range(expert_count)])

    def ring_up(v):
        return lax.ppermute(
            v, "expert", [(q, (q + 2) % expert_count) for q in range(expert_count)]
        )

    def ring_down(v):
        return lax.ppermute(
            v, "expert", [(q, (q - 2) % expert_count) for q in range(expert_count)]
        )

    dp_index = lax.axis_index("dp")
    expert_index = lax.axis_index("expert")
    mine = dp_index * expert_count + expert_index
    other = (dp_index ^ 1) * expert_count + expert_index

    hit = routes[:, :, None] == jnp.arange(device_count, dtype=jnp.int32)[None, None, :]
    gate_dense = jnp.sum(jnp.where(hit, gates[:, :, None].astype(f32), 0.0), axis=1)
    named = jnp.sum(hit.astype(f32), axis=1)
    token_iota = jnp.arange(tok_local)
    before = (token_iota[None, :] < token_iota[:, None]).astype(bf16)
    rank = jnp.dot(before, named.astype(bf16), preferred_element_type=f32)
    rank = jnp.where(named > 0.0, rank, -1.0)
    info_width = -(-2 * device_count // 128) * 128
    info = jnp.concatenate(
        [
            gate_dense.astype(bf16),
            rank.astype(bf16),
            jnp.zeros((tok_local, info_width - 2 * device_count), bf16),
        ],
        axis=1,
    )

    t_cuts = (0, model_width // 2, model_width)
    c_cuts = (0, model_width // 4, model_width // 2, model_width)
    cuts = (0, 3 * model_width // 8, 3 * model_width // 4, model_width)

    links = {"x": [], "y": [], "z": []}
    depth = {"x": 2, "y": 2, "z": 3}
    ways = {"x": swap_x, "y": swap_y, "z": ring_up, "d": ring_down}

    def send(way, v):
        link = "z" if way == "d" else way
        queue = links[link]
        if len(queue) >= depth[link]:
            v, _ = lax.optimization_barrier((v, queue[-depth[link]]))
        queue.append(ways[way](v))
        return queue[-1]

    order = [(g, i, j, s) for g in range(2) for i in range(2) for j in range(2) for s in range(2)]
    where = [{}, {}, {}, {}, {}]
    for g, i, j, s in order:
        where[0][g, i, j, s] = (2 * g + i, 2 * j + s)
        where[1][g, i, j, s] = (2 * g + j, 2 * i + s)
        where[2][g, i, j, s] = (2 * g + s, 2 * j + i)
        where[3][g, i, j, s] = (i, 4 * j + 2 * g + s)
        where[4][g, i, j, s] = (j, 4 * i + 2 * g + s)

    def with_other(way, v):
        return jnp.concatenate([v, send(way, v)])

    def compact(place_both, blocks, where):
        width = blocks[0].shape[-1]

        def body(places, *refs):
            ins, keep, give = refs[: len(blocks)], refs[-2], refs[-1]
            for n, source in enumerate(order):
                block, at = where[source]
                picked = jnp.dot(places[n], ins[block][at], preferred_element_type=f32)
                keep[n] = picked[:most_rows].astype(bf16)
                give[n] = picked[most_rows:].astype(bf16)

        shape = jax.ShapeDtypeStruct((source_count, most_rows, width), bf16)
        keep, give = pl.pallas_call(
            body,
            out_shape=(shape, shape),
            in_specs=[pl.BlockSpec(memory_space=pltpu.VMEM)] * (1 + len(blocks)),
            out_specs=(pl.BlockSpec(memory_space=pltpu.VMEM),) * 2,
            compiler_params=pltpu.CompilerParams(vmem_limit_bytes=24 * 2**20),
            cost_estimate=pl.CostEstimate(
                flops=2 * source_count * 2 * most_rows * tok_local * width, bytes_accessed=12 * 2**20, transcendentals=0,
            ),
        )(place_both, *blocks)
        return keep.reshape(half_rows, width), swap_core(give).reshape(half_rows, width)

    def row_call(body, ins, whole, outs, flops, steps=4, copies=2):
        block_rows_here = half_rows // steps
        row_spec = [pl.BlockSpec((block_rows_here, v.shape[1]), lambda b: (b, 0)) for v in ins]
        whole_spec = [
            pl.BlockSpec(shape, lambda b, place=place: place, pipeline_mode=pl.Buffered(1))
            for _, shape, place in whole
        ]
        outs = [out for out in outs for _ in range(copies)]
        return pl.pallas_call(
            body,
            grid=(steps,),
            out_shape=tuple(jax.ShapeDtypeStruct((half_rows, w), d) for w, d in outs),
            in_specs=row_spec + whole_spec,
            out_specs=tuple(pl.BlockSpec((block_rows_here, w), lambda b: (b, 0)) for w, _ in outs),
            compiler_params=pltpu.CompilerParams(vmem_limit_bytes=38 * 2**20),
            cost_estimate=pl.CostEstimate(
                flops=flops, bytes_accessed=flops // 200, transcendentals=0
            ),
        )(*ins, *[v for v, _, _ in whole])

    def both_halves(refs, at=slice(None)):
        return jnp.concatenate([refs[0][:, at], refs[1][:, at]])

    def put(refs, v, at=slice(None)):
        refs[0][:, at] = v[: v.shape[0] // 2]
        refs[1][:, at] = v[v.shape[0] // 2 :]

    nt = (((1,), (1,)), ((), ()))
    gate_matrix, up_matrix, down_matrix = w_gate[0], w_up[0], w_down[0]
    lanes = lax.broadcasted_iota(jnp.int32, (1, info_width), 1)
    lane_mask = (lanes == mine).astype(f32)
    mask_spec = (lane_mask, (1, info_width), (0, 0))
    unit = 2 * 2 * half_rows * model_width * hidden_width

    t0 = jnp.concatenate([tokens[:, : t_cuts[1]], info], axis=1)
    t1 = tokens[:, t_cuts[1] :]
    c0, c1, c2 = (cotangent[:, c_cuts[n] : c_cuts[n + 1]] for n in range(3))
    t0_hops, t1_hops, c0_hops, c1_hops = [t0], [t1], [c0], [c1]

    def hop(hops):
        hops.append(send("z", hops[-1]))

    def near(way, hops, g):
        return with_other(way, jnp.stack([hops[2 * g], hops[2 * g + 1]]))

    hop(t0_hops)
    hop(t1_hops)
    c2_hops = [with_other("y", with_other("x", c2[None]))]
    t0_near = [near("y", t0_hops, 0)]
    t1_near = [near("x", t1_hops, 0)]
    hop(t0_hops)
    hop(t1_hops)
    t0_far = [send("x", t0_near[0])]
    t1_far = [send("y", t1_near[0])]
    hop(t0_hops)
    hop(t1_hops)
    t1_near.append(near("x", t1_hops, 1))
    t0_near.append(near("y", t0_hops, 1))
    hop(c0_hops)
    hop(c1_hops)
    t0_far.append(send("x", t0_near[1]))
    t1_far.append(send("y", t1_near[1]))
    hop(c0_hops)
    hop(c1_hops)
    hop(c0_hops)
    hop(c1_hops)
    hop(c2_hops)
    ready, _, _ = lax.optimization_barrier((c2_hops[1], c0_hops[3], c1_hops[3]))
    c2_hops[1] = ready
    c1_own, c0_own = jnp.stack(c1_hops), jnp.stack(c0_hops)
    c1_other, c0_other = send("x", c1_own), send("y", c0_own)
    hop(c2_hops)
    t0_blocks = [t0_near[0], t0_far[0], t0_near[1], t0_far[1]]
    t1_blocks = [t1_near[0], t1_far[0], t1_near[1], t1_far[1]]
    got_info = jnp.stack(
        [t0_blocks[where[0][k][0]][where[0][k][1], :, t_cuts[1] :] for k in order]
    )
    slots = jnp.arange(most_rows, dtype=f32)

    def places_of(index):
        at = lax.broadcasted_iota(jnp.int32, got_info.shape, 2) == device_count + index
        ranks = jnp.sum(jnp.where(at, got_info, jnp.zeros((), bf16)).astype(f32), axis=-1)
        return (ranks[:, None, :] == slots[:, None]).astype(bf16)

    place_both = jnp.concatenate([places_of(mine), places_of(other)], axis=1)
    rows = [
        half
        for n, blocks in enumerate((t0_blocks, t1_blocks))
        for half in compact(place_both, blocks, where[n])
    ]

    def forward(*refs):
        (part0, part1), (gates_at, wg, wu), outs = refs[:2], refs[2:5], refs[5:]
        sent = part0[:, t_cuts[1] :].astype(f32)
        row_gate = jnp.sum(sent * gates_at[...], axis=1, keepdims=True)
        parts = (part0[:, : t_cuts[1]], part1[...])
        pre_gate, pre_up = 0.0, 0.0
        for n in range(2):
            rows_at = slice(t_cuts[n], t_cuts[n + 1])
            pre_gate += jnp.dot(parts[n], wg[rows_at], preferred_element_type=f32)
            pre_up += jnp.dot(parts[n], wu[rows_at], preferred_element_type=f32)
        sigmoid_gate = 1.0 / (1.0 + jnp.exp(-pre_gate))
        silu_gate = pre_gate * sigmoid_gate
        hidden = silu_gate * pre_up
        outs[0][...] = hidden
        slope = pre_up * sigmoid_gate * (1.0 + pre_gate * (1.0 - sigmoid_gate))
        outs[1][...] = row_gate * slope
        outs[2][...] = row_gate * silu_gate
        outs[3][...] = (row_gate * hidden).astype(bf16)

    square = (model_width, hidden_width)
    def forward_half(part0, part1, flops):
        return row_call(
            forward,
            [part0, part1],
            [mask_spec, (gate_matrix, square, (0, 0)), (up_matrix, square, (0, 0))],
            [(hidden_width, f32)] * 3 + [(hidden_width, bf16)],
            flops,
            2,
            1,
        )

    forward_own = forward_half(rows[0], rows[2], 2 * unit)
    c0_own, c1_own, first_kept = lax.optimization_barrier((c0_own, c1_own, forward_own[0]))
    c0_near = jnp.concatenate([c0_own, c0_other])
    c1_near = jnp.concatenate([c1_own, c1_other])
    c0_far = send("x", c0_near)
    c1_far = send("y", c1_near)
    hop(c2_hops)
    given_in, _ = lax.optimization_barrier((rows[1], c0_near))
    forward_out = [[first_kept, *forward_own[1:]], forward_half(given_in, rows[3], 2 * unit)]
    kept = [forward_out[h][n] for n in range(3) for h in range(2)]
    weighted = [forward_out[h][3] for h in range(2)]
    place_tied, kept[0], kept[1] = lax.optimization_barrier((place_both, kept[0], kept[1]))
    c1_rows = compact(place_tied, [c1_near, c1_far], where[4])
    c0_rows = compact(place_tied, [c0_near, c0_far], where[3])

    def early(*refs):
        total = 0.0
        for n in range(2):
            total += lax.dot_general(
                both_halves(refs[2 * n : 2 * n + 2]),
                refs[4][:, c_cuts[n] : c_cuts[n + 1]],
                nt,
                preferred_element_type=f32,
            )
        put(refs[5:], total)

    early_back = row_call(
        early,
        [*c0_rows, *c1_rows],
        [(down_matrix, (hidden_width, c_cuts[2]), (0, 0))],
        [(hidden_width, f32)],
        1024,
    )
    place_tied, early_first = lax.optimization_barrier((place_both, early_back[0]))
    early_back = [early_first, early_back[1]]
    c2_rows = compact(place_tied, c2_hops, where[2])
    cot_rows = [*c0_rows, *c1_rows, *c2_rows]

    def row_grad(pgg, pug, wg, wu):
        return lax.dot_general(pgg, wg, nt, preferred_element_type=f32) + lax.dot_general(
            pug, wu, nt, preferred_element_type=f32
        )

    def backward(*refs):
        half, first, gated, slope, silu, gates_at, wd, wg, wu = refs[:9]
        pgg, pug, grad0, grad1, grad2 = refs[9:]
        back = first[...] + lax.dot_general(
            half[...], wd[...], nt, preferred_element_type=f32
        )
        gate_grad = jnp.sum(gated[...] * back, axis=1, keepdims=True)
        gate_side = (back * slope[...]).astype(bf16)
        up_side = (back * silu[...]).astype(bf16)
        pgg[...] = gate_side
        pug[...] = up_side
        for n, out in ((2, grad2), (0, grad0), (1, grad1)):
            at = slice(cuts[n], cuts[n + 1])
            grad = row_grad(gate_side, up_side, wg[at], wu[at])
            out[:, : cuts[n + 1] - cuts[n]] = grad.astype(bf16)
        grad0[:, cuts[1] :] = (gate_grad * gates_at[...]).astype(bf16)

    def backward_half(h, half):
        return row_call(
            backward,
            [half, early_back[h], kept[h], kept[2 + h], kept[4 + h]],
            [
                mask_spec,
                (down_matrix, (hidden_width, c_cuts[3] - c_cuts[2]), (0, 1)),
                (gate_matrix, square, (0, 0)),
                (up_matrix, square, (0, 0)),
            ],
            [(hidden_width, bf16)] * 2
            + [(info_width + cuts[1], bf16), (cuts[2] - cuts[1], bf16), (cuts[3] - cuts[2], bf16)],
            1024,
            2,
            1,
        )

    given_out = backward_half(1, c2_rows[1])
    own_in, tied = lax.optimization_barrier((c2_rows[0], given_out[0]))
    own_out = backward_half(0, own_in)
    sides = [own_out[0], tied, own_out[1], given_out[1]]
    grad_first, grad_second, grad_last = ((own_out[n], given_out[n]) for n in (2, 3, 4))

    place_grid = place_both.reshape(2, 2, 2, 2, 2 * most_rows, tok_local)

    def pair_rows(halves):
        width = halves[0].shape[-1]
        own = halves[0].reshape(source_count, most_rows, width)
        given = swap_core(halves[1]).reshape(source_count, most_rows, width)
        return jnp.concatenate([own, given], axis=1).reshape(2, 2, 2, 2, 2 * most_rows, width)

    def spread(places, v):
        return jnp.einsum("...ct,...cd->...td", places, v, preferred_element_type=f32)

    def add(own, arrived):
        return (own.astype(f32) + arrived.astype(f32)).astype(bf16)

    links["x"].clear()
    links["y"].clear()
    links["z"].clear()
    depth.update(x=3, y=3, z=3)
    v2 = pair_rows(grad_last)
    v0 = pair_rows(grad_first)
    v1 = pair_rows(grad_second)

    def spread_last(r):
        return spread(place_grid[r // 2, :, :, r % 2], v2[r // 2, :, :, r % 2])

    first_last = spread_last(3).astype(bf16)
    far0 = [spread(place_grid[g, 1], v0[g, 1]).astype(bf16) for g in range(2)]
    far1 = [spread(place_grid[g, :, 1], v1[g, :, 1]).astype(bf16) for g in range(2)]
    first_last, far0, far1 = lax.optimization_barrier((first_last, far0, far1))
    moving2 = send("d", first_last)
    sent0, sent1, half0, half1, near0, near1 = ([None, None] for _ in range(6))
    sent0[1] = send("x", far0[1])
    sent1[1] = send("y", far1[1])
    sent0[0] = send("x", far0[0])
    sent1[0] = send("y", far1[0])
    gate_tied, _, _, _ = lax.optimization_barrier((sides[:2], far0, far1, first_last))
    moving2 = add(spread_last(2), moving2)
    up_tied, moving2 = lax.optimization_barrier((sides[2:], moving2))
    moving2 = send("d", moving2)
    half1[1] = add(spread(place_grid[1, :, 0], v1[1, :, 0]), sent1[1])
    half0[1] = add(spread(place_grid[1, 0], v0[1, 0]), sent0[1])
    moving2 = add(spread_last(1), moving2)
    half1[1], half0[1], moving2 = lax.optimization_barrier((half1[1], half0[1], moving2))
    moving2 = send("d", moving2)
    near1[1] = send("x", half1[1][1])
    near0[1] = send("y", half0[1][1])
    sum0_high = add(half0[1][0], near0[1])
    sum1_high = add(half1[1][0], near1[1])
    weighted_tied, grid_tied, _, _ = lax.optimization_barrier(
        (weighted, place_grid, sum0_high, sum1_high)
    )
    moving0 = send("d", sum0_high[1])
    moving1 = send("d", sum1_high[1])
    half1[0] = add(spread(grid_tied[0, :, 0], v1[0, :, 0]), sent1[0])
    half0[0] = add(spread(grid_tied[0, 0], v0[0, 0]), sent0[0])
    near1[0] = send("x", half1[0][1])
    near0[0] = send("y", half0[0][1])
    pair = add(spread_last(0), moving2)
    pair = add(pair[:, 0], send("y", pair[:, 1]))
    sum_last = add(pair[0], send("x", pair[1]))
    moving0 = send("d", add(sum0_high[0], moving0))
    moving1 = send("d", add(sum1_high[0], moving1))
    sum0_low = add(half0[0][0], near0[0])
    sum1_low = add(half1[0][0], near1[0])
    moving0 = send("d", add(sum0_low[1], moving0))
    moving1 = send("d", add(sum1_low[1], moving1))
    sum_first = add(sum0_low[0], moving0)
    sum_second = add(sum1_low[0], moving1)
    gate_back = sum_first[:, cuts[1] : cuts[1] + device_count].astype(f32)
    input_grad = jnp.concatenate([sum_first[:, : cuts[1]], sum_second, sum_last], axis=1)
    gate_grad_out = jnp.sum(jnp.where(hit, gate_back[:, None, :], 0.0), axis=2).astype(bf16)

    tile = 256
    tn = (((0,), (0,)), ((), ()))

    def tn_dot(a, b):
        return lax.dot_general(a, b, tn, preferred_element_type=f32)

    def weight_call(body, halves, cuts, wide, out_spec, out_shape):
        firsts = [cut // tile for cut in cuts]
        count = len(halves)

        def run(*refs):
            step = pl.program_id(0)
            for n in range(count // 2):

                @pl.when((step >= firsts[n]) & (step < firsts[n + 1]))
                def _(n=n):
                    tiles = (refs[2 * n][...], refs[2 * n + 1][...])
                    refs[-1][...] = body(tiles, refs[count : count + 2]).astype(bf16)

        def tile_spec(n):
            low, top = firsts[n], firsts[n + 1] - firsts[n] - 1
            return pl.BlockSpec((half_rows, tile), lambda b: (0, jnp.clip(b - low, 0, top)))

        half_spec = pl.BlockSpec(
            (half_rows, hidden_width), lambda b: (0, 0), pipeline_mode=pl.Buffered(1)
        )
        return pl.pallas_call(
            run,
            grid=(firsts[-1],),
            out_shape=jax.ShapeDtypeStruct(out_shape, bf16),
            in_specs=[tile_spec(n // 2) for n in range(count)] + [half_spec] * 2,
            out_specs=out_spec,
            compiler_params=pltpu.CompilerParams(vmem_limit_bytes=16 * 2**20),
            cost_estimate=pl.CostEstimate(
                flops=unit, bytes_accessed=14 * 2**20, transcendentals=0
            ),
        )(*halves, *wide)

    def side_weights(sides):
        return weight_call(
            lambda x, side: tn_dot(x[0], side[0][...]) + tn_dot(x[1], side[1][...]),
            rows,
            t_cuts,
            sides,
            pl.BlockSpec((tile, hidden_width), lambda b: (b, 0)),
            (model_width, hidden_width),
        )

    w_gate_grad = side_weights(gate_tied)
    w_up_grad = side_weights(up_tied)
    w_down_grad = weight_call(
        lambda c, w: tn_dot(w[0][...], c[0]) + tn_dot(w[1][...], c[1]),
        cot_rows,
        c_cuts,
        weighted_tied,
        pl.BlockSpec((hidden_width, tile), lambda b: (0, b)),
        (hidden_width, model_width),
    )
    return (input_grad, gate_grad_out, w_gate_grad[None], w_up_grad[None], w_down_grad[None])


def on_device(tokens, cotangent, routes, gates, w_gate, w_up, w_down):
    dp_count = lax.axis_size("dp")
    expert_count = lax.axis_size("expert")
    gathered_bytes = dp_count * expert_count * tokens.size * 2
    if dp_count == 4 and expert_count == 8 and gathered_bytes <= gather_limit:
        return gather_path(tokens, cotangent, routes, gates, w_gate, w_up, w_down)
    return exchange_path(tokens, cotangent, routes, gates, w_gate, w_up, w_down)


def solution(mesh):
    in_specs = (
        P(("dp", "expert"), None),
        P(("dp", "expert"), None),
        P(("dp", "expert"), None),
        P(("dp", "expert"), None),
        P(("dp", "expert"), None, None),
        P(("dp", "expert"), None, None),
        P(("dp", "expert"), None, None),
    )
    out_specs = (
        P(("dp", "expert"), None),
        P(("dp", "expert"), None),
        P(("dp", "expert"), None, None),
        P(("dp", "expert"), None, None),
        P(("dp", "expert"), None, None),
    )
    return jax.shard_map(
        on_device, mesh=mesh, in_specs=in_specs, out_specs=out_specs, check_vma=False
    )
```

```python
import jax
import jax.numpy as jnp
from jax import lax
from jax.experimental import pallas as pl
from jax.experimental.pallas import tpu as pltpu
from jax.sharding import PartitionSpec as P

block_rows = 256
gather_limit = 32 * 2**20


def expert_parts(inputs, cotangent_rows, router_weight, gate_matrix, up_matrix, down_matrix):
    pre_gate = jnp.dot(inputs, gate_matrix, preferred_element_type=jnp.float32)
    pre_up = jnp.dot(inputs, up_matrix, preferred_element_type=jnp.float32)
    sigmoid_gate = jax.nn.sigmoid(pre_gate)
    silu_gate = pre_gate * sigmoid_gate
    hidden = (silu_gate * pre_up).astype(jnp.bfloat16)
    expert_out = jnp.dot(hidden, down_matrix, preferred_element_type=jnp.float32)
    gate_grad = jnp.sum(cotangent_rows.astype(jnp.float32) * expert_out, axis=1).astype(
        jnp.bfloat16
    )
    out_grad = (
        router_weight.astype(jnp.float32)[:, None] * cotangent_rows.astype(jnp.float32)
    ).astype(jnp.bfloat16)
    hidden_grad = lax.dot_general(
        out_grad, down_matrix, (((1,), (1,)), ((), ())), preferred_element_type=jnp.float32
    )
    pre_gate_grad = (
        hidden_grad * pre_up * sigmoid_gate * (1.0 + pre_gate * (1.0 - sigmoid_gate))
    ).astype(jnp.bfloat16)
    pre_up_grad = (hidden_grad * silu_gate).astype(jnp.bfloat16)
    row_grad = lax.dot_general(
        pre_gate_grad, gate_matrix, (((1,), (1,)), ((), ())), preferred_element_type=jnp.float32
    )
    row_grad = row_grad + lax.dot_general(
        pre_up_grad, up_matrix, (((1,), (1,)), ((), ())), preferred_element_type=jnp.float32
    )
    return (row_grad.astype(jnp.bfloat16), gate_grad, pre_gate_grad, pre_up_grad, hidden, out_grad)


def outer_terms(inputs, pre_gate_grad, pre_up_grad, hidden, out_grad):
    gate_term = lax.dot_general(
        inputs, pre_gate_grad, (((0,), (0,)), ((), ())), preferred_element_type=jnp.float32
    )
    up_term = lax.dot_general(
        inputs, pre_up_grad, (((0,), (0,)), ((), ())), preferred_element_type=jnp.float32
    )
    down_term = lax.dot_general(
        hidden, out_grad, (((0,), (0,)), ((), ())), preferred_element_type=jnp.float32
    )
    return (gate_term, up_term, down_term)


def exchange_path(tokens, cotangent, routes, gates, w_gate, w_up, w_down):
    dp_count = lax.axis_size("dp")
    expert_count = lax.axis_size("expert")
    device_count = dp_count * expert_count
    tok_local, model_width = tokens.shape
    top_count = routes.shape[1]
    row_count = tok_local * top_count
    most_rows = 7 * row_count // (4 * device_count)
    slot_total = device_count * most_rows
    zero_value = jnp.zeros((), jnp.bfloat16)
    flat_expert = routes.reshape(row_count)
    onehot = (flat_expert[:, None] == jnp.arange(device_count, dtype=jnp.int32)[None, :]).astype(
        jnp.int32
    )
    rank_in_expert = jnp.sum(jnp.cumsum(onehot, axis=0) * onehot, axis=1) - 1
    slot_index = flat_expert * most_rows + rank_in_expert
    row_of_slot = (
        jnp.full((slot_total,), row_count, jnp.int32)
        .at[slot_index]
        .set(jnp.arange(row_count, dtype=jnp.int32))
    )
    slot_live = row_of_slot < row_count
    safe_row = jnp.minimum(row_of_slot, row_count - 1)
    token_of_slot = safe_row // top_count
    send_tokens = jnp.where(slot_live[:, None], tokens[token_of_slot], zero_value).reshape(
        device_count, most_rows, model_width
    )
    send_cotangent = jnp.where(slot_live[:, None], cotangent[token_of_slot], zero_value).reshape(
        device_count, most_rows, model_width
    )
    send_weight = jnp.where(slot_live, gates.reshape(row_count)[safe_row], zero_value).reshape(
        device_count, most_rows
    )
    arrived = (
        lax.all_to_all(send_tokens, ("dp", "expert"), split_axis=0, concat_axis=0, tiled=True),
        lax.all_to_all(send_cotangent, ("dp", "expert"), split_axis=0, concat_axis=0, tiled=True),
        lax.all_to_all(send_weight, ("dp", "expert"), split_axis=0, concat_axis=0, tiled=True),
    )
    got_tokens = arrived[0].reshape(slot_total, model_width)
    got_cotangent = arrived[1].reshape(slot_total, model_width)
    got_weight = arrived[2].reshape(slot_total)
    gate_matrix = w_gate[0]
    up_matrix = w_up[0]
    down_matrix = w_down[0]
    hidden_width = gate_matrix.shape[1]
    is_used = got_weight != zero_value
    used_count = jnp.sum(is_used.astype(jnp.int32))
    padded_total = -(-slot_total // block_rows) * block_rows
    compact_pos = jnp.cumsum(is_used.astype(jnp.int32)) - 1
    slot_of_compact = (
        jnp.full((padded_total,), slot_total, jnp.int32)
        .at[jnp.where(is_used, compact_pos, padded_total)]
        .set(jnp.arange(slot_total, dtype=jnp.int32), mode="drop")
    )
    block_count = (used_count + block_rows - 1) // block_rows

    def block_step(block_index, carried):
        gate_acc, up_acc, down_acc, grad_slots, gate_slots = carried
        picked = lax.dynamic_slice_in_dim(slot_of_compact, block_index * block_rows, block_rows)
        is_live = picked < slot_total
        safe_pick = jnp.minimum(picked, slot_total - 1)
        block_tokens = jnp.where(is_live[:, None], got_tokens[safe_pick], zero_value)
        block_cotangent = jnp.where(is_live[:, None], got_cotangent[safe_pick], zero_value)
        block_weight = jnp.where(is_live, got_weight[safe_pick], zero_value)
        row_grad, gate_grad, pre_gate_grad, pre_up_grad, hidden, out_grad = expert_parts(
            block_tokens, block_cotangent, block_weight, gate_matrix, up_matrix, down_matrix
        )
        gate_term, up_term, down_term = outer_terms(
            block_tokens, pre_gate_grad, pre_up_grad, hidden, out_grad
        )
        target = jnp.where(is_live, picked, slot_total)
        grad_slots = grad_slots.at[target].set(row_grad, mode="drop")
        gate_slots = gate_slots.at[target].set(gate_grad, mode="drop")
        return (
            gate_acc + gate_term,
            up_acc + up_term,
            down_acc + down_term,
            grad_slots,
            gate_slots,
        )

    initial = (
        jnp.zeros((model_width, hidden_width), jnp.float32),
        jnp.zeros((model_width, hidden_width), jnp.float32),
        jnp.zeros((hidden_width, model_width), jnp.float32),
        jnp.zeros((slot_total, model_width), jnp.bfloat16),
        jnp.zeros((slot_total,), jnp.bfloat16),
    )
    finished = lax.fori_loop(0, block_count, block_step, initial)
    gate_acc, up_acc, down_acc, grad_slots, gate_slots = finished
    grad_out = grad_slots.reshape(device_count, most_rows, model_width)
    gate_out = gate_slots.reshape(device_count, most_rows)
    returned = (
        lax.all_to_all(grad_out, ("dp", "expert"), split_axis=0, concat_axis=0, tiled=True),
        lax.all_to_all(gate_out, ("dp", "expert"), split_axis=0, concat_axis=0, tiled=True),
    )
    back_grad = returned[0].reshape(slot_total, model_width)
    back_gate = returned[1].reshape(slot_total)
    row_grads = back_grad[slot_index].reshape(tok_local, top_count, model_width)
    input_grad = jnp.sum(row_grads, axis=1, dtype=jnp.float32).astype(jnp.bfloat16)
    gate_grad = back_gate[slot_index].reshape(tok_local, top_count)
    return (
        input_grad,
        gate_grad,
        gate_acc.astype(jnp.bfloat16)[None],
        up_acc.astype(jnp.bfloat16)[None],
        down_acc.astype(jnp.bfloat16)[None],
    )


def gather_path(tokens, cotangent, routes, gates, w_gate, w_up, w_down):
    dp_count = lax.axis_size("dp")
    expert_count = lax.axis_size("expert")
    device_count = dp_count * expert_count
    tok_local, model_width = tokens.shape
    hidden_width = w_gate.shape[2]
    top_count = routes.shape[1]
    most_rows = 7 * tok_local * top_count // (4 * device_count)
    source_count = 16
    half_rows = source_count * most_rows
    bf16, f32 = jnp.bfloat16, jnp.float32

    def swap_core(v):
        return lax.ppermute(v, "dp", [(p, p ^ 1) for p in range(dp_count)])

    def swap_x(v):
        return lax.ppermute(v, "dp", [(p, p ^ 2) for p in range(dp_count)])

    def swap_y(v):
        return lax.ppermute(v, "expert", [(q, q ^ 1) for q in range(expert_count)])

    def ring_up(v):
        return lax.ppermute(
            v, "expert", [(q, (q + 2) % expert_count) for q in range(expert_count)]
        )

    def ring_down(v):
        return lax.ppermute(
            v, "expert", [(q, (q - 2) % expert_count) for q in range(expert_count)]
        )

    dp_index = lax.axis_index("dp")
    expert_index = lax.axis_index("expert")
    mine = dp_index * expert_count + expert_index
    other = (dp_index ^ 1) * expert_count + expert_index

    hit = routes[:, :, None] == jnp.arange(device_count, dtype=jnp.int32)[None, None, :]
    gate_dense = jnp.sum(jnp.where(hit, gates[:, :, None].astype(f32), 0.0), axis=1)
    named = jnp.sum(hit.astype(f32), axis=1)
    token_iota = jnp.arange(tok_local)
    before = (token_iota[None, :] < token_iota[:, None]).astype(bf16)
    rank = jnp.dot(before, named.astype(bf16), preferred_element_type=f32)
    rank = jnp.where(named > 0.0, rank, -1.0)
    info_width = -(-2 * device_count // 128) * 128
    info = jnp.concatenate(
        [
            gate_dense.astype(bf16),
            rank.astype(bf16),
            jnp.zeros((tok_local, info_width - 2 * device_count), bf16),
        ],
        axis=1,
    )

    t_cuts = (0, model_width // 2, model_width)
    c_cuts = (0, model_width // 4, model_width // 2, model_width)
    cuts = (0, 3 * model_width // 8, 3 * model_width // 4, model_width)

    links = {"x": [], "y": [], "z": []}
    depth = {"x": 2, "y": 2, "z": 3}
    ways = {"x": swap_x, "y": swap_y, "z": ring_up, "d": ring_down}

    def send(way, v):
        link = "z" if way == "d" else way
        queue = links[link]
        if len(queue) >= depth[link]:
            v, _ = lax.optimization_barrier((v, queue[-depth[link]]))
        queue.append(ways[way](v))
        return queue[-1]

    order = [(g, i, j, s) for g in range(2) for i in range(2) for j in range(2) for s in range(2)]
    where = [{}, {}, {}, {}, {}]
    for g, i, j, s in order:
        where[0][g, i, j, s] = (2 * g + i, 2 * j + s)
        where[1][g, i, j, s] = (2 * g + j, 2 * i + s)
        where[2][g, i, j, s] = (2 * g + s, 2 * j + i)
        where[3][g, i, j, s] = (i, 4 * j + 2 * g + s)
        where[4][g, i, j, s] = (j, 4 * i + 2 * g + s)

    def with_other(way, v):
        return jnp.concatenate([v, send(way, v)])

    def compact(place_both, blocks, where):
        width = blocks[0].shape[-1]

        def body(places, *refs):
            ins, keep, give = refs[: len(blocks)], refs[-2], refs[-1]
            for n, source in enumerate(order):
                block, at = where[source]
                picked = jnp.dot(places[n], ins[block][at], preferred_element_type=f32)
                keep[n] = picked[:most_rows].astype(bf16)
                give[n] = picked[most_rows:].astype(bf16)

        shape = jax.ShapeDtypeStruct((source_count, most_rows, width), bf16)
        keep, give = pl.pallas_call(
            body,
            out_shape=(shape, shape),
            in_specs=[pl.BlockSpec(memory_space=pltpu.VMEM)] * (1 + len(blocks)),
            out_specs=(pl.BlockSpec(memory_space=pltpu.VMEM),) * 2,
            compiler_params=pltpu.CompilerParams(vmem_limit_bytes=24 * 2**20),
            cost_estimate=pl.CostEstimate(
                flops=2 * source_count * 2 * most_rows * tok_local * width, bytes_accessed=12 * 2**20, transcendentals=0,
            ),
        )(place_both, *blocks)
        return keep.reshape(half_rows, width), swap_core(give).reshape(half_rows, width)

    def row_call(body, ins, whole, outs, flops, steps=4, copies=2):
        block_rows_here = half_rows // steps
        row_spec = [pl.BlockSpec((block_rows_here, v.shape[1]), lambda b: (b, 0)) for v in ins]
        whole_spec = [
            pl.BlockSpec(shape, lambda b, place=place: place, pipeline_mode=pl.Buffered(1))
            for _, shape, place in whole
        ]
        outs = [out for out in outs for _ in range(copies)]
        return pl.pallas_call(
            body,
            grid=(steps,),
            out_shape=tuple(jax.ShapeDtypeStruct((half_rows, w), d) for w, d in outs),
            in_specs=row_spec + whole_spec,
            out_specs=tuple(pl.BlockSpec((block_rows_here, w), lambda b: (b, 0)) for w, _ in outs),
            compiler_params=pltpu.CompilerParams(vmem_limit_bytes=38 * 2**20),
            cost_estimate=pl.CostEstimate(
                flops=flops, bytes_accessed=flops // 200, transcendentals=0
            ),
        )(*ins, *[v for v, _, _ in whole])

    def both_halves(refs, at=slice(None)):
        return jnp.concatenate([refs[0][:, at], refs[1][:, at]])

    def put(refs, v, at=slice(None)):
        refs[0][:, at] = v[: v.shape[0] // 2]
        refs[1][:, at] = v[v.shape[0] // 2 :]

    nt = (((1,), (1,)), ((), ()))
    gate_matrix, up_matrix, down_matrix = w_gate[0], w_up[0], w_down[0]
    lanes = lax.broadcasted_iota(jnp.int32, (1, info_width), 1)
    lane_mask = (lanes == mine).astype(f32)
    mask_spec = (lane_mask, (1, info_width), (0, 0))
    unit = 2 * 2 * half_rows * model_width * hidden_width

    t0 = jnp.concatenate([tokens[:, : t_cuts[1]], info], axis=1)
    t1 = tokens[:, t_cuts[1] :]
    c0, c1, c2 = (cotangent[:, c_cuts[n] : c_cuts[n + 1]] for n in range(3))
    t0_hops, t1_hops, c0_hops, c1_hops = [t0], [t1], [c0], [c1]

    def hop(hops):
        hops.append(send("z", hops[-1]))

    def near(way, hops, g):
        return with_other(way, jnp.stack([hops[2 * g], hops[2 * g + 1]]))

    hop(t0_hops)
    hop(t1_hops)
    c2_hops = [with_other("y", with_other("x", c2[None]))]
    t0_near = [near("y", t0_hops, 0)]
    t1_near = [near("x", t1_hops, 0)]
    hop(t0_hops)
    hop(t1_hops)
    t0_far = [send("x", t0_near[0])]
    t1_far = [send("y", t1_near[0])]
    hop(t0_hops)
    hop(t1_hops)
    t1_near.append(near("x", t1_hops, 1))
    t0_near.append(near("y", t0_hops, 1))
    hop(c0_hops)
    hop(c1_hops)
    t0_far.append(send("x", t0_near[1]))
    t1_far.append(send("y", t1_near[1]))
    hop(c0_hops)
    hop(c1_hops)
    hop(c0_hops)
    hop(c1_hops)
    hop(c2_hops)
    ready, _, _ = lax.optimization_barrier((c2_hops[1], c0_hops[3], c1_hops[3]))
    c2_hops[1] = ready
    c1_own, c0_own = jnp.stack(c1_hops), jnp.stack(c0_hops)
    c1_other, c0_other = send("x", c1_own), send("y", c0_own)
    hop(c2_hops)
    t0_blocks = [t0_near[0], t0_far[0], t0_near[1], t0_far[1]]
    t1_blocks = [t1_near[0], t1_far[0], t1_near[1], t1_far[1]]
    got_info = jnp.stack(
        [t0_blocks[where[0][k][0]][where[0][k][1], :, t_cuts[1] :] for k in order]
    )
    slots = jnp.arange(most_rows, dtype=f32)

    def places_of(index):
        at = lax.broadcasted_iota(jnp.int32, got_info.shape, 2) == device_count + index
        ranks = jnp.sum(jnp.where(at, got_info, jnp.zeros((), bf16)).astype(f32), axis=-1)
        return (ranks[:, None, :] == slots[:, None]).astype(bf16)

    place_both = jnp.concatenate([places_of(mine), places_of(other)], axis=1)
    rows = [
        half
        for n, blocks in enumerate((t0_blocks, t1_blocks))
        for half in compact(place_both, blocks, where[n])
    ]

    def forward(*refs):
        (part0, part1), (gates_at, wg, wu), outs = refs[:2], refs[2:5], refs[5:]
        sent = part0[:, t_cuts[1] :].astype(f32)
        row_gate = jnp.sum(sent * gates_at[...], axis=1, keepdims=True)
        parts = (part0[:, : t_cuts[1]], part1[...])
        pre_gate, pre_up = 0.0, 0.0
        for n in range(2):
            rows_at = slice(t_cuts[n], t_cuts[n + 1])
            pre_gate += jnp.dot(parts[n], wg[rows_at], preferred_element_type=f32)
            pre_up += jnp.dot(parts[n], wu[rows_at], preferred_element_type=f32)
        sigmoid_gate = 1.0 / (1.0 + jnp.exp(-pre_gate))
        silu_gate = pre_gate * sigmoid_gate
        hidden = silu_gate * pre_up
        outs[0][...] = hidden
        slope = pre_up * sigmoid_gate * (1.0 + pre_gate * (1.0 - sigmoid_gate))
        outs[1][...] = row_gate * slope
        outs[2][...] = row_gate * silu_gate
        outs[3][...] = (row_gate * hidden).astype(bf16)

    square = (model_width, hidden_width)
    def forward_half(part0, part1, flops):
        return row_call(
            forward,
            [part0, part1],
            [mask_spec, (gate_matrix, square, (0, 0)), (up_matrix, square, (0, 0))],
            [(hidden_width, f32)] * 3 + [(hidden_width, bf16)],
            flops,
            2,
            1,
        )

    forward_own = forward_half(rows[0], rows[2], 2 * unit)
    c0_own, c1_own, first_kept = lax.optimization_barrier((c0_own, c1_own, forward_own[0]))
    c0_near = jnp.concatenate([c0_own, c0_other])
    c1_near = jnp.concatenate([c1_own, c1_other])
    c0_far = send("x", c0_near)
    c1_far = send("y", c1_near)
    hop(c2_hops)
    given_in, _ = lax.optimization_barrier((rows[1], c0_near))
    forward_out = [[first_kept, *forward_own[1:]], forward_half(given_in, rows[3], 2 * unit)]
    kept = [forward_out[h][n] for n in range(3) for h in range(2)]
    weighted = [forward_out[h][3] for h in range(2)]
    place_tied, kept[0], kept[1] = lax.optimization_barrier((place_both, kept[0], kept[1]))
    c1_rows = compact(place_tied, [c1_near, c1_far], where[4])
    c0_rows = compact(place_tied, [c0_near, c0_far], where[3])

    def early(*refs):
        total = 0.0
        for n in range(2):
            total += lax.dot_general(
                both_halves(refs[2 * n : 2 * n + 2]),
                refs[4][:, c_cuts[n] : c_cuts[n + 1]],
                nt,
                preferred_element_type=f32,
            )
        put(refs[5:], total)

    early_back = row_call(
        early,
        [*c0_rows, *c1_rows],
        [(down_matrix, (hidden_width, c_cuts[2]), (0, 0))],
        [(hidden_width, f32)],
        1024,
    )
    place_tied, early_first = lax.optimization_barrier((place_both, early_back[0]))
    early_back = [early_first, early_back[1]]
    c2_rows = compact(place_tied, c2_hops, where[2])
    cot_rows = [*c0_rows, *c1_rows, *c2_rows]

    def row_grad(pgg, pug, wg, wu):
        return lax.dot_general(pgg, wg, nt, preferred_element_type=f32) + lax.dot_general(
            pug, wu, nt, preferred_element_type=f32
        )

    def backward(*refs):
        half, first, gated, slope, silu, gates_at, wd, wg, wu = refs[:9]
        pgg, pug, grad0, grad1, grad2 = refs[9:]
        back = first[...] + lax.dot_general(
            half[...], wd[...], nt, preferred_element_type=f32
        )
        gate_grad = jnp.sum(gated[...] * back, axis=1, keepdims=True)
        gate_side = (back * slope[...]).astype(bf16)
        up_side = (back * silu[...]).astype(bf16)
        pgg[...] = gate_side
        pug[...] = up_side
        for n, out in ((2, grad2), (0, grad0), (1, grad1)):
            at = slice(cuts[n], cuts[n + 1])
            grad = row_grad(gate_side, up_side, wg[at], wu[at])
            out[:, : cuts[n + 1] - cuts[n]] = grad.astype(bf16)
        grad0[:, cuts[1] :] = (gate_grad * gates_at[...]).astype(bf16)

    def backward_half(h, half):
        return row_call(
            backward,
            [half, early_back[h], kept[h], kept[2 + h], kept[4 + h]],
            [
                mask_spec,
                (down_matrix, (hidden_width, c_cuts[3] - c_cuts[2]), (0, 1)),
                (gate_matrix, square, (0, 0)),
                (up_matrix, square, (0, 0)),
            ],
            [(hidden_width, bf16)] * 2
            + [(info_width + cuts[1], bf16), (cuts[2] - cuts[1], bf16), (cuts[3] - cuts[2], bf16)],
            1024,
            2,
            1,
        )

    given_out = backward_half(1, c2_rows[1])
    own_in, tied = lax.optimization_barrier((c2_rows[0], given_out[0]))
    own_out = backward_half(0, own_in)
    sides = [own_out[0], tied, own_out[1], given_out[1]]
    grad_first, grad_second, grad_last = ((own_out[n], given_out[n]) for n in (2, 3, 4))

    place_grid = place_both.reshape(2, 2, 2, 2, 2 * most_rows, tok_local)

    def pair_rows(halves):
        width = halves[0].shape[-1]
        own = halves[0].reshape(source_count, most_rows, width)
        given = swap_core(halves[1]).reshape(source_count, most_rows, width)
        return jnp.concatenate([own, given], axis=1).reshape(2, 2, 2, 2, 2 * most_rows, width)

    def spread(places, v):
        return jnp.einsum("...ct,...cd->...td", places, v, preferred_element_type=f32)

    def add(own, arrived):
        return (own.astype(f32) + arrived.astype(f32)).astype(bf16)

    links["x"].clear()
    links["y"].clear()
    links["z"].clear()
    depth.update(x=3, y=3, z=3)
    v2 = pair_rows(grad_last)
    v0 = pair_rows(grad_first)
    v1 = pair_rows(grad_second)

    def spread_last(r):
        return spread(place_grid[r // 2, :, :, r % 2], v2[r // 2, :, :, r % 2])

    first_last = spread_last(3).astype(bf16)
    far0 = [spread(place_grid[g, 1], v0[g, 1]).astype(bf16) for g in range(2)]
    far1 = [spread(place_grid[g, :, 1], v1[g, :, 1]).astype(bf16) for g in range(2)]
    first_last, far0, far1 = lax.optimization_barrier((first_last, far0, far1))
    moving2 = send("d", first_last)
    sent0, sent1, half0, half1, near0, near1 = ([None, None] for _ in range(6))
    sent0[1] = send("x", far0[1])
    sent1[1] = send("y", far1[1])
    sent0[0] = send("x", far0[0])
    sent1[0] = send("y", far1[0])
    sides_tied, _, _, _ = lax.optimization_barrier((sides, far0, far1, first_last))
    gate_tied, up_tied = sides_tied[:2], sides_tied[2:]
    moving2 = add(spread_last(2), moving2)
    moving2 = send("d", moving2)
    half1[1] = add(spread(place_grid[1, :, 0], v1[1, :, 0]), sent1[1])
    half0[1] = add(spread(place_grid[1, 0], v0[1, 0]), sent0[1])
    moving2 = add(spread_last(1), moving2)
    weighted_tied, half1[1], half0[1], moving2 = lax.optimization_barrier(
        (weighted, half1[1], half0[1], moving2)
    )
    moving2 = send("d", moving2)
    near1[1] = send("x", half1[1][1])
    near0[1] = send("y", half0[1][1])
    sum0_high = add(half0[1][0], near0[1])
    sum1_high = add(half1[1][0], near1[1])
    grid_tied, _, _ = lax.optimization_barrier((place_grid, sum0_high, sum1_high))
    moving0 = send("d", sum0_high[1])
    moving1 = send("d", sum1_high[1])
    half1[0] = add(spread(grid_tied[0, :, 0], v1[0, :, 0]), sent1[0])
    half0[0] = add(spread(grid_tied[0, 0], v0[0, 0]), sent0[0])
    near1[0] = send("x", half1[0][1])
    near0[0] = send("y", half0[0][1])
    pair = add(spread_last(0), moving2)
    pair = add(pair[:, 0], send("y", pair[:, 1]))
    sum_last = add(pair[0], send("x", pair[1]))
    moving0 = send("d", add(sum0_high[0], moving0))
    moving1 = send("d", add(sum1_high[0], moving1))
    sum0_low = add(half0[0][0], near0[0])
    sum1_low = add(half1[0][0], near1[0])
    moving0 = send("d", add(sum0_low[1], moving0))
    moving1 = send("d", add(sum1_low[1], moving1))
    sum_first = add(sum0_low[0], moving0)
    sum_second = add(sum1_low[0], moving1)
    gate_back = sum_first[:, cuts[1] : cuts[1] + device_count].astype(f32)
    input_grad = jnp.concatenate([sum_first[:, : cuts[1]], sum_second, sum_last], axis=1)
    gate_grad_out = jnp.sum(jnp.where(hit, gate_back[:, None, :], 0.0), axis=2).astype(bf16)

    tile = 256
    tn = (((0,), (0,)), ((), ()))

    def tn_dot(a, b):
        return lax.dot_general(a, b, tn, preferred_element_type=f32)

    def weight_call(body, halves, cuts, wide, out_spec, out_shape):
        firsts = [cut // tile for cut in cuts]
        count = len(halves)

        def run(*refs):
            step = pl.program_id(0)
            for n in range(count // 2):

                @pl.when((step >= firsts[n]) & (step < firsts[n + 1]))
                def _(n=n):
                    tiles = (refs[2 * n][...], refs[2 * n + 1][...])
                    refs[-1][...] = body(tiles, refs[count : count + 2]).astype(bf16)

        def tile_spec(n):
            low, top = firsts[n], firsts[n + 1] - firsts[n] - 1
            return pl.BlockSpec((half_rows, tile), lambda b: (0, jnp.clip(b - low, 0, top)))

        half_spec = pl.BlockSpec(
            (half_rows, hidden_width), lambda b: (0, 0), pipeline_mode=pl.Buffered(1)
        )
        return pl.pallas_call(
            run,
            grid=(firsts[-1],),
            out_shape=jax.ShapeDtypeStruct(out_shape, bf16),
            in_specs=[tile_spec(n // 2) for n in range(count)] + [half_spec] * 2,
            out_specs=out_spec,
            compiler_params=pltpu.CompilerParams(vmem_limit_bytes=16 * 2**20),
            cost_estimate=pl.CostEstimate(
                flops=unit, bytes_accessed=14 * 2**20, transcendentals=0
            ),
        )(*halves, *wide)

    def side_weights(sides):
        return weight_call(
            lambda x, side: tn_dot(x[0], side[0][...]) + tn_dot(x[1], side[1][...]),
            rows,
            t_cuts,
            sides,
            pl.BlockSpec((tile, hidden_width), lambda b: (b, 0)),
            (model_width, hidden_width),
        )

    w_gate_grad = side_weights(gate_tied)
    w_up_grad = side_weights(up_tied)
    w_down_grad = weight_call(
        lambda c, w: tn_dot(w[0][...], c[0]) + tn_dot(w[1][...], c[1]),
        cot_rows,
        c_cuts,
        weighted_tied,
        pl.BlockSpec((hidden_width, tile), lambda b: (0, b)),
        (hidden_width, model_width),
    )
    return (input_grad, gate_grad_out, w_gate_grad[None], w_up_grad[None], w_down_grad[None])


def on_device(tokens, cotangent, routes, gates, w_gate, w_up, w_down):
    dp_count = lax.axis_size("dp")
    expert_count = lax.axis_size("expert")
    gathered_bytes = dp_count * expert_count * tokens.size * 2
    if dp_count == 4 and expert_count == 8 and gathered_bytes <= gather_limit:
        return gather_path(tokens, cotangent, routes, gates, w_gate, w_up, w_down)
    return exchange_path(tokens, cotangent, routes, gates, w_gate, w_up, w_down)


def solution(mesh):
    in_specs = (
        P(("dp", "expert"), None),
        P(("dp", "expert"), None),
        P(("dp", "expert"), None),
        P(("dp", "expert"), None),
        P(("dp", "expert"), None, None),
        P(("dp", "expert"), None, None),
        P(("dp", "expert"), None, None),
    )
    out_specs = (
        P(("dp", "expert"), None),
        P(("dp", "expert"), None),
        P(("dp", "expert"), None, None),
        P(("dp", "expert"), None, None),
        P(("dp", "expert"), None, None),
    )
    return jax.shard_map(
        on_device, mesh=mesh, in_specs=in_specs, out_specs=out_specs, check_vma=False
    )
```

```python
import jax
import jax.numpy as jnp
from jax import lax
from jax.experimental import pallas as pl
from jax.experimental.pallas import tpu as pltpu
from jax.sharding import PartitionSpec as P

block_rows = 256
gather_limit = 32 * 2**20


def expert_parts(inputs, cotangent_rows, router_weight, gate_matrix, up_matrix, down_matrix):
    pre_gate = jnp.dot(inputs, gate_matrix, preferred_element_type=jnp.float32)
    pre_up = jnp.dot(inputs, up_matrix, preferred_element_type=jnp.float32)
    sigmoid_gate = jax.nn.sigmoid(pre_gate)
    silu_gate = pre_gate * sigmoid_gate
    hidden = (silu_gate * pre_up).astype(jnp.bfloat16)
    expert_out = jnp.dot(hidden, down_matrix, preferred_element_type=jnp.float32)
    gate_grad = jnp.sum(cotangent_rows.astype(jnp.float32) * expert_out, axis=1).astype(
        jnp.bfloat16
    )
    out_grad = (
        router_weight.astype(jnp.float32)[:, None] * cotangent_rows.astype(jnp.float32)
    ).astype(jnp.bfloat16)
    hidden_grad = lax.dot_general(
        out_grad, down_matrix, (((1,), (1,)), ((), ())), preferred_element_type=jnp.float32
    )
    pre_gate_grad = (
        hidden_grad * pre_up * sigmoid_gate * (1.0 + pre_gate * (1.0 - sigmoid_gate))
    ).astype(jnp.bfloat16)
    pre_up_grad = (hidden_grad * silu_gate).astype(jnp.bfloat16)
    row_grad = lax.dot_general(
        pre_gate_grad, gate_matrix, (((1,), (1,)), ((), ())), preferred_element_type=jnp.float32
    )
    row_grad = row_grad + lax.dot_general(
        pre_up_grad, up_matrix, (((1,), (1,)), ((), ())), preferred_element_type=jnp.float32
    )
    return (row_grad.astype(jnp.bfloat16), gate_grad, pre_gate_grad, pre_up_grad, hidden, out_grad)


def outer_terms(inputs, pre_gate_grad, pre_up_grad, hidden, out_grad):
    gate_term = lax.dot_general(
        inputs, pre_gate_grad, (((0,), (0,)), ((), ())), preferred_element_type=jnp.float32
    )
    up_term = lax.dot_general(
        inputs, pre_up_grad, (((0,), (0,)), ((), ())), preferred_element_type=jnp.float32
    )
    down_term = lax.dot_general(
        hidden, out_grad, (((0,), (0,)), ((), ())), preferred_element_type=jnp.float32
    )
    return (gate_term, up_term, down_term)


def exchange_path(tokens, cotangent, routes, gates, w_gate, w_up, w_down):
    dp_count = lax.axis_size("dp")
    expert_count = lax.axis_size("expert")
    device_count = dp_count * expert_count
    tok_local, model_width = tokens.shape
    top_count = routes.shape[1]
    row_count = tok_local * top_count
    most_rows = 7 * row_count // (4 * device_count)
    slot_total = device_count * most_rows
    zero_value = jnp.zeros((), jnp.bfloat16)
    flat_expert = routes.reshape(row_count)
    onehot = (flat_expert[:, None] == jnp.arange(device_count, dtype=jnp.int32)[None, :]).astype(
        jnp.int32
    )
    rank_in_expert = jnp.sum(jnp.cumsum(onehot, axis=0) * onehot, axis=1) - 1
    slot_index = flat_expert * most_rows + rank_in_expert
    row_of_slot = (
        jnp.full((slot_total,), row_count, jnp.int32)
        .at[slot_index]
        .set(jnp.arange(row_count, dtype=jnp.int32))
    )
    slot_live = row_of_slot < row_count
    safe_row = jnp.minimum(row_of_slot, row_count - 1)
    token_of_slot = safe_row // top_count
    send_tokens = jnp.where(slot_live[:, None], tokens[token_of_slot], zero_value).reshape(
        device_count, most_rows, model_width
    )
    send_cotangent = jnp.where(slot_live[:, None], cotangent[token_of_slot], zero_value).reshape(
        device_count, most_rows, model_width
    )
    send_weight = jnp.where(slot_live, gates.reshape(row_count)[safe_row], zero_value).reshape(
        device_count, most_rows
    )
    arrived = (
        lax.all_to_all(send_tokens, ("dp", "expert"), split_axis=0, concat_axis=0, tiled=True),
        lax.all_to_all(send_cotangent, ("dp", "expert"), split_axis=0, concat_axis=0, tiled=True),
        lax.all_to_all(send_weight, ("dp", "expert"), split_axis=0, concat_axis=0, tiled=True),
    )
    got_tokens = arrived[0].reshape(slot_total, model_width)
    got_cotangent = arrived[1].reshape(slot_total, model_width)
    got_weight = arrived[2].reshape(slot_total)
    gate_matrix = w_gate[0]
    up_matrix = w_up[0]
    down_matrix = w_down[0]
    hidden_width = gate_matrix.shape[1]
    is_used = got_weight != zero_value
    used_count = jnp.sum(is_used.astype(jnp.int32))
    padded_total = -(-slot_total // block_rows) * block_rows
    compact_pos = jnp.cumsum(is_used.astype(jnp.int32)) - 1
    slot_of_compact = (
        jnp.full((padded_total,), slot_total, jnp.int32)
        .at[jnp.where(is_used, compact_pos, padded_total)]
        .set(jnp.arange(slot_total, dtype=jnp.int32), mode="drop")
    )
    block_count = (used_count + block_rows - 1) // block_rows

    def block_step(block_index, carried):
        gate_acc, up_acc, down_acc, grad_slots, gate_slots = carried
        picked = lax.dynamic_slice_in_dim(slot_of_compact, block_index * block_rows, block_rows)
        is_live = picked < slot_total
        safe_pick = jnp.minimum(picked, slot_total - 1)
        block_tokens = jnp.where(is_live[:, None], got_tokens[safe_pick], zero_value)
        block_cotangent = jnp.where(is_live[:, None], got_cotangent[safe_pick], zero_value)
        block_weight = jnp.where(is_live, got_weight[safe_pick], zero_value)
        row_grad, gate_grad, pre_gate_grad, pre_up_grad, hidden, out_grad = expert_parts(
            block_tokens, block_cotangent, block_weight, gate_matrix, up_matrix, down_matrix
        )
        gate_term, up_term, down_term = outer_terms(
            block_tokens, pre_gate_grad, pre_up_grad, hidden, out_grad
        )
        target = jnp.where(is_live, picked, slot_total)
        grad_slots = grad_slots.at[target].set(row_grad, mode="drop")
        gate_slots = gate_slots.at[target].set(gate_grad, mode="drop")
        return (
            gate_acc + gate_term,
            up_acc + up_term,
            down_acc + down_term,
            grad_slots,
            gate_slots,
        )

    initial = (
        jnp.zeros((model_width, hidden_width), jnp.float32),
        jnp.zeros((model_width, hidden_width), jnp.float32),
        jnp.zeros((hidden_width, model_width), jnp.float32),
        jnp.zeros((slot_total, model_width), jnp.bfloat16),
        jnp.zeros((slot_total,), jnp.bfloat16),
    )
    finished = lax.fori_loop(0, block_count, block_step, initial)
    gate_acc, up_acc, down_acc, grad_slots, gate_slots = finished
    grad_out = grad_slots.reshape(device_count, most_rows, model_width)
    gate_out = gate_slots.reshape(device_count, most_rows)
    returned = (
        lax.all_to_all(grad_out, ("dp", "expert"), split_axis=0, concat_axis=0, tiled=True),
        lax.all_to_all(gate_out, ("dp", "expert"), split_axis=0, concat_axis=0, tiled=True),
    )
    back_grad = returned[0].reshape(slot_total, model_width)
    back_gate = returned[1].reshape(slot_total)
    row_grads = back_grad[slot_index].reshape(tok_local, top_count, model_width)
    input_grad = jnp.sum(row_grads, axis=1, dtype=jnp.float32).astype(jnp.bfloat16)
    gate_grad = back_gate[slot_index].reshape(tok_local, top_count)
    return (
        input_grad,
        gate_grad,
        gate_acc.astype(jnp.bfloat16)[None],
        up_acc.astype(jnp.bfloat16)[None],
        down_acc.astype(jnp.bfloat16)[None],
    )


def gather_path(tokens, cotangent, routes, gates, w_gate, w_up, w_down):
    dp_count = lax.axis_size("dp")
    expert_count = lax.axis_size("expert")
    device_count = dp_count * expert_count
    tok_local, model_width = tokens.shape
    hidden_width = w_gate.shape[2]
    top_count = routes.shape[1]
    most_rows = 7 * tok_local * top_count // (4 * device_count)
    source_count = 16
    half_rows = source_count * most_rows
    bf16, f32 = jnp.bfloat16, jnp.float32

    def swap_core(v):
        return lax.ppermute(v, "dp", [(p, p ^ 1) for p in range(dp_count)])

    def swap_x(v):
        return lax.ppermute(v, "dp", [(p, p ^ 2) for p in range(dp_count)])

    def swap_y(v):
        return lax.ppermute(v, "expert", [(q, q ^ 1) for q in range(expert_count)])

    def ring_up(v):
        return lax.ppermute(
            v, "expert", [(q, (q + 2) % expert_count) for q in range(expert_count)]
        )

    def ring_down(v):
        return lax.ppermute(
            v, "expert", [(q, (q - 2) % expert_count) for q in range(expert_count)]
        )

    dp_index = lax.axis_index("dp")
    expert_index = lax.axis_index("expert")
    mine = dp_index * expert_count + expert_index
    other = (dp_index ^ 1) * expert_count + expert_index

    hit = routes[:, :, None] == jnp.arange(device_count, dtype=jnp.int32)[None, None, :]
    gate_dense = jnp.sum(jnp.where(hit, gates[:, :, None].astype(f32), 0.0), axis=1)
    named = jnp.sum(hit.astype(f32), axis=1)
    token_iota = jnp.arange(tok_local)
    before = (token_iota[None, :] < token_iota[:, None]).astype(bf16)
    rank = jnp.dot(before, named.astype(bf16), preferred_element_type=f32)
    rank = jnp.where(named > 0.0, rank, -1.0)
    info_width = -(-2 * device_count // 128) * 128
    info = jnp.concatenate(
        [
            gate_dense.astype(bf16),
            rank.astype(bf16),
            jnp.zeros((tok_local, info_width - 2 * device_count), bf16),
        ],
        axis=1,
    )

    t_cuts = (0, model_width // 2, model_width)
    c_cuts = (0, model_width // 4, model_width // 2, model_width)
    cuts = (0, 3 * model_width // 8, 3 * model_width // 4, model_width)

    links = {"x": [], "y": [], "z": []}
    depth = {"x": 2, "y": 2, "z": 3}
    ways = {"x": swap_x, "y": swap_y, "z": ring_up, "d": ring_down}

    def send(way, v):
        link = "z" if way == "d" else way
        queue = links[link]
        if len(queue) >= depth[link]:
            v, _ = lax.optimization_barrier((v, queue[-depth[link]]))
        queue.append(ways[way](v))
        return queue[-1]

    order = [(g, i, j, s) for g in range(2) for i in range(2) for j in range(2) for s in range(2)]
    where = [{}, {}, {}, {}, {}]
    for g, i, j, s in order:
        where[0][g, i, j, s] = (2 * g + i, 2 * j + s)
        where[1][g, i, j, s] = (2 * g + j, 2 * i + s)
        where[2][g, i, j, s] = (2 * g + s, 2 * j + i)
        where[3][g, i, j, s] = (i, 4 * j + 2 * g + s)
        where[4][g, i, j, s] = (j, 4 * i + 2 * g + s)

    def with_other(way, v):
        return jnp.concatenate([v, send(way, v)])

    def compact(place_both, blocks, where):
        width = blocks[0].shape[-1]

        def body(places, *refs):
            ins, keep, give = refs[: len(blocks)], refs[-2], refs[-1]
            for n, source in enumerate(order):
                block, at = where[source]
                picked = jnp.dot(places[n], ins[block][at], preferred_element_type=f32)
                keep[n] = picked[:most_rows].astype(bf16)
                give[n] = picked[most_rows:].astype(bf16)

        shape = jax.ShapeDtypeStruct((source_count, most_rows, width), bf16)
        keep, give = pl.pallas_call(
            body,
            out_shape=(shape, shape),
            in_specs=[pl.BlockSpec(memory_space=pltpu.VMEM)] * (1 + len(blocks)),
            out_specs=(pl.BlockSpec(memory_space=pltpu.VMEM),) * 2,
            compiler_params=pltpu.CompilerParams(vmem_limit_bytes=24 * 2**20),
            cost_estimate=pl.CostEstimate(
                flops=2 * source_count * 2 * most_rows * tok_local * width, bytes_accessed=12 * 2**20, transcendentals=0,
            ),
        )(place_both, *blocks)
        return keep.reshape(half_rows, width), swap_core(give).reshape(half_rows, width)

    def row_call(body, ins, whole, outs, flops, steps=4, copies=2):
        block_rows_here = half_rows // steps
        row_spec = [pl.BlockSpec((block_rows_here, v.shape[1]), lambda b: (b, 0)) for v in ins]
        whole_spec = [
            pl.BlockSpec(shape, lambda b, place=place: place, pipeline_mode=pl.Buffered(1))
            for _, shape, place in whole
        ]
        outs = [out for out in outs for _ in range(copies)]
        return pl.pallas_call(
            body,
            grid=(steps,),
            out_shape=tuple(jax.ShapeDtypeStruct((half_rows, w), d) for w, d in outs),
            in_specs=row_spec + whole_spec,
            out_specs=tuple(pl.BlockSpec((block_rows_here, w), lambda b: (b, 0)) for w, _ in outs),
            compiler_params=pltpu.CompilerParams(vmem_limit_bytes=38 * 2**20),
            cost_estimate=pl.CostEstimate(
                flops=flops, bytes_accessed=flops // 200, transcendentals=0
            ),
        )(*ins, *[v for v, _, _ in whole])

    def both_halves(refs, at=slice(None)):
        return jnp.concatenate([refs[0][:, at], refs[1][:, at]])

    def put(refs, v, at=slice(None)):
        refs[0][:, at] = v[: v.shape[0] // 2]
        refs[1][:, at] = v[v.shape[0] // 2 :]

    nt = (((1,), (1,)), ((), ()))
    gate_matrix, up_matrix, down_matrix = w_gate[0], w_up[0], w_down[0]
    lanes = lax.broadcasted_iota(jnp.int32, (1, info_width), 1)
    lane_mask = (lanes == mine).astype(f32)
    mask_spec = (lane_mask, (1, info_width), (0, 0))
    unit = 2 * 2 * half_rows * model_width * hidden_width

    t0 = jnp.concatenate([tokens[:, : t_cuts[1]], info], axis=1)
    t1 = tokens[:, t_cuts[1] :]
    c0, c1, c2 = (cotangent[:, c_cuts[n] : c_cuts[n + 1]] for n in range(3))
    t0_hops, t1_hops, c0_hops, c1_hops = [t0], [t1], [c0], [c1]

    def hop(hops):
        hops.append(send("z", hops[-1]))

    def near(way, hops, g):
        return with_other(way, jnp.stack([hops[2 * g], hops[2 * g + 1]]))

    hop(t0_hops)
    hop(t1_hops)
    c2_hops = [with_other("y", with_other("x", c2[None]))]
    t0_near = [near("y", t0_hops, 0)]
    t1_near = [near("x", t1_hops, 0)]
    hop(t0_hops)
    hop(t1_hops)
    t0_far = [send("x", t0_near[0])]
    t1_far = [send("y", t1_near[0])]
    hop(t0_hops)
    hop(t1_hops)
    t1_near.append(near("x", t1_hops, 1))
    t0_near.append(near("y", t0_hops, 1))
    hop(c0_hops)
    hop(c1_hops)
    t0_far.append(send("x", t0_near[1]))
    t1_far.append(send("y", t1_near[1]))
    hop(c0_hops)
    hop(c1_hops)
    hop(c0_hops)
    hop(c1_hops)
    hop(c2_hops)
    ready, _, _ = lax.optimization_barrier((c2_hops[1], c0_hops[3], c1_hops[3]))
    c2_hops[1] = ready
    c1_own, c0_own = jnp.stack(c1_hops), jnp.stack(c0_hops)
    c1_other, c0_other = send("x", c1_own), send("y", c0_own)
    hop(c2_hops)
    t0_blocks = [t0_near[0], t0_far[0], t0_near[1], t0_far[1]]
    t1_blocks = [t1_near[0], t1_far[0], t1_near[1], t1_far[1]]
    got_info = jnp.stack(
        [t0_blocks[where[0][k][0]][where[0][k][1], :, t_cuts[1] :] for k in order]
    )
    slots = jnp.arange(most_rows, dtype=f32)

    def places_of(index):
        at = lax.broadcasted_iota(jnp.int32, got_info.shape, 2) == device_count + index
        ranks = jnp.sum(jnp.where(at, got_info, jnp.zeros((), bf16)).astype(f32), axis=-1)
        return (ranks[:, None, :] == slots[:, None]).astype(bf16)

    place_both = jnp.concatenate([places_of(mine), places_of(other)], axis=1)
    rows = [
        half
        for n, blocks in enumerate((t0_blocks, t1_blocks))
        for half in compact(place_both, blocks, where[n])
    ]

    def forward(*refs):
        (part0, part1), (gates_at, wg, wu), outs = refs[:2], refs[2:5], refs[5:]
        sent = part0[:, t_cuts[1] :].astype(f32)
        row_gate = jnp.sum(sent * gates_at[...], axis=1, keepdims=True)
        parts = (part0[:, : t_cuts[1]], part1[...])
        pre_gate, pre_up = 0.0, 0.0
        for n in range(2):
            rows_at = slice(t_cuts[n], t_cuts[n + 1])
            pre_gate += jnp.dot(parts[n], wg[rows_at], preferred_element_type=f32)
            pre_up += jnp.dot(parts[n], wu[rows_at], preferred_element_type=f32)
        sigmoid_gate = 1.0 / (1.0 + jnp.exp(-pre_gate))
        silu_gate = pre_gate * sigmoid_gate
        hidden = silu_gate * pre_up
        outs[0][...] = hidden
        slope = pre_up * sigmoid_gate * (1.0 + pre_gate * (1.0 - sigmoid_gate))
        outs[1][...] = row_gate * slope
        outs[2][...] = row_gate * silu_gate
        outs[3][...] = (row_gate * hidden).astype(bf16)

    square = (model_width, hidden_width)
    def forward_half(part0, part1, flops):
        return row_call(
            forward,
            [part0, part1],
            [mask_spec, (gate_matrix, square, (0, 0)), (up_matrix, square, (0, 0))],
            [(hidden_width, f32)] * 3 + [(hidden_width, bf16)],
            flops,
            2,
            1,
        )

    forward_own = forward_half(rows[0], rows[2], 2 * unit)
    c0_own, c1_own, first_kept = lax.optimization_barrier((c0_own, c1_own, forward_own[0]))
    c0_near = jnp.concatenate([c0_own, c0_other])
    c1_near = jnp.concatenate([c1_own, c1_other])
    c0_far = send("x", c0_near)
    c1_far = send("y", c1_near)
    hop(c2_hops)
    given_in, _ = lax.optimization_barrier((rows[1], c0_near))
    forward_out = [[first_kept, *forward_own[1:]], forward_half(given_in, rows[3], 2 * unit)]
    kept = [forward_out[h][n] for n in range(3) for h in range(2)]
    weighted = [forward_out[h][3] for h in range(2)]
    place_tied, kept[0], kept[1] = lax.optimization_barrier((place_both, kept[0], kept[1]))
    c1_rows = compact(place_tied, [c1_near, c1_far], where[4])
    c0_rows = compact(place_tied, [c0_near, c0_far], where[3])

    def early(*refs):
        total = 0.0
        for n in range(2):
            total += lax.dot_general(
                both_halves(refs[2 * n : 2 * n + 2]),
                refs[4][:, c_cuts[n] : c_cuts[n + 1]],
                nt,
                preferred_element_type=f32,
            )
        put(refs[5:], total)

    early_back = row_call(
        early,
        [*c0_rows, *c1_rows],
        [(down_matrix, (hidden_width, c_cuts[2]), (0, 0))],
        [(hidden_width, f32)],
        1024,
        2,
    )
    place_tied, early_first = lax.optimization_barrier((place_both, early_back[0]))
    early_back = [early_first, early_back[1]]
    c2_rows = compact(place_tied, c2_hops, where[2])
    cot_rows = [*c0_rows, *c1_rows, *c2_rows]

    def row_grad(pgg, pug, wg, wu):
        return lax.dot_general(pgg, wg, nt, preferred_element_type=f32) + lax.dot_general(
            pug, wu, nt, preferred_element_type=f32
        )

    def backward(*refs):
        half, first, gated, slope, silu, gates_at, wd, wg, wu = refs[:9]
        pgg, pug, grad0, grad1, grad2 = refs[9:]
        back = first[...] + lax.dot_general(
            half[...], wd[...], nt, preferred_element_type=f32
        )
        gate_grad = jnp.sum(gated[...] * back, axis=1, keepdims=True)
        gate_side = (back * slope[...]).astype(bf16)
        up_side = (back * silu[...]).astype(bf16)
        pgg[...] = gate_side
        pug[...] = up_side
        for n, out in ((2, grad2), (0, grad0), (1, grad1)):
            at = slice(cuts[n], cuts[n + 1])
            grad = row_grad(gate_side, up_side, wg[at], wu[at])
            out[:, : cuts[n + 1] - cuts[n]] = grad.astype(bf16)
        grad0[:, cuts[1] :] = (gate_grad * gates_at[...]).astype(bf16)

    def backward_half(h, half):
        return row_call(
            backward,
            [half, early_back[h], kept[h], kept[2 + h], kept[4 + h]],
            [
                mask_spec,
                (down_matrix, (hidden_width, c_cuts[3] - c_cuts[2]), (0, 1)),
                (gate_matrix, square, (0, 0)),
                (up_matrix, square, (0, 0)),
            ],
            [(hidden_width, bf16)] * 2
            + [(info_width + cuts[1], bf16), (cuts[2] - cuts[1], bf16), (cuts[3] - cuts[2], bf16)],
            1024,
            2,
            1,
        )

    given_out = backward_half(1, c2_rows[1])
    own_in, tied = lax.optimization_barrier((c2_rows[0], given_out[0]))
    own_out = backward_half(0, own_in)
    sides = [own_out[0], tied, own_out[1], given_out[1]]
    grad_first, grad_second, grad_last = ((own_out[n], given_out[n]) for n in (2, 3, 4))

    place_grid = place_both.reshape(2, 2, 2, 2, 2 * most_rows, tok_local)

    def pair_rows(halves):
        width = halves[0].shape[-1]
        own = halves[0].reshape(source_count, most_rows, width)
        given = swap_core(halves[1]).reshape(source_count, most_rows, width)
        return jnp.concatenate([own, given], axis=1).reshape(2, 2, 2, 2, 2 * most_rows, width)

    def spread(places, v):
        return jnp.einsum("...ct,...cd->...td", places, v, preferred_element_type=f32)

    def add(own, arrived):
        return (own.astype(f32) + arrived.astype(f32)).astype(bf16)

    links["x"].clear()
    links["y"].clear()
    links["z"].clear()
    depth.update(x=3, y=3, z=3)
    v2 = pair_rows(grad_last)
    v0 = pair_rows(grad_first)
    v1 = pair_rows(grad_second)

    def spread_last(r):
        return spread(place_grid[r // 2, :, :, r % 2], v2[r // 2, :, :, r % 2])

    first_last = spread_last(3).astype(bf16)
    far0 = [spread(place_grid[g, 1], v0[g, 1]).astype(bf16) for g in range(2)]
    far1 = [spread(place_grid[g, :, 1], v1[g, :, 1]).astype(bf16) for g in range(2)]
    first_last, far0, far1 = lax.optimization_barrier((first_last, far0, far1))
    moving2 = send("d", first_last)
    sent0, sent1, half0, half1, near0, near1 = ([None, None] for _ in range(6))
    sent0[1] = send("x", far0[1])
    sent1[1] = send("y", far1[1])
    sent0[0] = send("x", far0[0])
    sent1[0] = send("y", far1[0])
    sides_tied, _, _, _ = lax.optimization_barrier((sides, far0, far1, first_last))
    gate_tied, up_tied = sides_tied[:2], sides_tied[2:]
    moving2 = add(spread_last(2), moving2)
    moving2 = send("d", moving2)
    half1[1] = add(spread(place_grid[1, :, 0], v1[1, :, 0]), sent1[1])
    half0[1] = add(spread(place_grid[1, 0], v0[1, 0]), sent0[1])
    moving2 = add(spread_last(1), moving2)
    weighted_tied, half1[1], half0[1], moving2 = lax.optimization_barrier(
        (weighted, half1[1], half0[1], moving2)
    )
    moving2 = send("d", moving2)
    near1[1] = send("x", half1[1][1])
    near0[1] = send("y", half0[1][1])
    sum0_high = add(half0[1][0], near0[1])
    sum1_high = add(half1[1][0], near1[1])
    grid_tied, _, _ = lax.optimization_barrier((place_grid, sum0_high, sum1_high))
    moving0 = send("d", sum0_high[1])
    moving1 = send("d", sum1_high[1])
    half1[0] = add(spread(grid_tied[0, :, 0], v1[0, :, 0]), sent1[0])
    half0[0] = add(spread(grid_tied[0, 0], v0[0, 0]), sent0[0])
    near1[0] = send("x", half1[0][1])
    near0[0] = send("y", half0[0][1])
    pair = add(spread_last(0), moving2)
    pair = add(pair[:, 0], send("y", pair[:, 1]))
    sum_last = add(pair[0], send("x", pair[1]))
    moving0 = send("d", add(sum0_high[0], moving0))
    moving1 = send("d", add(sum1_high[0], moving1))
    sum0_low = add(half0[0][0], near0[0])
    sum1_low = add(half1[0][0], near1[0])
    moving0 = send("d", add(sum0_low[1], moving0))
    moving1 = send("d", add(sum1_low[1], moving1))
    sum_first = add(sum0_low[0], moving0)
    sum_second = add(sum1_low[0], moving1)
    gate_back = sum_first[:, cuts[1] : cuts[1] + device_count].astype(f32)
    input_grad = jnp.concatenate([sum_first[:, : cuts[1]], sum_second, sum_last], axis=1)
    gate_grad_out = jnp.sum(jnp.where(hit, gate_back[:, None, :], 0.0), axis=2).astype(bf16)

    tile = 256
    tn = (((0,), (0,)), ((), ()))

    def tn_dot(a, b):
        return lax.dot_general(a, b, tn, preferred_element_type=f32)

    def weight_call(body, halves, cuts, wide, out_spec, out_shape):
        firsts = [cut // tile for cut in cuts]
        count = len(halves)

        def run(*refs):
            step = pl.program_id(0)
            for n in range(count // 2):

                @pl.when((step >= firsts[n]) & (step < firsts[n + 1]))
                def _(n=n):
                    tiles = (refs[2 * n][...], refs[2 * n + 1][...])
                    refs[-1][...] = body(tiles, refs[count : count + 2]).astype(bf16)

        def tile_spec(n):
            low, top = firsts[n], firsts[n + 1] - firsts[n] - 1
            return pl.BlockSpec((half_rows, tile), lambda b: (0, jnp.clip(b - low, 0, top)))

        half_spec = pl.BlockSpec(
            (half_rows, hidden_width), lambda b: (0, 0), pipeline_mode=pl.Buffered(1)
        )
        return pl.pallas_call(
            run,
            grid=(firsts[-1],),
            out_shape=jax.ShapeDtypeStruct(out_shape, bf16),
            in_specs=[tile_spec(n // 2) for n in range(count)] + [half_spec] * 2,
            out_specs=out_spec,
            compiler_params=pltpu.CompilerParams(vmem_limit_bytes=16 * 2**20),
            cost_estimate=pl.CostEstimate(
                flops=unit, bytes_accessed=14 * 2**20, transcendentals=0
            ),
        )(*halves, *wide)

    def side_weights(sides):
        return weight_call(
            lambda x, side: tn_dot(x[0], side[0][...]) + tn_dot(x[1], side[1][...]),
            rows,
            t_cuts,
            sides,
            pl.BlockSpec((tile, hidden_width), lambda b: (b, 0)),
            (model_width, hidden_width),
        )

    w_gate_grad = side_weights(gate_tied)
    w_up_grad = side_weights(up_tied)
    w_down_grad = weight_call(
        lambda c, w: tn_dot(w[0][...], c[0]) + tn_dot(w[1][...], c[1]),
        cot_rows,
        c_cuts,
        weighted_tied,
        pl.BlockSpec((hidden_width, tile), lambda b: (0, b)),
        (hidden_width, model_width),
    )
    return (input_grad, gate_grad_out, w_gate_grad[None], w_up_grad[None], w_down_grad[None])


def on_device(tokens, cotangent, routes, gates, w_gate, w_up, w_down):
    dp_count = lax.axis_size("dp")
    expert_count = lax.axis_size("expert")
    gathered_bytes = dp_count * expert_count * tokens.size * 2
    if dp_count == 4 and expert_count == 8 and gathered_bytes <= gather_limit:
        return gather_path(tokens, cotangent, routes, gates, w_gate, w_up, w_down)
    return exchange_path(tokens, cotangent, routes, gates, w_gate, w_up, w_down)


def solution(mesh):
    in_specs = (
        P(("dp", "expert"), None),
        P(("dp", "expert"), None),
        P(("dp", "expert"), None),
        P(("dp", "expert"), None),
        P(("dp", "expert"), None, None),
        P(("dp", "expert"), None, None),
        P(("dp", "expert"), None, None),
    )
    out_specs = (
        P(("dp", "expert"), None),
        P(("dp", "expert"), None),
        P(("dp", "expert"), None, None),
        P(("dp", "expert"), None, None),
        P(("dp", "expert"), None, None),
    )
    return jax.shard_map(
        on_device, mesh=mesh, in_specs=in_specs, out_specs=out_specs, check_vma=False
    )
```
